512 devices in a mesh: blk: 32 (over x, y, core), smp: 16 (over z).
Axes of the slice: x: 4, y: 4, z: 16, core: 2. Of those that a mesh axis runs over, the one named last changes fastest.
Arguments:
- features: bfloat16 [16, 96, 8192], P('smp', None, 'blk'), may hold values from -6 to 6
- active: int32 [16, 8192], P('smp', 'blk'), may hold values 0 or 1
- neighbour_rows: int32 [16, 27, 8192], P('smp', None, 'blk'), may hold values from 0 to 400, as said below
- send_rows: int32 [16, 32, 8, 32], P('smp', 'blk'), may hold values from 0 to 256, as said below
- first_weight: bfloat16 [27, 96, 96], replicated, may hold values from -0.125 to 0.125
- second_weight: bfloat16 [27, 96, 96], replicated, may hold values from -0.125 to 0.125
- cotangent: bfloat16 [16, 96, 8192], P('smp', None, 'blk'), may hold values from -6 to 6
Outputs:
- out_field: bfloat16 [16, 96, 8192], P('smp', None, 'blk')
- input_grad: bfloat16 [16, 96, 8192], P('smp', None, 'blk')
- first_grad: float32 [27, 96, 96], replicated
- second_grad: float32 [27, 96, 96], replicated
The draws below stay inside these ranges and needn't reach their ends.
Inputs may be any that keep to these rules, and one draw needn't show every extreme that they name: `neighbour_rows`: offset o = 9 (a + 1) + 3 (b + 1) + (c + 1) for a step (a, b, c) in -1..1 along the three dimensions; o = 13 names the voxel itself. The relation is symmetric: if v = nbr(u, o) then u = nbr(v, 26 - o). A value naming list d, place s occurs only where send_rows[t, p, d, s] is a row. send_rows[t, p, d] lists distinct rows of device p in rising order, then the filler 256; lists of directions 4 to 7 hold at most 4 rows; in every draw some list of a direction below 4 has 32 rows and some list of a direction from 4 has 4 rows.
All inputs are finite; a program needn't handle non-finite values. No bound on the sum of `active` on one device may be relied on, other than what follows from the above.
Results may differ from the reference program's by a relative error of at most 0.005.
Values may be sent and summed in bfloat16 or wider, within the bound.
A program may use at most 64 MiB of HBM per device.

```python
import jax
import jax.numpy as jnp
import numpy as np
from jax import lax

C = 96
BE = 4
TALL = 4
LV = 256
SEND = 32
HALO = 144
VOX = 8192
SAMPLES = 16
N_BLK = 32


STEPS = ((-1, 0), (1, 0), (0, -1), (0, 1), (-1, -1), (-1, 1), (1, -1), (1, 1))


def patch_layout():
    across = N_BLK // TALL
    column_device = np.zeros((2 * across, 2 * TALL), np.int64)
    column_slot = np.zeros((2 * across, 2 * TALL), np.int64)
    column_first = np.zeros((N_BLK, 4), np.int64)
    column_second = np.zeros((N_BLK, 4), np.int64)
    for col_first in range(2 * across):
        for col_second in range(2 * TALL):
            device = col_first // 2 * TALL + col_second // 2
            slot_num = col_first % 2 * 2 + col_second % 2
            column_device[col_first, col_second] = device
            column_slot[col_first, col_second] = slot_num
            column_first[device, slot_num] = col_first
            column_second[device, slot_num] = col_second
    return (across, column_device, column_slot, column_first, column_second)


def static_tables():
    across, column_device, column_slot, column_first, column_second = patch_layout()
    cells = BE ** 3
    owner = np.arange(N_BLK)[:, None, None]
    voxel = np.arange(LV)[None, None, :]
    offset = np.arange(27)[None, :, None]
    slot_num = voxel // cells
    base_first = column_first[owner, slot_num]
    base_second = column_second[owner, slot_num]
    coord_x = voxel // (BE * BE) % BE + offset // 9 - 1
    coord_y = voxel // BE % BE + offset // 3 % 3 - 1
    coord_z = voxel % BE + offset % 3 - 1
    shift_x = (coord_x >= BE).astype(np.int64) - (coord_x < 0).astype(np.int64)
    shift_y = (coord_y >= BE).astype(np.int64) - (coord_y < 0).astype(np.int64)
    shift_z = (coord_z >= BE).astype(np.int64) - (coord_z < 0).astype(np.int64)
    near_first = base_first + shift_x
    near_second = base_second + shift_y
    inside = (near_first >= 0) & (near_first < 2 * across) & (near_second >= 0) & (near_second < 2 * TALL)
    near_first = np.clip(near_first, 0, 2 * across - 1)
    near_second = np.clip(near_second, 0, 2 * TALL - 1)
    near_device = column_device[near_first, near_second]
    near_local = column_slot[near_first, near_second] * cells
    near_local = near_local + (coord_x - shift_x * BE) * BE * BE + (coord_y - shift_y * BE) * BE + coord_z - shift_z * BE
    patch_dx = near_first // 2 - base_first // 2
    patch_dy = near_second // 2 - base_second // 2
    direction_of = np.full((3, 3), 8, np.int64)
    for index in range(8):
        direction_of[STEPS[index][0] + 1, STEPS[index][1] + 1] = index
    direction = direction_of[1 - patch_dx, 1 - patch_dy]
    near_device = np.broadcast_to(near_device, (N_BLK, 27, LV))
    near_local = np.broadcast_to(near_local, (N_BLK, 27, LV))
    direction = np.broadcast_to(direction, (N_BLK, 27, LV))
    return (across, base_first, base_second, near_first, near_second, shift_z, inside, near_device, near_local, direction)


def random_walk(walk_key, span):
    moves_drawn = jax.random.randint(walk_key, (span - 1,), 0, 4)
    moves = (moves_drawn == 3).astype(jnp.int32) - (moves_drawn == 0).astype(jnp.int32)
    return moves


def geometry(key):
    across, base_first, base_second, near_first, near_second, shift_z, inside, near_device, near_local, direction = static_tables()
    owner = np.arange(N_BLK)[:, None, None]
    device_ids = jnp.asarray(near_device.astype(np.int32))
    local_ids = jnp.asarray(near_local.astype(np.int32))
    direction_ids = jnp.asarray(direction.astype(np.int32))
    starts = np.array([LV + k * SEND for k in range(4)] + [LV + 4 * SEND + k * BE for k in range(4)] + [0], np.int32)
    deltas = np.array([STEPS[k][0] * TALL + STEPS[k][1] for k in range(8)], np.int64)
    target = np.arange(N_BLK)[:, None] + deltas[None, :]
    target_ok = (target >= 0) & (target < N_BLK)
    target_clip = np.clip(target, 0, N_BLK - 1)

    def one_sample(sample_key):
        key_first, key_second = jax.random.split(sample_key)
        moves_first = random_walk(key_first, 2 * across).at[1].set(0)
        moves_second = random_walk(key_second, 2 * TALL).at[1].set(0)
        height_first = jnp.concatenate([jnp.zeros((1,), jnp.int32), jnp.cumsum(moves_first)])
        height_second = jnp.concatenate([jnp.zeros((1,), jnp.int32), jnp.cumsum(moves_second)])
        heights = height_first[:, None] + height_second[None, :]
        own_height = heights[base_first, base_second]
        near_height = heights[near_first, near_second]
        valid = jnp.asarray(inside) & (near_height == own_height + jnp.asarray(shift_z.astype(np.int32)))
        remote = valid & (device_ids != owner)
        need = jnp.zeros((N_BLK, 9, LV + 1), jnp.int32)
        need = need.at[owner, direction_ids, jnp.where(remote, local_ids, LV)].max(1)[:, :8, :LV]
        ranks = jnp.cumsum(need, axis=2) - 1
        slot_pos = jnp.where(need > 0, ranks, SEND)
        receivers = np.arange(N_BLK)[:, None, None]
        directions = np.arange(8)[None, :, None]
        locals_all = jnp.broadcast_to(jnp.arange(LV, dtype=jnp.int32)[None, None, :], (N_BLK, 8, LV))
        lists = jnp.full((N_BLK, 8, SEND + 1), LV, jnp.int32)
        lists = lists.at[receivers, directions, slot_pos].set(locals_all)[:, :, :SEND]
        send_lists = lists[target_clip, np.arange(8)[None, :]]
        send_lists = jnp.where(jnp.asarray(target_ok)[:, :, None], send_lists, LV)
        clipped = jnp.minimum(direction_ids, 7)
        far_index = jnp.asarray(starts)[direction_ids] + ranks[owner, clipped, local_ids]
        table = jnp.where(device_ids == owner, local_ids, far_index)
        table = jnp.where(valid, table, LV + HALO)
        row_table = table.transpose(1, 0, 2).reshape(27, N_BLK * LV)
        return (row_table.astype(jnp.int32), send_lists.astype(jnp.int32))
    return lax.map(one_sample, jax.random.split(key, SAMPLES))


def draw_neighbour_rows(key, part):
    row_table, send_lists = geometry(key)
    return row_table


def draw_send_rows(key, part):
    row_table, send_lists = geometry(key)
    return send_lists


def with_ends(values, key, low, top_value):
    longest = values.shape.index(max(values.shape))
    spots = []
    for shift in (0, 1):
        where = [jax.random.randint(jax.random.fold_in(key, axis), (), 0, length) for axis, length in enumerate(values.shape)]
        where[longest] = (where[longest] + shift) % values.shape[longest]
        spots.append(tuple(where))
    return values.at[spots[0]].set(low).at[spots[1]].set(top_value)


def block_scale(stream_key, extent, cuts, smallest, largest):
    def one(position, shards_of):
        steps = jax.random.uniform(jax.random.fold_in(jax.random.fold_in(stream_key, 6), position), (shards_of,), jnp.float32, smallest / len(cuts), largest / len(cuts))
        return jnp.repeat(jnp.exp(steps), extent[position] // shards_of).reshape((-1,) + (1,) * (len(extent) - position - 1))

    loudness = one(*cuts[0])
    for cut in cuts[1:]:
        loudness = loudness * one(*cut)
    return loudness


def normal_values(rng, shape, spread, most, cuts=(), kind=jnp.bfloat16):
    entries = spread * jax.random.normal(rng, shape, jnp.float32)
    if cuts:
        entries = entries * block_scale(rng, shape, cuts, -0.22, 0.18)
    return jnp.clip(entries, -most, most).astype(kind)


def setup_inputs(seed: int = 0) -> dict:
    streams_of = jax.random.split(jax.random.key(seed), 8)
    features = normal_values(streams_of[0], (SAMPLES, C, VOX), 1.0, 6.0, ((0, 16), (2, 32)))
    active = with_ends((jax.random.randint(streams_of[1], (SAMPLES, VOX), 0, 5) < 3).astype(jnp.int32), jax.random.fold_in(streams_of[1], 1), 0, 1)
    neighbour_rows = draw_neighbour_rows(jax.random.fold_in(streams_of[7], 71), 0)
    send_rows = draw_send_rows(jax.random.fold_in(streams_of[7], 71), 0)
    first_weight = normal_values(streams_of[4], (27, C, C), (27 * C) ** -0.5, 0.125)
    second_weight = normal_values(streams_of[5], (27, C, C), (27 * C) ** -0.5, 0.125)
    cotangent = normal_values(streams_of[6], (SAMPLES, C, VOX), 1.0, 6.0, ((0, 16), (2, 32)))
    return dict(features=features, active=active, neighbour_rows=neighbour_rows, send_rows=send_rows, first_weight=first_weight, second_weight=second_weight, cotangent=cotangent)


STEPS = ((-1, 0), (1, 0), (0, -1), (0, 1), (-1, -1), (-1, 1), (1, -1), (1, 1))


def share(values_in, send_lists):
    channels = values_in.shape[1]
    padded = jnp.concatenate([values_in, jnp.zeros((N_BLK, channels, 1), values_in.dtype)], axis=2)
    flat_lists = send_lists.reshape(N_BLK, 8 * SEND)
    sent = jax.vmap(lambda portion, indices: portion[:, indices])(padded, flat_lists)
    sent = sent.reshape(N_BLK, channels, 8, SEND)
    pieces = [values_in]
    for direction in range(8):
        width = SEND if direction < 4 else BE
        offset = STEPS[direction][0] * TALL + STEPS[direction][1]
        source = jnp.arange(N_BLK, dtype=jnp.int32) - offset
        inside = (source >= 0) & (source < N_BLK)
        got = sent[jnp.clip(source, 0, N_BLK - 1), :, direction, :width]
        pieces.append(jnp.where(inside[:, None, None], got, jnp.zeros_like(got)))
    pieces.append(jnp.zeros((N_BLK, channels, 1), values_in.dtype))
    return jnp.concatenate(pieces, axis=2)


def convolve(extended, row_table, weights):
    def accumulate(offset, running):
        picked = jax.vmap(lambda portion, indices: portion[:, indices])(extended, row_table[:, offset])
        matrix = weights[offset].astype(jnp.float32)
        return running + jnp.einsum("ij,njv->niv", matrix, picked.astype(jnp.float32))

    start_value = jnp.zeros((N_BLK, weights.shape[1], LV), jnp.float32)
    return lax.fori_loop(0, 27, accumulate, start_value)


def correlate(gradient, extended, row_table):
    def accumulate(offset, running):
        picked = jax.vmap(lambda portion, indices: portion[:, indices])(extended, row_table[:, offset])
        product = jnp.einsum("niv,njv->ij", gradient.astype(jnp.float32), picked.astype(jnp.float32))
        return running.at[offset].add(product)

    channels = gradient.shape[1]
    return lax.fori_loop(0, 27, accumulate, jnp.zeros((27, channels, channels), jnp.float32))


def to_devices(values_in):
    return values_in.reshape(values_in.shape[0], N_BLK, LV).transpose(1, 0, 2)


def to_sample(values_in):
    return values_in.transpose(1, 0, 2).reshape(values_in.shape[1], N_BLK * LV)


def reference(features, active, neighbour_rows, send_rows, first_weight, second_weight, cotangent):
    first_flipped = jnp.flip(first_weight, 0).transpose(0, 2, 1)
    second_flipped = jnp.flip(second_weight, 0).transpose(0, 2, 1)

    def one_sample(sample_items):
        feature_rows, active_rows, table_rows, send_lists, cotangent_rows = sample_items
        live_mask = active_rows.reshape(N_BLK, 1, LV).astype(jnp.float32)
        live_sites = live_mask > 0
        row_table = to_devices(table_rows)
        inputs = to_devices(feature_rows)
        masked = jnp.where(live_sites, inputs, jnp.zeros_like(inputs))
        masked_ext = share(masked, send_lists)
        pre_first = live_mask * convolve(masked_ext, row_table, first_weight)
        hidden = (live_mask * jax.nn.silu(pre_first)).astype(jnp.bfloat16)
        hidden_ext = share(hidden, send_lists)
        out_field = (live_mask * convolve(hidden_ext, row_table, second_weight)).astype(jnp.bfloat16)
        upstream = to_devices(cotangent_rows)
        grad_out = jnp.where(live_sites, upstream, jnp.zeros_like(upstream))
        grad_hidden = live_mask * convolve(share(grad_out, send_lists), row_table, second_flipped)
        sigmoid_pre = jax.nn.sigmoid(pre_first)
        grad_pre = (grad_hidden * sigmoid_pre * (1.0 + pre_first * (1.0 - sigmoid_pre))).astype(jnp.bfloat16)
        input_grad = (live_mask * convolve(share(grad_pre, send_lists), row_table, first_flipped)).astype(jnp.bfloat16)
        second_part = correlate(grad_out, hidden_ext, row_table)
        first_part = correlate(grad_pre, masked_ext, row_table)
        return to_sample(out_field), to_sample(input_grad), first_part, second_part

    results = lax.map(one_sample, (features, active, neighbour_rows, send_rows, cotangent))
    grad_scale = 1.0 / (SAMPLES * VOX) ** 0.5
    first_grad = jnp.sum(results[2], axis=0) * grad_scale
    second_grad = jnp.sum(results[3], axis=0) * grad_scale
    return results[0], results[1], first_grad, second_grad
```

```python
import functools

import jax
import jax.numpy as jnp
from jax import lax
from jax.experimental import pallas as pl
from jax.experimental.pallas import tpu as pltpu
from jax.sharding import PartitionSpec as P

MESH = pl.DeviceIdType.MESH
TALL = 4
STEPS = ((-1, 0), (1, 0), (0, -1), (0, 1), (-1, -1), (-1, 1), (1, -1), (1, 1))
DELTAS = tuple(a * TALL + b for a, b in STEPS)
OFFSETS = 27
GROUP = 4
GROUPS = 7
CORNER = 16
UNROLL = 3


def nn(a, b):
    return lax.dot_general(a, b, (((1,), (0,)), ((), ())), preferred_element_type=jnp.float32)


def nt(a, b):
    return lax.dot_general(a, b, (((1,), (1,)), ((), ())), preferred_element_type=jnp.float32)


def eye(n, dtype):
    rows = lax.broadcasted_iota(jnp.int32, (n, n), 0)
    cols = lax.broadcasted_iota(jnp.int32, (n, n), 1)
    return (rows == cols).astype(jnp.float32).astype(dtype)


def one_hot(rows, codes):
    return jnp.where(rows == codes, 1.0, 0.0).astype(jnp.bfloat16)


def main_kernel(
    nb, nz,
    feat, act, nbr, lists, w1, w2, cot,
    out_field, input_grad, gathered,
    field, pick, sent_a, halo_a, sent_c, halo_c,
    local_hot, halo_hot, turned, picked, sides,
    to_core, own, from_core, summed, arrived, z_part, z_in, z_out,
    sem_a, sem_c, sem_core, sem_plane, sem_z, sem_zg, sem_gather, sem_forward,
):
    bf16, f32 = jnp.bfloat16, jnp.float32
    channels, voxels = feat.shape[1], feat.shape[2]
    both = 2 * channels
    per_list = lists.shape[3]
    halo_rows = halo_a.shape[0]
    nj = nb // 2
    half_rows = own.shape[0]
    piece = half_rows // nj
    sliver = piece // nz
    group_rows = GROUP * channels * channels // 128
    blk = lax.axis_index("blk")
    smp = lax.axis_index("smp")
    core = lax.rem(blk, 2)
    chip = lax.div(blk, 2)
    other = 1 - core
    partner = (chip * 2 + other, smp)

    def plane(i):
        return lax.rem(chip + i, nj)

    def along(i):
        return lax.rem(smp + i, nz)

    def remote(src, dst, sems, source, target, device):
        return pltpu.make_async_remote_copy(
            src_ref=src, dst_ref=dst, send_sem=sems.at[0, target], recv_sem=sems.at[1, source],
            device_id=device, device_id_type=MESH,
        )

    halo_a[...] = jnp.zeros_like(halo_a)
    halo_c[...] = jnp.zeros_like(halo_c)
    barrier = pltpu.get_barrier_semaphore()

    def greet_blk(i, _):
        pl.semaphore_signal(
            barrier, inc=1, device_id=(lax.rem(blk + i, nb), smp), device_id_type=MESH
        )
        return 0

    def greet_smp(i, _):
        pl.semaphore_signal(barrier, inc=1, device_id=(blk, along(i)), device_id_type=MESH)
        return 0

    lax.fori_loop(1, nb, greet_blk, 0)
    lax.fori_loop(1, nz, greet_smp, 0)

    live = act[...] > 0
    live_f = live.astype(f32)
    field[0:channels, :] = jnp.where(live, feat[0].astype(f32), 0.0).astype(bf16)
    field[channels:both, :] = jnp.where(live, cot[0].astype(f32), 0.0).astype(bf16)

    spread = jnp.concatenate(
        [jnp.broadcast_to(lists[0, 0, d : d + 1, :], (per_list, per_list)) for d in range(8)], axis=0
    )
    at_row = lax.broadcasted_iota(jnp.int32, spread.shape, 0)
    at_col = lax.broadcasted_iota(jnp.int32, spread.shape, 1)
    column = jnp.sum(jnp.where(lax.rem(at_row, per_list) == at_col, spread, 0), axis=1, keepdims=True)
    pick[...] = one_hot(lax.broadcasted_iota(jnp.int32, (8 * per_list, voxels), 1), column)

    def face_copies(sent, halo, sems):
        copies = []
        for d, delta in enumerate(DELTAS):
            if d < 4:
                rows = pl.ds(d * per_list, per_list)
                into = rows
            else:
                rows = pl.ds(d * per_list, CORNER)
                into = pl.ds(4 * per_list + (d - 4) * CORNER, CORNER)
            target, source = blk + delta, blk - delta
            copy = pltpu.make_async_remote_copy(
                src_ref=sent.at[rows, :], dst_ref=halo.at[into, :],
                send_sem=sems.at[0, d], recv_sem=sems.at[1, d],
                device_id=(jnp.clip(target, 0, nb - 1), smp), device_id_type=MESH,
            )
            has_target = (target >= 0) & (target < nb)
            has_source = (source >= 0) & (source < nb)
            copies.append((copy, has_target, has_source))
        return copies

    def start_faces(copies):
        for copy, has_target, _ in copies:
            pl.when(has_target)(copy.start)

    def arrive_faces(copies):
        for copy, _, has_source in copies:
            pl.when(has_source)(copy.wait_recv)

    def finish_faces(copies):
        for copy, has_target, _ in copies:
            pl.when(has_target)(copy.wait_send)

    faces_a = face_copies(sent_a, halo_a, sem_a)
    faces_c = face_copies(sent_c, halo_c, sem_c)
    sent_a[:, 0:both] = nt(pick[...], field[...]).astype(bf16)
    sent_a[:, both:] = jnp.zeros((8 * per_list, sent_a.shape[1] - both), bf16)
    pl.semaphore_wait(barrier, (nb - 1) + (nz - 1))
    start_faces(faces_a)

    unit = eye(channels, bf16)
    local_rows = lax.broadcasted_iota(jnp.int32, (voxels, voxels), 0)
    place = lax.broadcasted_iota(jnp.int32, (halo_rows, voxels), 0)
    past = place - 4 * per_list
    corner_code = jnp.where(
        lax.rem(past, CORNER) < 4, voxels + 4 * per_list + lax.div(past, CORNER) * 4 + lax.rem(past, CORNER), -1
    )
    halo_codes = jnp.where(past < 0, voxels + place, corner_code)

    def at(o):
        return pl.ds(pl.multiple_of(o * channels, 32), channels)

    def prepare(step, _):
        for u in range(UNROLL):
            o = step * UNROLL + u
            codes = nbr[0, pl.ds(o, 1), :]
            hot = one_hot(local_rows, codes)
            local_hot[o] = hot
            halo_hot[o] = one_hot(halo_codes, codes)
            got = nn(field[...], hot).astype(bf16)
            picked[0, at(o), :] = got[:channels]
            picked[1, at(OFFSETS - 1 - o), :] = got[channels:]
            turned[0, o] = nt(unit, w1[o]).astype(bf16)
            turned[1, o] = nt(unit, w2[o]).astype(bf16)
        return 0

    lax.fori_loop(0, OFFSETS // UNROLL, prepare, 0)
    tail = picked.shape[1] - OFFSETS * channels
    picked[:, OFFSETS * channels :, :] = jnp.zeros((2, tail, voxels), bf16)
    rest = half_rows - GROUPS * group_rows
    own[GROUPS * group_rows :, :] = jnp.zeros((rest, 128), f32)
    summed[GROUPS * group_rows :, :] = jnp.zeros((rest, 128), bf16)

    arrive_faces(faces_a)
    turned_halo = nt(eye(halo_a.shape[1], bf16)[:both], halo_a[...]).astype(bf16)
    zeros = jnp.zeros((channels, voxels), f32)

    def first_pass(step, sums):
        forth, back = sums
        for u in range(UNROLL):
            o = step * UNROLL + u
            mirror = OFFSETS - 1 - o
            got = nn(turned_halo, halo_hot[o]).astype(bf16)
            mine = picked[0, at(o), :] + got[:channels]
            theirs = picked[1, at(mirror), :] + got[channels:]
            picked[0, at(o), :] = mine
            picked[1, at(mirror), :] = theirs
            forth = forth + nn(w1[o], mine)
            back = back + nn(turned[1, mirror], theirs)
        return forth, back

    forth, back = lax.fori_loop(0, OFFSETS // UNROLL, first_pass, (zeros, zeros))
    pre = live_f * forth
    gate = 1.0 / (1.0 + jnp.exp(-pre))
    hidden = (live_f * (pre * gate)).astype(bf16)
    grad_pre = ((live_f * back) * gate * (1.0 + pre * (1.0 - gate))).astype(bf16)
    sides[0] = grad_pre
    sides[1] = hidden
    field[0:channels, :] = hidden
    field[channels:both, :] = grad_pre
    sent_c[:, 0:both] = nt(pick[...], field[...]).astype(bf16)
    sent_c[:, both:] = jnp.zeros((8 * per_list, sent_c.shape[1] - both), bf16)
    start_faces(faces_c)

    def core_copy(g):
        rows = pl.ds(pl.multiple_of(g * group_rows, 32), group_rows)
        return remote(to_core.at[rows, :], from_core.at[rows, :], sem_core, g, g, partner)

    def correlate(which, g):
        rows = pl.ds(pl.multiple_of(g * (GROUP * channels), 128), GROUP * channels)
        return nt(sides[which], picked[which, rows, :])

    def give(g, _):
        product = correlate(other, g)
        for t in range(group_rows // channels):
            rows = pl.ds(pl.multiple_of(g * group_rows + t * channels, 32), channels)
            to_core[rows, :] = product[:, t * 128 : (t + 1) * 128].astype(bf16)
        core_copy(g).start()
        return 0

    def keep(g, _):
        product = correlate(core, g)
        for t in range(group_rows // channels):
            rows = pl.ds(pl.multiple_of(g * group_rows + t * channels, 32), channels)
            own[rows, :] = product[:, t * 128 : (t + 1) * 128]
        return 0

    def join(g, _):
        core_copy(g).wait_recv()
        rows = pl.ds(pl.multiple_of(g * group_rows, 32), group_rows)
        total = own[rows, :] + from_core[rows, :].astype(f32)
        own[rows, :] = total
        summed[rows, :] = total.astype(bf16)
        return 0

    lax.fori_loop(0, GROUPS, give, 0)
    lax.fori_loop(0, GROUPS, keep, 0)
    lax.fori_loop(0, GROUPS, join, 0)

    def piece_rows(p):
        return pl.ds(pl.multiple_of(p * piece, piece), piece)

    def plane_copy(source, target):
        return remote(
            summed.at[piece_rows(target), :], arrived.at[source], sem_plane, source, target,
            (target * 2 + core, smp),
        )

    def loop(start, stop, act_on):
        def run(i, _):
            act_on(i)
            return 0

        lax.fori_loop(start, stop, run, 0)

    loop(1, nj, lambda i: plane_copy(chip, plane(i)).start())

    arrive_faces(faces_c)
    turned_halo_c = nt(eye(halo_c.shape[1], bf16)[:both], halo_c[...]).astype(bf16)

    def second_pass(step, sums):
        forth, back = sums
        for u in range(UNROLL):
            o = step * UNROLL + u
            got = (nn(field[...], local_hot[o]) + nn(turned_halo_c, halo_hot[o])).astype(bf16)
            forth = forth + nn(w2[o], got[:channels])
            back = back + nn(turned[0, OFFSETS - 1 - o], got[channels:])
        return forth, back

    forth, back = lax.fori_loop(0, OFFSETS // UNROLL, second_pass, (zeros, zeros))
    out_field[...] = (live_f * forth).astype(bf16)
    input_grad[...] = (live_f * back).astype(bf16)

    z_part[...] = own[piece_rows(chip), :]

    def add_piece(i):
        source = plane(i)
        plane_copy(source, source).wait_recv()
        z_part[...] += arrived[source].astype(f32)

    loop(1, nj, add_piece)

    def sliver_rows(s):
        return pl.ds(pl.multiple_of(s * sliver, 8), sliver)

    def z_copy(source, target):
        return remote(
            z_part.at[sliver_rows(target), :], z_in.at[source], sem_z, source, target, (blk, target)
        )

    def zg_copy(source, target):
        return remote(
            z_out.at[sliver_rows(source), :], z_out.at[sliver_rows(source), :], sem_zg, source, target,
            (blk, target),
        )

    loop(1, nz, lambda i: z_copy(smp, along(i)).start())
    z_in[smp] = z_part[sliver_rows(smp), :]
    loop(1, nz, lambda i: z_copy(along(i), along(i)).wait_recv())
    total = z_in[0]
    for s in range(1, nz):
        total = total + z_in[s]
    z_out[sliver_rows(smp), :] = total
    loop(1, nz, lambda i: zg_copy(smp, along(i)).start())
    loop(1, nz, lambda i: zg_copy(along(i), along(i)).wait_recv())

    def gather_copy(source, target):
        here = gathered.at[core, piece_rows(source), :]
        return remote(here, here, sem_gather, source, target, (target * 2 + core, smp))

    def forward_copy(which, p):
        here = gathered.at[which, piece_rows(p), :]
        return remote(here, here, sem_forward, p, p, partner)

    gathered[core, piece_rows(chip), :] = z_out[...].astype(bf16)
    loop(1, nj, lambda i: gather_copy(chip, plane(i)).start())
    forward_copy(core, chip).start()

    def hand_on(i):
        source = plane(i)
        gather_copy(source, source).wait_recv()
        forward_copy(core, source).start()

    loop(1, nj, hand_on)
    loop(0, nj, lambda p: forward_copy(other, p).wait_recv())

    finish_faces(faces_a)
    finish_faces(faces_c)
    loop(0, GROUPS, lambda g: core_copy(g).wait_send())
    loop(1, nj, lambda i: plane_copy(chip, plane(i)).wait_send())
    loop(1, nz, lambda i: z_copy(smp, along(i)).wait_send())
    loop(1, nz, lambda i: zg_copy(smp, along(i)).wait_send())
    loop(1, nj, lambda i: gather_copy(chip, plane(i)).wait_send())
    loop(0, nj, lambda p: forward_copy(core, p).wait_send())


def unpack_kernel(scale, sums, field_in, grad_in, first, second, field_out, grad_out):
    channels = first.shape[1]
    field_out[0] = field_in[...]
    grad_out[0] = grad_in[...]
    unit = eye(channels, jnp.bfloat16)
    tiles = GROUP * channels // 128
    for which, out in enumerate((first, second)):
        wide = jnp.concatenate(
            [sums[which, t * channels : (t + 1) * channels, :] for t in range(tiles)], axis=1
        )
        for k in range(GROUP):
            block = wide[:, k * channels : (k + 1) * channels]
            block = nt(unit, block) if which else block.astype(jnp.float32)
            out[k] = block * scale


def body(nb, nz, features, active, neighbour_rows, send_rows, first_weight, second_weight, cotangent):
    channels, voxels = features.shape[1], features.shape[2]
    both = 2 * channels
    per_list = send_rows.shape[3]
    halo_rows = 4 * per_list + 4 * CORNER
    nj = nb // 2
    half_rows = 2048
    piece = half_rows // nj
    bf16, f32 = jnp.bfloat16, jnp.float32
    vmem = pl.BlockSpec(memory_space=pltpu.VMEM)
    dma = pltpu.SemaphoreType.DMA
    wide = 256
    out_field, input_grad, gathered = pl.pallas_call(
        functools.partial(main_kernel, nb, nz),
        out_shape=[
            jax.ShapeDtypeStruct((channels, voxels), bf16),
            jax.ShapeDtypeStruct((channels, voxels), bf16),
            jax.ShapeDtypeStruct((2, half_rows, 128), bf16),
        ],
        in_specs=[vmem] * 7,
        out_specs=[vmem] * 3,
        scratch_shapes=[
            pltpu.VMEM((both, voxels), bf16),
            pltpu.VMEM((8 * per_list, voxels), bf16),
            pltpu.VMEM((8 * per_list, wide), bf16),
            pltpu.VMEM((halo_rows, wide), bf16),
            pltpu.VMEM((8 * per_list, wide), bf16),
            pltpu.VMEM((halo_rows, wide), bf16),
            pltpu.VMEM((OFFSETS, voxels, voxels), bf16),
            pltpu.VMEM((OFFSETS, halo_rows, voxels), bf16),
            pltpu.VMEM((2, OFFSETS, channels, channels), bf16),
            pltpu.VMEM((2, GROUP * GROUPS * channels, voxels), bf16),
            pltpu.VMEM((2, channels, voxels), bf16),
            pltpu.VMEM((half_rows, 128), bf16),
            pltpu.VMEM((half_rows, 128), f32),
            pltpu.VMEM((half_rows, 128), bf16),
            pltpu.VMEM((half_rows, 128), bf16),
            pltpu.VMEM((nj, piece, 128), bf16),
            pltpu.VMEM((piece, 128), f32),
            pltpu.VMEM((nz, piece // nz, 128), f32),
            pltpu.VMEM((piece, 128), f32),
            dma((2, 8)),
            dma((2, 8)),
            dma((2, GROUPS)),
            dma((2, nj)),
            dma((2, nz)),
            dma((2, nz)),
            dma((2, nj)),
            dma((2, nj)),
        ],
        compiler_params=pltpu.CompilerParams(
            collective_id=0, has_side_effects=True, vmem_limit_bytes=40 * 2**20
        ),
        name="halo_conv_and_sum",
    )(features, active, neighbour_rows, send_rows, first_weight, second_weight, cotangent)

    slots = lax.axis_size("smp") * features.shape[0] * nb * voxels
    group_rows = GROUP * channels * channels // 128
    whole = pl.BlockSpec((channels, voxels), lambda g: (0, 0))
    whole_out = pl.BlockSpec((1, channels, voxels), lambda g: (0, 0, 0))
    grads = pl.BlockSpec((GROUP, channels, channels), lambda g: (g, 0, 0))
    first_grad, second_grad, out_field, input_grad = pl.pallas_call(
        functools.partial(unpack_kernel, 1.0 / slots**0.5),
        grid=(GROUPS,),
        out_shape=[
            jax.ShapeDtypeStruct((OFFSETS, channels, channels), f32),
            jax.ShapeDtypeStruct((OFFSETS, channels, channels), f32),
            jax.ShapeDtypeStruct((1, channels, voxels), bf16),
            jax.ShapeDtypeStruct((1, channels, voxels), bf16),
        ],
        in_specs=[pl.BlockSpec((2, group_rows, 128), lambda g: (0, g, 0)), whole, whole],
        out_specs=[grads, grads, whole_out, whole_out],
        name="unpack",
    )(gathered, out_field, input_grad)
    return out_field, input_grad, first_grad, second_grad


def solution(mesh):
    return jax.shard_map(
        functools.partial(body, mesh.shape["blk"], mesh.shape["smp"]),
        mesh=mesh,
        in_specs=(
            P("smp", None, "blk"),
            P("smp", "blk"),
            P("smp", None, "blk"),
            P("smp", "blk", None, None),
            P(),
            P(),
            P("smp", None, "blk"),
        ),
        out_specs=(P("smp", None, "blk"), P("smp", None, "blk"), P(), P()),
        check_vma=False,
    )
```

```python
import functools

import jax
import jax.numpy as jnp
from jax import lax
from jax.experimental import pallas as pl
from jax.experimental.pallas import tpu as pltpu
from jax.sharding import PartitionSpec as P

MESH = pl.DeviceIdType.MESH
TALL = 4
STEPS = ((-1, 0), (1, 0), (0, -1), (0, 1), (-1, -1), (-1, 1), (1, -1), (1, 1))
DELTAS = tuple(a * TALL + b for a, b in STEPS)
OFFSETS = 27
GROUP = 4
GROUPS = 7
CORNER = 16
UNROLL = 3


def nn(a, b):
    return lax.dot_general(a, b, (((1,), (0,)), ((), ())), preferred_element_type=jnp.float32)


def nt(a, b):
    return lax.dot_general(a, b, (((1,), (1,)), ((), ())), preferred_element_type=jnp.float32)


def eye(n, dtype):
    rows = lax.broadcasted_iota(jnp.int32, (n, n), 0)
    cols = lax.broadcasted_iota(jnp.int32, (n, n), 1)
    return (rows == cols).astype(jnp.float32).astype(dtype)


def one_hot(rows, codes):
    return jnp.where(rows == codes, 1.0, 0.0).astype(jnp.bfloat16)


def far_quarter(smp, nz):
    per_quarter = nz // 4
    late = lax.rem(smp, per_quarter) >= per_quarter // 2
    return lax.rem(lax.div(smp, per_quarter) + jnp.where(late, 2, 1), 4)


def main_kernel(
    nb, nz,
    feat_in, act_in, nbr_in, lists_in, w1_in, w2_in, cot_in,
    out_field, input_grad, gathered,
    feat, act, nbr, lists, w1, w2, cot, results, spreading,
    field, pick, sent_a, halo_a, sent_c, halo_c,
    local_hot, halo_hot, turned, picked, sides,
    to_core, own, from_core, summed, arrived, z_part, z_in, z_out,
    sem_in, sem_out, sem_a, sem_c, sem_core, sem_plane, sem_z, sem_zg, sem_gather, sem_keep, sem_forward,
):
    bf16, f32 = jnp.bfloat16, jnp.float32
    channels, voxels = feat.shape[1], feat.shape[2]
    both = 2 * channels
    per_list = lists.shape[3]
    halo_rows = halo_a.shape[0]
    nj = nb // 2
    half_rows = own.shape[0]
    piece = half_rows // nj
    sliver = piece // nz
    quarter = piece // 4
    some = piece // 2
    group_rows = GROUP * channels * channels // 128
    tiles = GROUP * channels // 128
    blk = lax.axis_index("blk")
    smp = lax.axis_index("smp")
    core = lax.rem(blk, 2)
    chip = lax.div(blk, 2)
    other = 1 - core
    partner = (chip * 2 + other, smp)

    def loop(start, stop, act_on):
        def run(i, _):
            act_on(i)
            return 0

        lax.fori_loop(start, stop, run, 0)

    far = far_quarter(smp, nz)
    near = lax.rem(far + 2, 4)

    def plane(i):
        return lax.rem(chip + i, nj)

    def along(i):
        return lax.rem(smp + i, nz)

    def remote(src, dst, sems, source, target, device):
        return pltpu.make_async_remote_copy(
            src_ref=src, dst_ref=dst, send_sem=sems.at[0, target], recv_sem=sems.at[1, source],
            device_id=device, device_id_type=MESH,
        )

    loads = [
        pltpu.make_async_copy(src, dst, sem_in.at[i])
        for i, (src, dst) in enumerate(
            ((feat_in, feat), (cot_in, cot), (act_in, act), (lists_in, lists), (nbr_in, nbr), (w1_in, w1), (w2_in, w2))
        )
    ]
    for load in loads:
        load.start()
    halo_a[...] = jnp.zeros_like(halo_a)
    halo_c[...] = jnp.zeros_like(halo_c)
    barrier = pltpu.get_barrier_semaphore()

    def greet_blk(i, _):
        pl.semaphore_signal(
            barrier, inc=1, device_id=(lax.rem(blk + i, nb), smp), device_id_type=MESH
        )
        return 0

    def greet_smp(i, _):
        pl.semaphore_signal(barrier, inc=1, device_id=(blk, along(i)), device_id_type=MESH)
        return 0

    lax.fori_loop(1, nb, greet_blk, 0)
    lax.fori_loop(1, nz, greet_smp, 0)

    for load in loads[:4]:
        load.wait()
    live = act[...] > 0
    live_f = live.astype(f32)
    field[0:channels, :] = jnp.where(live, feat[0].astype(f32), 0.0).astype(bf16)
    field[channels:both, :] = jnp.where(live, cot[0].astype(f32), 0.0).astype(bf16)

    spread = jnp.concatenate(
        [jnp.broadcast_to(lists[0, 0, d : d + 1, :], (per_list, per_list)) for d in range(8)], axis=0
    )
    at_row = lax.broadcasted_iota(jnp.int32, spread.shape, 0)
    at_col = lax.broadcasted_iota(jnp.int32, spread.shape, 1)
    column = jnp.sum(jnp.where(lax.rem(at_row, per_list) == at_col, spread, 0), axis=1, keepdims=True)
    pick[...] = one_hot(lax.broadcasted_iota(jnp.int32, (8 * per_list, voxels), 1), column)

    def face_copies(sent, halo, sems):
        copies = []
        for d, delta in enumerate(DELTAS):
            if d < 4:
                rows = pl.ds(d * per_list, per_list)
                into = rows
            else:
                rows = pl.ds(d * per_list, CORNER)
                into = pl.ds(4 * per_list + (d - 4) * CORNER, CORNER)
            target, source = blk + delta, blk - delta
            copy = pltpu.make_async_remote_copy(
                src_ref=sent.at[rows, :], dst_ref=halo.at[into, :],
                send_sem=sems.at[0, d], recv_sem=sems.at[1, d],
                device_id=(jnp.clip(target, 0, nb - 1), smp), device_id_type=MESH,
            )
            has_target = (target >= 0) & (target < nb)
            has_source = (source >= 0) & (source < nb)
            copies.append((copy, has_target, has_source))
        return copies

    def start_faces(copies):
        for copy, has_target, _ in copies:
            pl.when(has_target)(copy.start)

    def arrive_faces(copies):
        for copy, _, has_source in copies:
            pl.when(has_source)(copy.wait_recv)

    def finish_faces(copies):
        for copy, has_target, _ in copies:
            pl.when(has_target)(copy.wait_send)

    faces_a = face_copies(sent_a, halo_a, sem_a)
    faces_c = face_copies(sent_c, halo_c, sem_c)
    sent_a[:, 0:both] = nt(pick[...], field[...]).astype(bf16)
    sent_a[:, both:] = jnp.zeros((8 * per_list, sent_a.shape[1] - both), bf16)
    pl.semaphore_wait(barrier, (nb - 1) + (nz - 1))
    start_faces(faces_a)

    for load in loads[4:]:
        load.wait()
    unit = eye(channels, bf16)
    local_rows = lax.broadcasted_iota(jnp.int32, (voxels, voxels), 0)
    place = lax.broadcasted_iota(jnp.int32, (halo_rows, voxels), 0)
    past = place - 4 * per_list
    corner_code = jnp.where(
        lax.rem(past, CORNER) < 4, voxels + 4 * per_list + lax.div(past, CORNER) * 4 + lax.rem(past, CORNER), -1
    )
    halo_codes = jnp.where(past < 0, voxels + place, corner_code)

    def at(o):
        return pl.ds(pl.multiple_of(o * channels, 32), channels)

    def prepare(step, _):
        for u in range(UNROLL):
            o = step * UNROLL + u
            codes = nbr[o]
            hot = one_hot(local_rows, codes)
            local_hot[o] = hot
            halo_hot[o] = one_hot(halo_codes, codes)
            got = nn(field[...], hot).astype(bf16)
            picked[0, at(o), :] = got[:channels]
            picked[1, at(OFFSETS - 1 - o), :] = got[channels:]
            turned[0, o] = nt(unit, w1[o]).astype(bf16)
            turned[1, o] = nt(unit, w2[o]).astype(bf16)
        return 0

    lax.fori_loop(0, OFFSETS // UNROLL, prepare, 0)
    tail = picked.shape[1] - OFFSETS * channels
    picked[:, OFFSETS * channels :, :] = jnp.zeros((2, tail, voxels), bf16)
    rest = half_rows - GROUPS * group_rows
    own[GROUPS * group_rows :, :] = jnp.zeros((rest, 128), f32)
    from_core[GROUPS * group_rows :, :] = jnp.zeros((rest, 128), bf16)

    arrive_faces(faces_a)
    turned_halo = nt(eye(halo_a.shape[1], bf16)[:both], halo_a[...]).astype(bf16)
    zeros = jnp.zeros((channels, voxels), f32)

    def first_pass(step, sums):
        forth, back = sums
        for u in range(UNROLL):
            o = step * UNROLL + u
            mirror = OFFSETS - 1 - o
            got = nn(turned_halo, halo_hot[o]).astype(bf16)
            mine = picked[0, at(o), :] + got[:channels]
            theirs = picked[1, at(mirror), :] + got[channels:]
            picked[0, at(o), :] = mine
            picked[1, at(mirror), :] = theirs
            forth = forth + nn(w1[o], mine)
            back = back + nn(turned[1, mirror], theirs)
        return forth, back

    forth, back = lax.fori_loop(0, OFFSETS // UNROLL, first_pass, (zeros, zeros))
    pre = live_f * forth
    gate = 1.0 / (1.0 + jnp.exp(-pre))
    hidden = (live_f * (pre * gate)).astype(bf16)
    grad_pre = ((live_f * back) * gate * (1.0 + pre * (1.0 - gate))).astype(bf16)
    sides[0] = grad_pre
    sides[1] = hidden
    field[0:channels, :] = hidden
    field[channels:both, :] = grad_pre
    sent_c[:, 0:both] = nt(pick[...], field[...]).astype(bf16)
    sent_c[:, both:] = jnp.zeros((8 * per_list, sent_c.shape[1] - both), bf16)
    start_faces(faces_c)

    def core_copy(g):
        rows = pl.ds(pl.multiple_of(g * group_rows, 32), group_rows)
        return remote(to_core.at[rows, :], from_core.at[rows, :], sem_core, g, g, partner)

    def correlate(which, g):
        rows = pl.ds(pl.multiple_of(g * (GROUP * channels), 128), GROUP * channels)
        if which == 0:
            return nt(sides[0], picked[0, rows, :])
        tall = nt(picked[1, rows, :], sides[1])
        return jnp.concatenate([tall[k * channels : (k + 1) * channels] for k in range(GROUP)], axis=1)

    def tile_rows(g, t):
        return pl.ds(pl.multiple_of(g * group_rows + t * channels, 32), channels)

    def give(which, g):
        product = correlate(which, g)
        for t in range(tiles):
            to_core[tile_rows(g, t), :] = product[:, t * 128 : (t + 1) * 128].astype(bf16)
        core_copy(g).start()

    def keep(which, g):
        product = correlate(which, g)
        for t in range(tiles):
            own[tile_rows(g, t), :] = product[:, t * 128 : (t + 1) * 128]

    def join():
        done = 0
        for p in range(nj):
            while done < GROUPS and done * group_rows < (p + 1) * piece:
                core_copy(done).wait_recv()
                done += 1
            rows = pl.ds(p * piece, piece)
            total = own[rows, :] + from_core[rows, :].astype(f32)
            own[rows, :] = total
            summed[p, 0:piece, :] = total.astype(bf16)
            summed[p, piece:, :] = total[:quarter].astype(bf16)

    for which in range(2):

        @pl.when(other == which)
        def _():
            loop(0, GROUPS, functools.partial(give, which))

    for which in range(2):

        @pl.when(core == which)
        def _():
            loop(0, GROUPS, functools.partial(keep, which))

    join()

    def quarter_rows(q):
        return pl.ds(pl.multiple_of(q * quarter, 8), quarter)

    starts = (far, near)

    def plane_copy(part, source, target):
        rows = pl.ds(pl.multiple_of(starts[part] * quarter, 8), some)
        return pltpu.make_async_remote_copy(
            src_ref=summed.at[target, rows, :], dst_ref=arrived.at[part, source],
            send_sem=sem_plane.at[0, part, target], recv_sem=sem_plane.at[1, part, source],
            device_id=(target * 2 + core, smp), device_id_type=MESH,
        )

    for part in range(2):
        loop(1, nj, lambda i: plane_copy(part, chip, plane(i)).start())

    arrive_faces(faces_c)
    turned_halo_c = nt(eye(halo_c.shape[1], bf16)[:both], halo_c[...]).astype(bf16)

    def second_pass(step, sums):
        forth, back = sums
        for u in range(UNROLL):
            o = step * UNROLL + u
            got = (nn(field[...], local_hot[o]) + nn(turned_halo_c, halo_hot[o])).astype(bf16)
            forth = forth + nn(w2[o], got[:channels])
            back = back + nn(turned[0, OFFSETS - 1 - o], got[channels:])
        return forth, back

    forth, back = lax.fori_loop(0, OFFSETS // UNROLL, second_pass, (zeros, zeros))
    results[0] = (live_f * forth).astype(bf16)
    results[1] = (live_f * back).astype(bf16)
    keeps = [
        pltpu.make_async_copy(results.at[0], out_field, sem_out.at[0]),
        pltpu.make_async_copy(results.at[1], input_grad, sem_out.at[1]),
    ]
    for copy in keeps:
        copy.start()

    def z_copy(source, target, rows):
        return remote(z_part.at[rows, :], z_in.at[source], sem_z, source, target, (blk, target))

    def z_sends(part, act_on):
        def run(k):
            target = lax.rem(starts[part] * (nz // 4) + k, nz)
            rows = pl.ds(pl.multiple_of(part * some + k * sliver, 8), sliver)

            if part == 0:
                act_on(target, rows)
            else:

                @pl.when(target != smp)
                def _():
                    act_on(target, rows)

        loop(0, nz // 2, run)

    base = pl.multiple_of(chip * piece, piece)
    for part in range(2):
        for k in range(2):
            first_row = base + lax.rem(starts[part] + k, 4) * quarter
            z_part[part * some + k * quarter : part * some + (k + 1) * quarter, :] = own[
                pl.ds(pl.multiple_of(first_row, 8), quarter), :
            ]

        def add_piece(i):
            source = plane(i)
            plane_copy(part, source, source).wait_recv()
            z_part[part * some : (part + 1) * some, :] += arrived[part, source].astype(f32)

        loop(1, nj, add_piece)
        z_sends(part, lambda target, rows: z_copy(smp, target, rows).start())

    place_here = lax.rem(smp + nz - near * (nz // 4), nz)
    total = z_part[pl.ds(pl.multiple_of(some + place_here * sliver, 8), sliver), :]

    def add_sliver(i, running):
        source = along(i)
        z_copy(source, source, pl.ds(0, sliver)).wait_recv()
        return running + z_in[source]

    total = lax.fori_loop(1, nz, add_sliver, total)

    def sliver_rows(s):
        return pl.ds(pl.multiple_of(s * sliver, 8), sliver)

    def zg_copy(source, target):
        return remote(
            z_out.at[sliver_rows(source), :], z_out.at[sliver_rows(source), :], sem_zg, source, target,
            (blk, target),
        )

    z_out[sliver_rows(smp), :] = total
    loop(0, nz - 1, lambda i: zg_copy(smp, along(lax.rem(i + nz // 2 - 1, nz - 1) + 1)).start())

    def gather_copy(part, source, target):
        return pltpu.make_async_remote_copy(
            src_ref=spreading.at[chip, part], dst_ref=spreading.at[source, part],
            send_sem=sem_gather.at[0, part, target], recv_sem=sem_gather.at[1, part, source],
            device_id=(target * 2 + core, smp), device_id_type=MESH,
        )

    def keep_copy(part, p):
        return pltpu.make_async_copy(spreading.at[p, part], gathered.at[core, p, part], sem_keep.at[part, p])

    def forward_copy(which, part, p):
        return pltpu.make_async_remote_copy(
            src_ref=spreading.at[p, part], dst_ref=gathered.at[which, p, part],
            send_sem=sem_forward.at[0, part, p], recv_sem=sem_forward.at[1, part, p],
            device_id=partner, device_id_type=MESH,
        )

    def store(part, p):
        keep_copy(part, p).start()
        forward_copy(core, part, p).start()

    for part, start in enumerate((near, far)):

        def sliver_here(k):
            source = lax.rem(start * (nz // 4) + k, nz)
            if part == 0:
                pl.when(source != smp)(lambda: zg_copy(source, source).wait_recv())
            else:
                zg_copy(source, source).wait_recv()

        loop(0, nz // 2, sliver_here)
        for k in range(2):
            spreading[chip, part, k * quarter : (k + 1) * quarter, :] = z_out[
                quarter_rows(lax.rem(start + k, 4)), :
            ].astype(bf16)
        loop(1, nj, lambda i: gather_copy(part, chip, plane(i)).start())
        store(part, chip)

    for part in range(2):

        def hand_on(i):
            source = plane(i)
            gather_copy(part, source, source).wait_recv()
            store(part, source)

        loop(1, nj, hand_on)

    finish_faces(faces_a)
    finish_faces(faces_c)
    loop(0, GROUPS, lambda g: core_copy(g).wait_send())
    for part in range(2):
        loop(1, nj, lambda i: plane_copy(part, chip, plane(i)).wait_send())
        z_sends(part, lambda target, rows: z_copy(smp, target, rows).wait_send())
        loop(1, nj, lambda i: gather_copy(part, chip, plane(i)).wait_send())
    loop(1, nz, lambda i: zg_copy(smp, along(i)).wait_send())
    for copy in keeps:
        copy.wait()
    for part in range(2):

        def settle(p):
            keep_copy(part, p).wait()
            forward_copy(core, part, p).wait_send()
            forward_copy(other, part, p).wait_recv()

        loop(0, nj, settle)


def unpack_kernel(
    nj, nz, scale, field_in, grad_in, gathered, first, second, field_out, grad_out,
    fields, stage, wide_sums, sem_field, sem_in, sem_out,
):
    channels, offsets = first.shape[1], first.shape[0]
    half_rows = stage.shape[1]
    quarter = half_rows // nj // 4
    group_rows = GROUP * channels * channels // 128
    tiles = GROUP * channels // 128
    run = 32
    near = lax.rem(far_quarter(lax.axis_index("smp"), nz) + 2, 4)
    turned = [pl.multiple_of(lax.rem(q + 4 - near, 4) * quarter, 8) for q in range(4)]

    def load(which, k):
        rows = pl.ds(k * (half_rows // 4), half_rows // 4)
        return pltpu.make_async_copy(gathered.at[which, rows], stage.at[which, rows], sem_in.at[which, k])

    def save(which, g):
        some = pl.ds(g * GROUP, min(GROUP, offsets - g * GROUP))
        return pltpu.make_async_copy(
            wide_sums.at[which, some], (first, second)[which].at[some], sem_out.at[which, g]
        )

    loads = [pltpu.make_async_copy(x, fields.at[i], sem_field.at[0, i]) for i, x in enumerate((field_in, grad_in))]
    saves = [
        pltpu.make_async_copy(fields.at[i], x.at[0], sem_field.at[1, i]) for i, x in enumerate((field_out, grad_out))
    ]
    for which in range(2):
        for k in range(4):
            load(which, k).start()
    for copy in loads:
        copy.start()
    for which in range(2):
        here = 0
        for g in range(GROUPS):
            while here < 4 and here * (half_rows // 4) < (g + 1) * group_rows:
                load(which, here).wait()
                here += 1

            def part_of(row):
                first_row = row - row % (quarter * 4) + turned[row // quarter % 4] + row % quarter
                return stage[which, pl.ds(pl.multiple_of(first_row, 8), run), :].astype(jnp.float32)

            parts = [part_of(g * group_rows + n) for n in range(0, group_rows, run)]
            step = channels // run
            wide = jnp.concatenate(
                [jnp.concatenate(parts[t * step : (t + 1) * step], axis=0) for t in range(tiles)], axis=1
            )
            wide = wide * scale
            for k in range(GROUP):
                wide_sums[which, g * GROUP + k] = wide[:, k * channels : (k + 1) * channels]
            save(which, g).start()
    for copy in loads:
        copy.wait()
    for copy in saves:
        copy.start()
    for which in range(2):
        for g in range(GROUPS):
            save(which, g).wait()
    for copy in saves:
        copy.wait()


def body(nb, nz, features, active, neighbour_rows, send_rows, first_weight, second_weight, cotangent):
    channels, voxels = features.shape[1], features.shape[2]
    both = 2 * channels
    per_list = send_rows.shape[3]
    halo_rows = 4 * per_list + 4 * CORNER
    nj = nb // 2
    half_rows = 2048
    piece = half_rows // nj
    bf16, f32 = jnp.bfloat16, jnp.float32
    anywhere = pl.BlockSpec(memory_space=pl.ANY)
    slots = lax.axis_size("smp") * features.shape[0] * nb * voxels
    table = jnp.transpose(neighbour_rows, (1, 0, 2))
    operands = (features, active, table, send_rows, first_weight, second_weight, cotangent)
    dma = pltpu.SemaphoreType.DMA
    wide = 256
    out_field, input_grad, gathered = pl.pallas_call(
        functools.partial(main_kernel, nb, nz),
        out_shape=[
            jax.ShapeDtypeStruct((channels, voxels), bf16),
            jax.ShapeDtypeStruct((channels, voxels), bf16),
            jax.ShapeDtypeStruct((2, nj, 2, piece // 2, 128), bf16),
        ],
        in_specs=[anywhere] * 7,
        out_specs=[anywhere] * 3,
        scratch_shapes=[
            *(pltpu.VMEM(x.shape, x.dtype) for x in operands),
            pltpu.VMEM((2, channels, voxels), bf16),
            pltpu.VMEM((nj, 2, piece // 2, 128), bf16),
            pltpu.VMEM((both, voxels), bf16),
            pltpu.VMEM((8 * per_list, voxels), bf16),
            pltpu.VMEM((8 * per_list, wide), bf16),
            pltpu.VMEM((halo_rows, wide), bf16),
            pltpu.VMEM((8 * per_list, wide), bf16),
            pltpu.VMEM((halo_rows, wide), bf16),
            pltpu.VMEM((OFFSETS, voxels, voxels), bf16),
            pltpu.VMEM((OFFSETS, halo_rows, voxels), bf16),
            pltpu.VMEM((2, OFFSETS, channels, channels), bf16),
            pltpu.VMEM((2, GROUP * GROUPS * channels, voxels), bf16),
            pltpu.VMEM((2, channels, voxels), bf16),
            pltpu.VMEM((half_rows, 128), bf16),
            pltpu.VMEM((half_rows, 128), f32),
            pltpu.VMEM((half_rows, 128), bf16),
            pltpu.VMEM((nj, piece + piece // 4, 128), bf16),
            pltpu.VMEM((2, nj, piece // 2, 128), bf16),
            pltpu.VMEM((piece, 128), f32),
            pltpu.VMEM((nz, piece // nz, 128), f32),
            pltpu.VMEM((piece, 128), f32),
            dma((7,)),
            dma((2,)),
            dma((2, 8)),
            dma((2, 8)),
            dma((2, GROUPS)),
            dma((2, 2, nj)),
            dma((2, nz)),
            dma((2, nz)),
            dma((2, 2, nj)),
            dma((2, nj)),
            dma((2, 2, nj)),
        ],
        compiler_params=pltpu.CompilerParams(
            collective_id=0, has_side_effects=True, vmem_limit_bytes=56 * 2**20
        ),
        name="halo_conv_and_sum",
    )(*operands)

    grad = jax.ShapeDtypeStruct((OFFSETS, channels, channels), f32)
    field = jax.ShapeDtypeStruct((1, channels, voxels), bf16)
    first_grad, second_grad, out_field, input_grad = pl.pallas_call(
        functools.partial(unpack_kernel, nj, nz, 1.0 / slots**0.5),
        out_shape=[grad, grad, field, field],
        in_specs=[anywhere] * 3,
        out_specs=[anywhere] * 4,
        scratch_shapes=[
            pltpu.VMEM((2, channels, voxels), bf16),
            pltpu.VMEM((2, half_rows, 128), bf16),
            pltpu.VMEM((2, GROUP * GROUPS, channels, channels), f32),
            dma((2, 2)),
            dma((2, 4)),
            dma((2, GROUPS)),
        ],
        compiler_params=pltpu.CompilerParams(vmem_limit_bytes=56 * 2**20),
        name="unpack",
    )(out_field, input_grad, gathered.reshape(2, half_rows, 128))
    return out_field, input_grad, first_grad, second_grad


def solution(mesh):
    return jax.shard_map(
        functools.partial(body, mesh.shape["blk"], mesh.shape["smp"]),
        mesh=mesh,
        in_specs=(
            P("smp", None, "blk"),
            P("smp", "blk"),
            P("smp", None, "blk"),
            P("smp", "blk", None, None),
            P(),
            P(),
            P("smp", None, "blk"),
        ),
        out_specs=(P("smp", None, "blk"), P("smp", None, "blk"), P(), P()),
        check_vma=False,
    )
```

```python
import functools

import jax
import jax.numpy as jnp
from jax import lax
from jax.experimental import pallas as pl
from jax.experimental.pallas import tpu as pltpu
from jax.sharding import PartitionSpec as P

MESH = pl.DeviceIdType.MESH
TALL = 4
STEPS = ((-1, 0), (1, 0), (0, -1), (0, 1), (-1, -1), (-1, 1), (1, -1), (1, 1))
DELTAS = tuple(a * TALL + b for a, b in STEPS)
OFFSETS = 27
GROUP = 4
GROUPS = 7
CORNER = 16
UNROLL = 9


def nn(a, b):
    return lax.dot_general(a, b, (((1,), (0,)), ((), ())), preferred_element_type=jnp.float32)


def nt(a, b):
    return lax.dot_general(a, b, (((1,), (1,)), ((), ())), preferred_element_type=jnp.float32)


def eye(n, dtype):
    rows = lax.broadcasted_iota(jnp.int32, (n, n), 0)
    cols = lax.broadcasted_iota(jnp.int32, (n, n), 1)
    return (rows == cols).astype(jnp.float32).astype(dtype)


def one_hot(rows, codes):
    return jnp.where(rows == codes, 1.0, 0.0).astype(jnp.bfloat16)


def far_quarter(smp, nz):
    per_quarter = nz // 4
    late = lax.rem(smp, per_quarter) >= per_quarter // 2
    return lax.rem(lax.div(smp, per_quarter) + jnp.where(late, 2, 1), 4)


def main_kernel(
    nb, nz,
    feat_in, act_in, nbr_in, lists_in, w1_in, w2_in, cot_in,
    out_field, input_grad, gathered,
    feat, act, nbr, lists, w1, w2, cot, results, spreading,
    field, pick, sent_a, halo_a, sent_c, halo_c,
    local_hot, halo_hot, turned, picked, sides,
    to_core, own, from_core, summed, arrived, z_part, z_in, z_out,
    heard, sem_in, sem_out, sem_a, sem_c, sem_core, sem_plane, sem_z, sem_zg, sem_gather, sem_keep, sem_forward,
):
    bf16, f32 = jnp.bfloat16, jnp.float32
    channels, voxels = feat.shape[1], feat.shape[2]
    both = 2 * channels
    per_list = lists.shape[3]
    halo_rows = halo_a.shape[0]
    nj = nb // 2
    half_rows = own.shape[0]
    piece = half_rows // nj
    sliver = piece // nz
    quarter = piece // 4
    some = piece // 2
    group_rows = GROUP * channels * channels // 128
    tiles = GROUP * channels // 128
    blk = lax.axis_index("blk")
    smp = lax.axis_index("smp")
    core = lax.rem(blk, 2)
    chip = lax.div(blk, 2)
    other = 1 - core
    partner = (chip * 2 + other, smp)

    def loop(start, stop, act_on):
        def run(i, _):
            act_on(i)
            return 0

        lax.fori_loop(start, stop, run, 0)

    far = far_quarter(smp, nz)
    near = lax.rem(far + 2, 4)

    def plane(i):
        return lax.rem(chip + i, nj)

    def along(i):
        return lax.rem(smp + i, nz)

    def remote(src, dst, sems, source, target, device):
        return pltpu.make_async_remote_copy(
            src_ref=src, dst_ref=dst, send_sem=sems.at[0, target], recv_sem=sems.at[1, source],
            device_id=device, device_id_type=MESH,
        )

    loads = [
        pltpu.make_async_copy(src, dst, sem_in.at[i])
        for i, (src, dst) in enumerate(
            ((feat_in, feat), (cot_in, cot), (act_in, act), (lists_in, lists), (nbr_in, nbr), (w1_in, w1), (w2_in, w2))
        )
    ]
    for load in loads:
        load.start()
    halo_a[...] = jnp.zeros_like(halo_a)
    halo_c[...] = jnp.zeros_like(halo_c)
    barrier = pltpu.get_barrier_semaphore()

    def greet_blk(i, _):
        pl.semaphore_signal(
            barrier, inc=1, device_id=(lax.rem(blk + i, nb), smp), device_id_type=MESH
        )
        return 0

    def greet_smp(i, _):
        pl.semaphore_signal(barrier, inc=1, device_id=(blk, along(i)), device_id_type=MESH)
        return 0

    def tell(step):
        for i in (1 << step, nz - (1 << step)):
            pl.semaphore_signal(heard.at[step], inc=1, device_id=(blk, along(i)), device_id_type=MESH)

    def hear(step):
        pl.semaphore_wait(heard.at[step], 2)

    rounds = max(nz // 4, 1).bit_length()
    lax.fori_loop(1, nb, greet_blk, 0)
    for i in (1, nz - 1):
        greet_smp(i, 0)

    for load in loads[:4]:
        load.wait()
    live = act[...] > 0
    live_f = live.astype(f32)
    field[0:channels, :] = jnp.where(live, feat[0].astype(f32), 0.0).astype(bf16)
    field[channels:both, :] = jnp.where(live, cot[0].astype(f32), 0.0).astype(bf16)

    spread = jnp.concatenate(
        [jnp.broadcast_to(lists[0, 0, d : d + 1, :], (per_list, per_list)) for d in range(8)], axis=0
    )
    at_row = lax.broadcasted_iota(jnp.int32, spread.shape, 0)
    at_col = lax.broadcasted_iota(jnp.int32, spread.shape, 1)
    column = jnp.sum(jnp.where(lax.rem(at_row, per_list) == at_col, spread, 0), axis=1, keepdims=True)
    pick[...] = one_hot(lax.broadcasted_iota(jnp.int32, (8 * per_list, voxels), 1), column)

    def face_copies(sent, halo, sems):
        copies = []
        for d, delta in enumerate(DELTAS):
            if d < 4:
                rows = pl.ds(d * per_list, per_list)
                into = rows
            else:
                rows = pl.ds(d * per_list, CORNER)
                into = pl.ds(4 * per_list + (d - 4) * CORNER, CORNER)
            target, source = blk + delta, blk - delta
            copy = pltpu.make_async_remote_copy(
                src_ref=sent.at[rows, :], dst_ref=halo.at[into, :],
                send_sem=sems.at[0, d], recv_sem=sems.at[1, d],
                device_id=(jnp.clip(target, 0, nb - 1), smp), device_id_type=MESH,
            )
            has_target = (target >= 0) & (target < nb)
            has_source = (source >= 0) & (source < nb)
            copies.append((copy, has_target, has_source))
        return copies

    def start_faces(copies):
        for copy, has_target, _ in copies:
            pl.when(has_target)(copy.start)

    def arrive_faces(copies):
        for copy, _, has_source in copies:
            pl.when(has_source)(copy.wait_recv)

    def finish_faces(copies):
        for copy, has_target, _ in copies:
            pl.when(has_target)(copy.wait_send)

    faces_a = face_copies(sent_a, halo_a, sem_a)
    faces_c = face_copies(sent_c, halo_c, sem_c)
    sent_a[:, 0:both] = nt(pick[...], field[...]).astype(bf16)
    sent_a[:, both:] = jnp.zeros((8 * per_list, sent_a.shape[1] - both), bf16)
    pl.semaphore_wait(barrier, (nb - 1) + 2)
    start_faces(faces_a)
    tell(0)

    for load in loads[4:]:
        load.wait()
    unit = eye(channels, bf16)
    local_rows = lax.broadcasted_iota(jnp.int32, (voxels, voxels), 0)
    place = lax.broadcasted_iota(jnp.int32, (halo_rows, voxels), 0)
    past = place - 4 * per_list
    corner_code = jnp.where(
        lax.rem(past, CORNER) < 4, voxels + 4 * per_list + lax.div(past, CORNER) * 4 + lax.rem(past, CORNER), -1
    )
    halo_codes = jnp.where(past < 0, voxels + place, corner_code)

    def at(o):
        return pl.ds(pl.multiple_of(o * channels, 32), channels)

    def prepare(step, _):
        for u in range(UNROLL):
            o = step * UNROLL + u
            codes = nbr[o]
            hot = one_hot(local_rows, codes)
            local_hot[o] = hot
            halo_hot[o] = one_hot(halo_codes, codes)
            got = nn(field[...], hot).astype(bf16)
            picked[0, at(o), :] = got[:channels]
            picked[1, at(OFFSETS - 1 - o), :] = got[channels:]
            turned[0, o] = nt(unit, w1[o]).astype(bf16)
            turned[1, o] = nt(unit, w2[o]).astype(bf16)
        return 0

    lax.fori_loop(0, OFFSETS // UNROLL, prepare, 0)
    tail = picked.shape[1] - OFFSETS * channels
    picked[:, OFFSETS * channels :, :] = jnp.zeros((2, tail, voxels), bf16)
    rest = half_rows - GROUPS * group_rows
    own[GROUPS * group_rows :, :] = jnp.zeros((rest, 128), f32)
    from_core[GROUPS * group_rows :, :] = jnp.zeros((rest, 128), bf16)

    for step in range(1, rounds):
        hear(step - 1)
        tell(step)
        if step == 1:
            break
    arrive_faces(faces_a)
    turned_halo = nt(eye(halo_a.shape[1], bf16)[:both], halo_a[...]).astype(bf16)
    zeros = jnp.zeros((channels, voxels), f32)

    def first_pass(step, sums):
        forth, back = sums
        for u in range(UNROLL):
            o = step * UNROLL + u
            mirror = OFFSETS - 1 - o
            got = nn(turned_halo, halo_hot[o]).astype(bf16)
            mine = picked[0, at(o), :] + got[:channels]
            theirs = picked[1, at(mirror), :] + got[channels:]
            picked[0, at(o), :] = mine
            picked[1, at(mirror), :] = theirs
            forth = forth + nn(w1[o], mine)
            back = back + nn(turned[1, mirror], theirs)
        return forth, back

    forth, back = lax.fori_loop(0, OFFSETS // UNROLL, first_pass, (zeros, zeros))
    pre = live_f * forth
    gate = 1.0 / (1.0 + jnp.exp(-pre))
    hidden = (live_f * (pre * gate)).astype(bf16)
    grad_pre = ((live_f * back) * gate * (1.0 + pre * (1.0 - gate))).astype(bf16)
    sides[0] = grad_pre
    sides[1] = hidden
    field[0:channels, :] = hidden
    field[channels:both, :] = grad_pre
    sent_c[:, 0:both] = nt(pick[...], field[...]).astype(bf16)
    sent_c[:, both:] = jnp.zeros((8 * per_list, sent_c.shape[1] - both), bf16)
    start_faces(faces_c)
    for step in range(2, rounds):
        hear(step - 1)
        tell(step)

    def core_copy(g):
        rows = pl.ds(pl.multiple_of(g * group_rows, 32), group_rows)
        return remote(to_core.at[rows, :], from_core.at[rows, :], sem_core, g, g, partner)

    def correlate(which, g):
        rows = pl.ds(pl.multiple_of(g * (GROUP * channels), 128), GROUP * channels)
        if which == 0:
            return nt(sides[0], picked[0, rows, :])
        tall = nt(picked[1, rows, :], sides[1])
        return jnp.concatenate([tall[k * channels : (k + 1) * channels] for k in range(GROUP)], axis=1)

    def tile_rows(g, t):
        return pl.ds(pl.multiple_of(g * group_rows + t * channels, 32), channels)

    def give(which, g):
        product = correlate(which, g)
        for t in range(tiles):
            to_core[tile_rows(g, t), :] = product[:, t * 128 : (t + 1) * 128].astype(bf16)
        core_copy(g).start()

    def keep(which, g):
        product = correlate(which, g)
        for t in range(tiles):
            own[tile_rows(g, t), :] = product[:, t * 128 : (t + 1) * 128]

    def join():
        done = 0
        for p in range(nj):
            while done < GROUPS and done * group_rows < (p + 1) * piece:
                core_copy(done).wait_recv()
                done += 1
            rows = pl.ds(p * piece, piece)
            total = own[rows, :] + from_core[rows, :].astype(f32)
            own[rows, :] = total
            summed[p, 0:piece, :] = total.astype(bf16)
            summed[p, piece:, :] = total[:quarter].astype(bf16)

    for which in range(2):

        @pl.when(core == which)
        def _():
            for g in range(GROUPS):
                give(1 - which, g)
            for g in range(GROUPS):
                keep(which, g)

    join()

    def quarter_rows(q):
        return pl.ds(pl.multiple_of(q * quarter, 8), quarter)

    starts = (far, near)

    def plane_copy(part, source, target):
        rows = pl.ds(pl.multiple_of(starts[part] * quarter, 8), some)
        return pltpu.make_async_remote_copy(
            src_ref=summed.at[target, rows, :], dst_ref=arrived.at[part, source],
            send_sem=sem_plane.at[0, part, target], recv_sem=sem_plane.at[1, part, source],
            device_id=(target * 2 + core, smp), device_id_type=MESH,
        )

    for part in range(2):
        loop(1, nj, lambda i: plane_copy(part, chip, plane(i)).start())
    hear(rounds - 1)

    arrive_faces(faces_c)
    turned_halo_c = nt(eye(halo_c.shape[1], bf16)[:both], halo_c[...]).astype(bf16)

    def second_pass(step, sums):
        forth, back = sums
        for u in range(UNROLL):
            o = step * UNROLL + u
            got = (nn(field[...], local_hot[o]) + nn(turned_halo_c, halo_hot[o])).astype(bf16)
            forth = forth + nn(w2[o], got[:channels])
            back = back + nn(turned[0, OFFSETS - 1 - o], got[channels:])
        return forth, back

    forth, back = lax.fori_loop(0, OFFSETS // UNROLL, second_pass, (zeros, zeros))
    results[0] = (live_f * forth).astype(bf16)
    results[1] = (live_f * back).astype(bf16)
    keeps = [
        pltpu.make_async_copy(results.at[0], out_field, sem_out.at[0]),
        pltpu.make_async_copy(results.at[1], input_grad, sem_out.at[1]),
    ]
    for copy in keeps:
        copy.start()

    def z_copy(source, target, rows):
        return remote(z_part.at[rows, :], z_in.at[source], sem_z, source, target, (blk, target))

    def z_sends(part, act_on):
        def run(k):
            target = lax.rem(starts[part] * (nz // 4) + k, nz)
            rows = pl.ds(pl.multiple_of(part * some + k * sliver, 8), sliver)

            if part == 0:
                act_on(target, rows)
            else:

                @pl.when(target != smp)
                def _():
                    act_on(target, rows)

        loop(0, nz // 2, run)

    base = pl.multiple_of(chip * piece, piece)
    for part in range(2):
        for k in range(2):
            first_row = base + lax.rem(starts[part] + k, 4) * quarter
            z_part[part * some + k * quarter : part * some + (k + 1) * quarter, :] = own[
                pl.ds(pl.multiple_of(first_row, 8), quarter), :
            ]

        def add_piece(i):
            source = plane(i)
            plane_copy(part, source, source).wait_recv()
            z_part[part * some : (part + 1) * some, :] += arrived[part, source].astype(f32)

        loop(1, nj, add_piece)
        z_sends(part, lambda target, rows: z_copy(smp, target, rows).start())

    place_here = lax.rem(smp + nz - near * (nz // 4), nz)
    total = z_part[pl.ds(pl.multiple_of(some + place_here * sliver, 8), sliver), :]

    def add_sliver(i, running):
        source = along(i)
        z_copy(source, source, pl.ds(0, sliver)).wait_recv()
        return running + z_in[source]

    total = lax.fori_loop(1, nz, add_sliver, total)

    def sliver_rows(s):
        return pl.ds(pl.multiple_of(s * sliver, 8), sliver)

    def zg_copy(source, target):
        return remote(
            z_out.at[sliver_rows(source), :], z_out.at[sliver_rows(source), :], sem_zg, source, target,
            (blk, target),
        )

    z_out[sliver_rows(smp), :] = total
    loop(0, nz - 1, lambda i: zg_copy(smp, along(lax.rem(i + nz // 2 - 1, nz - 1) + 1)).start())

    def gather_copy(part, source, target):
        return pltpu.make_async_remote_copy(
            src_ref=spreading.at[chip, part], dst_ref=spreading.at[source, part],
            send_sem=sem_gather.at[0, part, target], recv_sem=sem_gather.at[1, part, source],
            device_id=(target * 2 + core, smp), device_id_type=MESH,
        )

    def keep_copy(part, p):
        return pltpu.make_async_copy(spreading.at[p, part], gathered.at[core, p, part], sem_keep.at[part, p])

    def forward_copy(which, part, p):
        return pltpu.make_async_remote_copy(
            src_ref=spreading.at[p, part], dst_ref=gathered.at[which, p, part],
            send_sem=sem_forward.at[0, part, p], recv_sem=sem_forward.at[1, part, p],
            device_id=partner, device_id_type=MESH,
        )

    def store(part, p):
        keep_copy(part, p).start()
        forward_copy(core, part, p).start()

    for part, start in enumerate((near, far)):

        def sliver_here(k):
            source = lax.rem(start * (nz // 4) + k, nz)
            if part == 0:
                pl.when(source != smp)(lambda: zg_copy(source, source).wait_recv())
            else:
                zg_copy(source, source).wait_recv()

        loop(0, nz // 2, sliver_here)
        for k in range(2):
            spreading[chip, part, k * quarter : (k + 1) * quarter, :] = z_out[
                quarter_rows(lax.rem(start + k, 4)), :
            ].astype(bf16)
        loop(1, nj, lambda i: gather_copy(part, chip, plane(i)).start())
        store(part, chip)

    for part in range(2):

        def hand_on(i):
            source = plane(i)
            gather_copy(part, source, source).wait_recv()
            store(part, source)

        loop(1, nj, hand_on)

    finish_faces(faces_a)
    finish_faces(faces_c)
    loop(0, GROUPS, lambda g: core_copy(g).wait_send())
    for part in range(2):
        loop(1, nj, lambda i: plane_copy(part, chip, plane(i)).wait_send())
        z_sends(part, lambda target, rows: z_copy(smp, target, rows).wait_send())
        loop(1, nj, lambda i: gather_copy(part, chip, plane(i)).wait_send())
    loop(1, nz, lambda i: zg_copy(smp, along(i)).wait_send())
    for copy in keeps:
        copy.wait()
    for part in range(2):

        def settle(p):
            keep_copy(part, p).wait()
            forward_copy(core, part, p).wait_send()
            forward_copy(other, part, p).wait_recv()

        loop(0, nj, settle)


def unpack_kernel(
    nj, nz, scale, field_in, grad_in, gathered, first, second, field_out, grad_out,
    fields, stage, wide_sums, sem_field, sem_in, sem_out,
):
    channels, offsets = first.shape[1], first.shape[0]
    half_rows = stage.shape[1]
    quarter = half_rows // nj // 4
    group_rows = GROUP * channels * channels // 128
    tiles = GROUP * channels // 128
    run = 32
    near = lax.rem(far_quarter(lax.axis_index("smp"), nz) + 2, 4)
    turned = [pl.multiple_of(lax.rem(q + 4 - near, 4) * quarter, 8) for q in range(4)]

    def load(which, k):
        rows = pl.ds(k * (half_rows // 4), half_rows // 4)
        return pltpu.make_async_copy(gathered.at[which, rows], stage.at[which, rows], sem_in.at[which, k])

    def save(which, g):
        some = pl.ds(g * GROUP, min(GROUP, offsets - g * GROUP))
        return pltpu.make_async_copy(
            wide_sums.at[which, some], (first, second)[which].at[some], sem_out.at[which, g]
        )

    loads = [pltpu.make_async_copy(x, fields.at[i], sem_field.at[0, i]) for i, x in enumerate((field_in, grad_in))]
    saves = [
        pltpu.make_async_copy(fields.at[i], x.at[0], sem_field.at[1, i]) for i, x in enumerate((field_out, grad_out))
    ]
    for which in range(2):
        for k in range(4):
            load(which, k).start()
    for copy in loads:
        copy.start()
    for which in range(2):
        here = 0
        for g in range(GROUPS):
            while here < 4 and here * (half_rows // 4) < (g + 1) * group_rows:
                load(which, here).wait()
                here += 1

            def part_of(row):
                first_row = row - row % (quarter * 4) + turned[row // quarter % 4] + row % quarter
                return stage[which, pl.ds(pl.multiple_of(first_row, 8), run), :].astype(jnp.float32)

            parts = [part_of(g * group_rows + n) for n in range(0, group_rows, run)]
            step = channels // run
            wide = jnp.concatenate(
                [jnp.concatenate(parts[t * step : (t + 1) * step], axis=0) for t in range(tiles)], axis=1
            )
            wide = wide * scale
            for k in range(GROUP):
                wide_sums[which, g * GROUP + k] = wide[:, k * channels : (k + 1) * channels]
            save(which, g).start()
    for copy in loads:
        copy.wait()
    for copy in saves:
        copy.start()
    for which in range(2):
        for g in range(GROUPS):
            save(which, g).wait()
    for copy in saves:
        copy.wait()


def body(nb, nz, features, active, neighbour_rows, send_rows, first_weight, second_weight, cotangent):
    channels, voxels = features.shape[1], features.shape[2]
    both = 2 * channels
    per_list = send_rows.shape[3]
    halo_rows = 4 * per_list + 4 * CORNER
    nj = nb // 2
    half_rows = 2048
    piece = half_rows // nj
    bf16, f32 = jnp.bfloat16, jnp.float32
    anywhere = pl.BlockSpec(memory_space=pl.ANY)
    slots = lax.axis_size("smp") * features.shape[0] * nb * voxels
    table = jnp.transpose(neighbour_rows, (1, 0, 2))
    operands = (features, active, table, send_rows, first_weight, second_weight, cotangent)
    dma = pltpu.SemaphoreType.DMA
    wide = 256
    out_field, input_grad, gathered = pl.pallas_call(
        functools.partial(main_kernel, nb, nz),
        out_shape=[
            jax.ShapeDtypeStruct((channels, voxels), bf16),
            jax.ShapeDtypeStruct((channels, voxels), bf16),
            jax.ShapeDtypeStruct((2, nj, 2, piece // 2, 128), bf16),
        ],
        in_specs=[anywhere] * 7,
        out_specs=[anywhere] * 3,
        scratch_shapes=[
            *(pltpu.VMEM(x.shape, x.dtype) for x in operands),
            pltpu.VMEM((2, channels, voxels), bf16),
            pltpu.VMEM((nj, 2, piece // 2, 128), bf16),
            pltpu.VMEM((both, voxels), bf16),
            pltpu.VMEM((8 * per_list, voxels), bf16),
            pltpu.VMEM((8 * per_list, wide), bf16),
            pltpu.VMEM((halo_rows, wide), bf16),
            pltpu.VMEM((8 * per_list, wide), bf16),
            pltpu.VMEM((halo_rows, wide), bf16),
            pltpu.VMEM((OFFSETS, voxels, voxels), bf16),
            pltpu.VMEM((OFFSETS, halo_rows, voxels), bf16),
            pltpu.VMEM((2, OFFSETS, channels, channels), bf16),
            pltpu.VMEM((2, GROUP * GROUPS * channels, voxels), bf16),
            pltpu.VMEM((2, channels, voxels), bf16),
            pltpu.VMEM((half_rows, 128), bf16),
            pltpu.VMEM((half_rows, 128), f32),
            pltpu.VMEM((half_rows, 128), bf16),
            pltpu.VMEM((nj, piece + piece // 4, 128), bf16),
            pltpu.VMEM((2, nj, piece // 2, 128), bf16),
            pltpu.VMEM((piece, 128), f32),
            pltpu.VMEM((nz, piece // nz, 128), f32),
            pltpu.VMEM((piece, 128), f32),
            pltpu.SemaphoreType.REGULAR((max(nz // 4, 1).bit_length(),)),
            dma((7,)),
            dma((2,)),
            dma((2, 8)),
            dma((2, 8)),
            dma((2, GROUPS)),
            dma((2, 2, nj)),
            dma((2, nz)),
            dma((2, nz)),
            dma((2, 2, nj)),
            dma((2, nj)),
            dma((2, 2, nj)),
        ],
        compiler_params=pltpu.CompilerParams(
            collective_id=0, has_side_effects=True, vmem_limit_bytes=56 * 2**20
        ),
        name="halo_conv_and_sum",
    )(*operands)

    grad = jax.ShapeDtypeStruct((OFFSETS, channels, channels), f32)
    field = jax.ShapeDtypeStruct((1, channels, voxels), bf16)
    first_grad, second_grad, out_field, input_grad = pl.pallas_call(
        functools.partial(unpack_kernel, nj, nz, 1.0 / slots**0.5),
        out_shape=[grad, grad, field, field],
        in_specs=[anywhere] * 3,
        out_specs=[anywhere] * 4,
        scratch_shapes=[
            pltpu.VMEM((2, channels, voxels), bf16),
            pltpu.VMEM((2, half_rows, 128), bf16),
            pltpu.VMEM((2, GROUP * GROUPS, channels, channels), f32),
            dma((2, 2)),
            dma((2, 4)),
            dma((2, GROUPS)),
        ],
        compiler_params=pltpu.CompilerParams(vmem_limit_bytes=56 * 2**20),
        name="unpack",
    )(out_field, input_grad, gathered.reshape(2, half_rows, 128))
    return out_field, input_grad, first_grad, second_grad


def solution(mesh):
    return jax.shard_map(
        functools.partial(body, mesh.shape["blk"], mesh.shape["smp"]),
        mesh=mesh,
        in_specs=(
            P("smp", None, "blk"),
            P("smp", "blk"),
            P("smp", None, "blk"),
            P("smp", "blk", None, None),
            P(),
            P(),
            P("smp", None, "blk"),
        ),
        out_specs=(P("smp", None, "blk"), P("smp", None, "blk"), P(), P()),
        check_vma=False,
    )
```

```python
import functools

import jax
import jax.numpy as jnp
from jax import lax
from jax.experimental import pallas as pl
from jax.experimental.pallas import tpu as pltpu
from jax.sharding import PartitionSpec as P

MESH = pl.DeviceIdType.MESH
TALL = 4
STEPS = ((-1, 0), (1, 0), (0, -1), (0, 1), (-1, -1), (-1, 1), (1, -1), (1, 1))
DELTAS = tuple(a * TALL + b for a, b in STEPS)
OFFSETS = 27
GROUP = 4
GROUPS = 7
CORNER = 16
UNROLL = 9


def nn(a, b):
    return lax.dot_general(a, b, (((1,), (0,)), ((), ())), preferred_element_type=jnp.float32)


def nt(a, b):
    return lax.dot_general(a, b, (((1,), (1,)), ((), ())), preferred_element_type=jnp.float32)


def eye(n, dtype):
    rows = lax.broadcasted_iota(jnp.int32, (n, n), 0)
    cols = lax.broadcasted_iota(jnp.int32, (n, n), 1)
    return (rows == cols).astype(jnp.float32).astype(dtype)


def one_hot(rows, codes):
    return jnp.where(rows == codes, 1.0, 0.0).astype(jnp.bfloat16)


def far_quarter(smp, nz):
    per_quarter = nz // 4
    late = lax.rem(smp, per_quarter) >= per_quarter // 2
    return lax.rem(lax.div(smp, per_quarter) + jnp.where(late, 2, 1), 4)


def main_kernel(
    nb, nz,
    feat_in, act_in, nbr_in, lists_in, w1_in, w2_in, cot_in,
    out_field, input_grad, gathered,
    feat, act, nbr, lists, w1, w2, cot, results, spreading,
    field, pick, sent_a, halo_a, sent_c, halo_c,
    local_hot, halo_hot, turned, side_by_side, picked, sides,
    to_core, own, from_core, summed, arrived, z_part, z_in, z_out,
    heard, sem_in, sem_out, sem_a, sem_c, sem_core, sem_plane, sem_z, sem_zg, sem_gather, sem_keep, sem_forward,
):
    bf16, f32 = jnp.bfloat16, jnp.float32
    channels, voxels = feat.shape[1], feat.shape[2]
    both = 2 * channels
    per_list = lists.shape[3]
    halo_rows = halo_a.shape[0]
    nj = nb // 2
    half_rows = own.shape[0]
    piece = half_rows // nj
    sliver = piece // nz
    quarter = piece // 4
    some = piece // 2
    group_rows = GROUP * channels * channels // 128
    tiles = GROUP * channels // 128
    blk = lax.axis_index("blk")
    smp = lax.axis_index("smp")
    core = lax.rem(blk, 2)
    chip = lax.div(blk, 2)
    other = 1 - core
    partner = (chip * 2 + other, smp)

    def loop(start, stop, act_on):
        def run(i, _):
            act_on(i)
            return 0

        lax.fori_loop(start, stop, run, 0)

    far = far_quarter(smp, nz)
    near = lax.rem(far + 2, 4)

    def plane(i):
        return lax.rem(chip + i, nj)

    def along(i):
        return lax.rem(smp + i, nz)

    def remote(src, dst, sems, source, target, device):
        return pltpu.make_async_remote_copy(
            src_ref=src, dst_ref=dst, send_sem=sems.at[0, target], recv_sem=sems.at[1, source],
            device_id=device, device_id_type=MESH,
        )

    halo_a[...] = jnp.zeros_like(halo_a)
    halo_c[...] = jnp.zeros_like(halo_c)
    barrier = pltpu.get_barrier_semaphore()
    in_range = [(blk + delta >= 0) & (blk + delta < nb) for delta in DELTAS]

    def greet(device):
        pl.semaphore_signal(barrier, inc=1, device_id=device, device_id_type=MESH)

    for delta, there in zip(DELTAS, in_range):
        pl.when(there)(functools.partial(greet, (jnp.clip(blk + delta, 0, nb - 1), smp)))
    loads = [
        pltpu.make_async_copy(src, dst, sem_in.at[i])
        for i, (src, dst) in enumerate(
            ((feat_in, feat), (cot_in, cot), (act_in, act), (lists_in, lists), (nbr_in, nbr), (w1_in, w1), (w2_in, w2))
        )
    ]
    for load in loads:
        load.start()

    across = min(4, nj)
    row, place_in_row = lax.div(chip, across), lax.rem(chip, across)
    beside = [row * across + lax.rem(place_in_row + step, across) for step in (1, across - 1)]
    if nj > across:
        beside += [lax.rem(chip + step, nj) for step in (across, nj - across)]
    beside = [(p * 2 + core, smp) for p in beside]
    for device in beside + [(blk, along(1)), (blk, along(nz - 1))]:
        greet(device)
    greeted = sum(there.astype(jnp.int32) for there in in_range) + len(beside) + 2

    def tell(step):
        for device in beside:
            pl.semaphore_signal(heard.at[0, step], inc=1, device_id=device, device_id_type=MESH)
        if step < rounds:
            for i in (1 << step, nz - (1 << step)):
                pl.semaphore_signal(heard.at[1, step], inc=1, device_id=(blk, along(i)), device_id_type=MESH)

    def hear_plane(step):
        pl.semaphore_wait(heard.at[0, step], len(beside))

    def hear_samples(step):
        if step < rounds:
            pl.semaphore_wait(heard.at[1, step], 2)

    rounds = max(nz // 4, 1).bit_length()

    for load in loads[:4]:
        load.wait()
    live = act[...] > 0
    live_f = live.astype(f32)
    field[0:channels, :] = jnp.where(live, feat[0].astype(f32), 0.0).astype(bf16)
    field[channels:both, :] = jnp.where(live, cot[0].astype(f32), 0.0).astype(bf16)

    spread = jnp.concatenate(
        [jnp.broadcast_to(lists[0, 0, d : d + 1, :], (per_list, per_list)) for d in range(8)], axis=0
    )
    at_row = lax.broadcasted_iota(jnp.int32, spread.shape, 0)
    at_col = lax.broadcasted_iota(jnp.int32, spread.shape, 1)
    column = jnp.sum(jnp.where(lax.rem(at_row, per_list) == at_col, spread, 0), axis=1, keepdims=True)
    pick[...] = one_hot(lax.broadcasted_iota(jnp.int32, (8 * per_list, voxels), 1), column)

    def face_copies(sent, halo, sems):
        copies = []
        for d, delta in enumerate(DELTAS):
            if d < 4:
                rows = pl.ds(d * per_list, per_list)
                into = rows
            else:
                rows = pl.ds(d * per_list, CORNER)
                into = pl.ds(4 * per_list + (d - 4) * CORNER, CORNER)
            target, source = blk + delta, blk - delta
            copy = pltpu.make_async_remote_copy(
                src_ref=sent.at[rows, :], dst_ref=halo.at[into, :],
                send_sem=sems.at[0, d], recv_sem=sems.at[1, d],
                device_id=(jnp.clip(target, 0, nb - 1), smp), device_id_type=MESH,
            )
            has_target = (target >= 0) & (target < nb)
            has_source = (source >= 0) & (source < nb)
            copies.append((copy, has_target, has_source))
        return copies

    def start_faces(copies):
        for copy, has_target, _ in copies:
            pl.when(has_target)(copy.start)

    def arrive_faces(copies):
        for copy, _, has_source in copies:
            pl.when(has_source)(copy.wait_recv)

    def finish_faces(copies):
        for copy, has_target, _ in copies:
            pl.when(has_target)(copy.wait_send)

    faces_a = face_copies(sent_a, halo_a, sem_a)
    faces_c = face_copies(sent_c, halo_c, sem_c)
    sent_a[:, 0:both] = nt(pick[...], field[...]).astype(bf16)
    sent_a[:, both:] = jnp.zeros((8 * per_list, sent_a.shape[1] - both), bf16)
    pl.semaphore_wait(barrier, greeted)
    start_faces(faces_a)
    tell(0)

    for load in loads[4:]:
        load.wait()
    unit = eye(channels, bf16)
    local_rows = lax.broadcasted_iota(jnp.int32, (voxels, voxels), 0)
    place = lax.broadcasted_iota(jnp.int32, (halo_rows, voxels), 0)
    past = place - 4 * per_list
    corner_code = jnp.where(
        lax.rem(past, CORNER) < 4, voxels + 4 * per_list + lax.div(past, CORNER) * 4 + lax.rem(past, CORNER), -1
    )
    halo_codes = jnp.where(past < 0, voxels + place, corner_code)

    def at(o):
        return pl.ds(pl.multiple_of(o * channels, 32), channels)

    def prepare(step, _):
        for u in range(UNROLL):
            o = step * UNROLL + u
            codes = nbr[o]
            hot = one_hot(local_rows, codes)
            local_hot[o] = hot
            halo_hot[o] = one_hot(halo_codes, codes)
            got = nn(field[...], hot).astype(bf16)
            picked[0, at(o), :] = got[:channels]
            picked[1, at(OFFSETS - 1 - o), :] = got[channels:]
            turned[o] = nt(unit, w1[o]).astype(bf16)
        return 0

    lax.fori_loop(0, OFFSETS // UNROLL, prepare, 0)
    blank = jnp.zeros((channels, channels), bf16)
    for g in range(GROUPS):
        lanes = pl.ds(g * GROUP * channels, GROUP * channels)
        group = range(g * GROUP, (g + 1) * GROUP)
        side_by_side[0, :, lanes] = jnp.concatenate([w1[o] if o < OFFSETS else blank for o in group], axis=1)
        side_by_side[1, :, lanes] = jnp.concatenate(
            [nt(unit, w2[o]) if o < OFFSETS else blank.astype(f32) for o in group], axis=1
        ).astype(bf16)
    tail = picked.shape[1] - OFFSETS * channels
    picked[:, OFFSETS * channels :, :] = jnp.zeros((2, tail, voxels), bf16)
    rest = half_rows - GROUPS * group_rows
    own[GROUPS * group_rows :, :] = jnp.zeros((rest, 128), f32)
    from_core[GROUPS * group_rows :, :] = jnp.zeros((rest, 128), bf16)

    hear_plane(0)
    hear_samples(0)
    tell(1)
    arrive_faces(faces_a)
    turned_halo = nt(eye(halo_a.shape[1], bf16)[:both], halo_a[...]).astype(bf16)
    zeros = jnp.zeros((channels, voxels), f32)

    def first_pass(step, _):
        for u in range(UNROLL):
            o = step * UNROLL + u
            mirror = OFFSETS - 1 - o
            got = nn(turned_halo, halo_hot[o]).astype(bf16)
            picked[0, at(o), :] += got[:channels]
            picked[1, at(mirror), :] += got[channels:]
        return 0

    lax.fori_loop(0, OFFSETS // UNROLL, first_pass, 0)
    hear_plane(1)
    hear_samples(1)
    tell(2)
    forth = nn(side_by_side[0], picked[0])
    back = nn(side_by_side[1], picked[1])
    pre = live_f * forth
    gate = 1.0 / (1.0 + jnp.exp(-pre))
    hidden = (live_f * (pre * gate)).astype(bf16)
    grad_pre = ((live_f * back) * gate * (1.0 + pre * (1.0 - gate))).astype(bf16)
    sides[0] = grad_pre
    sides[1] = hidden
    field[0:channels, :] = hidden
    field[channels:both, :] = grad_pre
    sent_c[:, 0:both] = nt(pick[...], field[...]).astype(bf16)
    sent_c[:, both:] = jnp.zeros((8 * per_list, sent_c.shape[1] - both), bf16)
    start_faces(faces_c)

    def core_copy(g):
        rows = pl.ds(pl.multiple_of(g * group_rows, 32), group_rows)
        return remote(to_core.at[rows, :], from_core.at[rows, :], sem_core, g, g, partner)

    def correlate(which, g):
        rows = pl.ds(pl.multiple_of(g * (GROUP * channels), 128), GROUP * channels)
        if which == 0:
            return nt(sides[0], picked[0, rows, :])
        tall = nt(picked[1, rows, :], sides[1])
        return jnp.concatenate([tall[k * channels : (k + 1) * channels] for k in range(GROUP)], axis=1)

    def tile_rows(g, t):
        return pl.ds(pl.multiple_of(g * group_rows + t * channels, 32), channels)

    def give(which, g):
        product = correlate(which, g)
        for t in range(tiles):
            to_core[tile_rows(g, t), :] = product[:, t * 128 : (t + 1) * 128].astype(bf16)
        core_copy(g).start()

    def keep(which, g):
        product = correlate(which, g)
        for t in range(tiles):
            own[tile_rows(g, t), :] = product[:, t * 128 : (t + 1) * 128]

    def join():
        done = 0
        for p in range(nj):
            while done < GROUPS and done * group_rows < (p + 1) * piece:
                core_copy(done).wait_recv()
                done += 1
            rows = pl.ds(p * piece, piece)
            total = own[rows, :] + from_core[rows, :].astype(f32)
            own[rows, :] = total
            summed[p, 0:piece, :] = total.astype(bf16)
            summed[p, piece:, :] = total[:quarter].astype(bf16)

    for which in range(2):

        @pl.when(core == which)
        def _():
            for g in range(GROUPS):
                give(1 - which, g)
            for g in range(GROUPS):
                keep(which, g)

    join()

    def quarter_rows(q):
        return pl.ds(pl.multiple_of(q * quarter, 8), quarter)

    starts = (far, near)

    def plane_copy(part, source, target):
        rows = pl.ds(pl.multiple_of(starts[part] * quarter, 8), some)
        return pltpu.make_async_remote_copy(
            src_ref=summed.at[target, rows, :], dst_ref=arrived.at[part, source],
            send_sem=sem_plane.at[0, part, target], recv_sem=sem_plane.at[1, part, source],
            device_id=(target * 2 + core, smp), device_id_type=MESH,
        )

    hear_plane(2)
    for part in range(2):
        loop(1, nj, lambda i: plane_copy(part, chip, plane(i)).start())

    def z_copy(source, target, rows):
        return remote(z_part.at[rows, :], z_in.at[source], sem_z, source, target, (blk, target))

    def z_sends(part, act_on):
        def run(k):
            target = lax.rem(starts[part] * (nz // 4) + k, nz)
            rows = pl.ds(pl.multiple_of(part * some + k * sliver, 8), sliver)

            if part == 0:
                act_on(target, rows)
            else:

                @pl.when(target != smp)
                def _():
                    act_on(target, rows)

        loop(0, nz // 2, run)

    hear_samples(2)
    base = pl.multiple_of(chip * piece, piece)
    for part in range(2):
        for k in range(2):
            first_row = base + lax.rem(starts[part] + k, 4) * quarter
            z_part[part * some + k * quarter : part * some + (k + 1) * quarter, :] = own[
                pl.ds(pl.multiple_of(first_row, 8), quarter), :
            ]

        def add_piece(i):
            source = plane(i)
            plane_copy(part, source, source).wait_recv()
            z_part[part * some : (part + 1) * some, :] += arrived[part, source].astype(f32)

        loop(1, nj, add_piece)
        z_sends(part, lambda target, rows: z_copy(smp, target, rows).start())

    arrive_faces(faces_c)
    turned_halo_c = nt(eye(halo_c.shape[1], bf16)[:both], halo_c[...]).astype(bf16)

    def second_pass(step, sums):
        forth, back = sums
        for u in range(UNROLL):
            o = step * UNROLL + u
            got = (nn(field[...], local_hot[o]) + nn(turned_halo_c, halo_hot[o])).astype(bf16)
            forth = forth + nn(w2[o], got[:channels])
            back = back + nn(turned[OFFSETS - 1 - o], got[channels:])
        return forth, back

    most = OFFSETS // UNROLL - 1
    forth, back = lax.fori_loop(0, most, second_pass, (zeros, zeros))

    place_here = lax.rem(smp + nz - near * (nz // 4), nz)
    total = z_part[pl.ds(pl.multiple_of(some + place_here * sliver, 8), sliver), :]

    def add_sliver(i, running):
        source = along(i)
        z_copy(source, source, pl.ds(0, sliver)).wait_recv()
        return running + z_in[source]

    total = lax.fori_loop(1, nz, add_sliver, total)

    def sliver_rows(s):
        return pl.ds(pl.multiple_of(s * sliver, 8), sliver)

    def zg_copy(source, target):
        return remote(
            z_out.at[sliver_rows(source), :], z_out.at[sliver_rows(source), :], sem_zg, source, target,
            (blk, target),
        )

    z_out[sliver_rows(smp), :] = total
    loop(0, nz - 1, lambda i: zg_copy(smp, along(lax.rem(i + nz // 2 - 1, nz - 1) + 1)).start())

    forth, back = lax.fori_loop(most, OFFSETS // UNROLL, second_pass, (forth, back))
    results[0] = (live_f * forth).astype(bf16)
    results[1] = (live_f * back).astype(bf16)
    keeps = [
        pltpu.make_async_copy(results.at[0], out_field, sem_out.at[0]),
        pltpu.make_async_copy(results.at[1], input_grad, sem_out.at[1]),
    ]
    for copy in keeps:
        copy.start()

    def gather_copy(part, source, target):
        return pltpu.make_async_remote_copy(
            src_ref=spreading.at[chip, part], dst_ref=spreading.at[source, part],
            send_sem=sem_gather.at[0, part, target], recv_sem=sem_gather.at[1, part, source],
            device_id=(target * 2 + core, smp), device_id_type=MESH,
        )

    def keep_copy(part, p):
        return pltpu.make_async_copy(spreading.at[p, part], gathered.at[core, p, part], sem_keep.at[part, p])

    def forward_copy(which, part, p):
        return pltpu.make_async_remote_copy(
            src_ref=spreading.at[p, part], dst_ref=gathered.at[which, p, part],
            send_sem=sem_forward.at[0, part, p], recv_sem=sem_forward.at[1, part, p],
            device_id=partner, device_id_type=MESH,
        )

    def store(part, p):
        keep_copy(part, p).start()
        forward_copy(core, part, p).start()

    for part, start in enumerate((near, far)):

        def sliver_here(k):
            source = lax.rem(start * (nz // 4) + k, nz)
            if part == 0:
                pl.when(source != smp)(lambda: zg_copy(source, source).wait_recv())
            else:
                zg_copy(source, source).wait_recv()

        loop(0, nz // 2, sliver_here)
        for k in range(2):
            spreading[chip, part, k * quarter : (k + 1) * quarter, :] = z_out[
                quarter_rows(lax.rem(start + k, 4)), :
            ].astype(bf16)
        loop(1, nj, lambda i: gather_copy(part, chip, plane(i)).start())
        store(part, chip)

    for part in range(2):

        def hand_on(i):
            source = plane(i)
            gather_copy(part, source, source).wait_recv()
            store(part, source)

        loop(1, nj, hand_on)

    finish_faces(faces_a)
    finish_faces(faces_c)
    loop(0, GROUPS, lambda g: core_copy(g).wait_send())
    for part in range(2):
        loop(1, nj, lambda i: plane_copy(part, chip, plane(i)).wait_send())
        z_sends(part, lambda target, rows: z_copy(smp, target, rows).wait_send())
        loop(1, nj, lambda i: gather_copy(part, chip, plane(i)).wait_send())
    loop(1, nz, lambda i: zg_copy(smp, along(i)).wait_send())
    for copy in keeps:
        copy.wait()
    for part in range(2):

        def settle(p):
            keep_copy(part, p).wait()
            forward_copy(core, part, p).wait_send()
            forward_copy(other, part, p).wait_recv()

        loop(0, nj, settle)


def unpack_kernel(
    nj, nz, scale, field_in, grad_in, gathered, first, second, field_out, grad_out,
    fields, stage, wide_sums, sem_field, sem_in, sem_out,
):
    channels, offsets = first.shape[1], first.shape[0]
    half_rows = stage.shape[1]
    quarter = half_rows // nj // 4
    group_rows = GROUP * channels * channels // 128
    tiles = GROUP * channels // 128
    run = 32
    near = lax.rem(far_quarter(lax.axis_index("smp"), nz) + 2, 4)
    turned = [pl.multiple_of(lax.rem(q + 4 - near, 4) * quarter, 8) for q in range(4)]

    def load(which, k):
        rows = pl.ds(k * (half_rows // 4), half_rows // 4)
        return pltpu.make_async_copy(gathered.at[which, rows], stage.at[which, rows], sem_in.at[which, k])

    def save(which, g):
        some = pl.ds(g * GROUP, min(GROUP, offsets - g * GROUP))
        return pltpu.make_async_copy(
            wide_sums.at[which, some], (first, second)[which].at[some], sem_out.at[which, g]
        )

    loads = [pltpu.make_async_copy(x, fields.at[i], sem_field.at[0, i]) for i, x in enumerate((field_in, grad_in))]
    saves = [
        pltpu.make_async_copy(fields.at[i], x.at[0], sem_field.at[1, i]) for i, x in enumerate((field_out, grad_out))
    ]
    for which in range(2):
        for k in range(4):
            load(which, k).start()
    for copy in loads:
        copy.start()
    for which in range(2):
        here = 0
        for g in range(GROUPS):
            while here < 4 and here * (half_rows // 4) < (g + 1) * group_rows:
                load(which, here).wait()
                here += 1

            def part_of(row):
                first_row = row - row % (quarter * 4) + turned[row // quarter % 4] + row % quarter
                return stage[which, pl.ds(pl.multiple_of(first_row, 8), run), :].astype(jnp.float32)

            parts = [part_of(g * group_rows + n) for n in range(0, group_rows, run)]
            step = channels // run
            wide = jnp.concatenate(
                [jnp.concatenate(parts[t * step : (t + 1) * step], axis=0) for t in range(tiles)], axis=1
            )
            wide = wide * scale
            for k in range(GROUP):
                wide_sums[which, g * GROUP + k] = wide[:, k * channels : (k + 1) * channels]
            save(which, g).start()
    for copy in loads:
        copy.wait()
    for copy in saves:
        copy.start()
    for which in range(2):
        for g in range(GROUPS):
            save(which, g).wait()
    for copy in saves:
        copy.wait()


def body(nb, nz, features, active, neighbour_rows, send_rows, first_weight, second_weight, cotangent):
    channels, voxels = features.shape[1], features.shape[2]
    both = 2 * channels
    per_list = send_rows.shape[3]
    halo_rows = 4 * per_list + 4 * CORNER
    nj = nb // 2
    half_rows = 2048
    piece = half_rows // nj
    bf16, f32 = jnp.bfloat16, jnp.float32
    anywhere = pl.BlockSpec(memory_space=pl.ANY)
    slots = lax.axis_size("smp") * features.shape[0] * nb * voxels
    table = jnp.transpose(neighbour_rows, (1, 0, 2))
    operands = (features, active, table, send_rows, first_weight, second_weight, cotangent)
    dma = pltpu.SemaphoreType.DMA
    wide = 256
    out_field, input_grad, gathered = pl.pallas_call(
        functools.partial(main_kernel, nb, nz),
        out_shape=[
            jax.ShapeDtypeStruct((channels, voxels), bf16),
            jax.ShapeDtypeStruct((channels, voxels), bf16),
            jax.ShapeDtypeStruct((2, nj, 2, piece // 2, 128), bf16),
        ],
        in_specs=[anywhere] * 7,
        out_specs=[anywhere] * 3,
        scratch_shapes=[
            *(pltpu.VMEM(x.shape, x.dtype) for x in operands),
            pltpu.VMEM((2, channels, voxels), bf16),
            pltpu.VMEM((nj, 2, piece // 2, 128), bf16),
            pltpu.VMEM((both, voxels), bf16),
            pltpu.VMEM((8 * per_list, voxels), bf16),
            pltpu.VMEM((8 * per_list, wide), bf16),
            pltpu.VMEM((halo_rows, wide), bf16),
            pltpu.VMEM((8 * per_list, wide), bf16),
            pltpu.VMEM((halo_rows, wide), bf16),
            pltpu.VMEM((OFFSETS, voxels, voxels), bf16),
            pltpu.VMEM((OFFSETS, halo_rows, voxels), bf16),
            pltpu.VMEM((OFFSETS, channels, channels), bf16),
            pltpu.VMEM((2, channels, GROUP * GROUPS * channels), bf16),
            pltpu.VMEM((2, GROUP * GROUPS * channels, voxels), bf16),
            pltpu.VMEM((2, channels, voxels), bf16),
            pltpu.VMEM((half_rows, 128), bf16),
            pltpu.VMEM((half_rows, 128), f32),
            pltpu.VMEM((half_rows, 128), bf16),
            pltpu.VMEM((nj, piece + piece // 4, 128), bf16),
            pltpu.VMEM((2, nj, piece // 2, 128), bf16),
            pltpu.VMEM((piece, 128), f32),
            pltpu.VMEM((nz, piece // nz, 128), f32),
            pltpu.VMEM((piece, 128), f32),
            pltpu.SemaphoreType.REGULAR((2, 3)),
            dma((7,)),
            dma((2,)),
            dma((2, 8)),
            dma((2, 8)),
            dma((2, GROUPS)),
            dma((2, 2, nj)),
            dma((2, nz)),
            dma((2, nz)),
            dma((2, 2, nj)),
            dma((2, nj)),
            dma((2, 2, nj)),
        ],
        compiler_params=pltpu.CompilerParams(
            collective_id=0, has_side_effects=True, vmem_limit_bytes=56 * 2**20
        ),
        name="halo_conv_and_sum",
    )(*operands)

    grad = jax.ShapeDtypeStruct((OFFSETS, channels, channels), f32)
    field = jax.ShapeDtypeStruct((1, channels, voxels), bf16)
    first_grad, second_grad, out_field, input_grad = pl.pallas_call(
        functools.partial(unpack_kernel, nj, nz, 1.0 / slots**0.5),
        out_shape=[grad, grad, field, field],
        in_specs=[anywhere] * 3,
        out_specs=[anywhere] * 4,
        scratch_shapes=[
            pltpu.VMEM((2, channels, voxels), bf16),
            pltpu.VMEM((2, half_rows, 128), bf16),
            pltpu.VMEM((2, GROUP * GROUPS, channels, channels), f32),
            dma((2, 2)),
            dma((2, 4)),
            dma((2, GROUPS)),
        ],
        compiler_params=pltpu.CompilerParams(vmem_limit_bytes=56 * 2**20),
        name="unpack",
    )(out_field, input_grad, gathered.reshape(2, half_rows, 128))
    return out_field, input_grad, first_grad, second_grad


def solution(mesh):
    return jax.shard_map(
        functools.partial(body, mesh.shape["blk"], mesh.shape["smp"]),
        mesh=mesh,
        in_specs=(
            P("smp", None, "blk"),
            P("smp", "blk"),
            P("smp", None, "blk"),
            P("smp", "blk", None, None),
            P(),
            P(),
            P("smp", None, "blk"),
        ),
        out_specs=(P("smp", None, "blk"), P("smp", None, "blk"), P(), P()),
        check_vma=False,
    )
```

```python
import functools

import jax
import jax.numpy as jnp
from jax import lax
from jax.experimental import pallas as pl
from jax.experimental.pallas import tpu as pltpu
from jax.sharding import PartitionSpec as P

MESH = pl.DeviceIdType.MESH
TALL = 4
STEPS = ((-1, 0), (1, 0), (0, -1), (0, 1), (-1, -1), (-1, 1), (1, -1), (1, 1))
DELTAS = tuple(a * TALL + b for a, b in STEPS)
OFFSETS = 27
GROUP = 4
GROUPS = 7
CORNER = 16
UNROLL = 9


def nn(a, b):
    return lax.dot_general(a, b, (((1,), (0,)), ((), ())), preferred_element_type=jnp.float32)


def nt(a, b):
    return lax.dot_general(a, b, (((1,), (1,)), ((), ())), preferred_element_type=jnp.float32)


def eye(n, dtype):
    rows = lax.broadcasted_iota(jnp.int32, (n, n), 0)
    cols = lax.broadcasted_iota(jnp.int32, (n, n), 1)
    return (rows == cols).astype(jnp.float32).astype(dtype)


def one_hot(rows, codes):
    return jnp.where(rows == codes, 1.0, 0.0).astype(jnp.bfloat16)


def far_quarter(smp, nz):
    per_quarter = nz // 4
    late = lax.rem(smp, per_quarter) >= per_quarter // 2
    return lax.rem(lax.div(smp, per_quarter) + jnp.where(late, 2, 1), 4)


def main_kernel(
    nb, nz,
    feat_in, act_in, nbr_in, lists_in, w1_in, w2_in, cot_in,
    out_field, input_grad, gathered,
    feat, act, nbr, lists, w1, w2, cot, results, spreading,
    field, pick, sent_a, halo_a, sent_c, halo_c,
    local_hot, halo_hot, turned, side_by_side, picked, sides,
    to_core, own, from_core, summed, arrived, z_part, z_in, z_out,
    heard, sem_in, sem_out, sem_a, sem_c, sem_core, sem_plane, sem_z, sem_zg, sem_gather, sem_keep, sem_forward,
):
    bf16, f32 = jnp.bfloat16, jnp.float32
    channels, voxels = feat.shape[1], feat.shape[2]
    both = 2 * channels
    per_list = lists.shape[3]
    halo_rows = halo_a.shape[0]
    nj = nb // 2
    half_rows = own.shape[0]
    piece = half_rows // nj
    sliver = piece // nz
    quarter = piece // 4
    some = piece // 2
    group_rows = GROUP * channels * channels // 128
    tiles = GROUP * channels // 128
    blk = lax.axis_index("blk")
    smp = lax.axis_index("smp")
    core = lax.rem(blk, 2)
    chip = lax.div(blk, 2)
    other = 1 - core
    partner = (chip * 2 + other, smp)

    def loop(start, stop, act_on):
        def run(i, _):
            act_on(i)
            return 0

        lax.fori_loop(start, stop, run, 0)

    far = far_quarter(smp, nz)
    near = lax.rem(far + 2, 4)

    across = min(4, nj)
    row, place_in_row = lax.div(chip, across), lax.rem(chip, across)

    def ring_step(k, n):
        return jnp.where(k == n - 1, 0, n // 2 + jnp.where(lax.rem(k, 2) == 1, -lax.div(k + 1, 2), lax.div(k, 2)))

    def plane(k):
        down = lax.rem(row + ring_step(lax.div(k, across), nj // across), nj // across) if nj > across else row
        return down * across + lax.rem(place_in_row + ring_step(lax.rem(k, across), across), across)

    def plane_back(k):
        return plane(nj - 2 - k)

    def along(i):
        return lax.rem(smp + i, nz)

    def remote(src, dst, sems, source, target, device):
        return pltpu.make_async_remote_copy(
            src_ref=src, dst_ref=dst, send_sem=sems.at[0, target], recv_sem=sems.at[1, source],
            device_id=device, device_id_type=MESH,
        )

    halo_a[...] = jnp.zeros_like(halo_a)
    halo_c[...] = jnp.zeros_like(halo_c)
    barrier = pltpu.get_barrier_semaphore()
    in_range = [(blk + delta >= 0) & (blk + delta < nb) for delta in DELTAS]

    def greet(device):
        pl.semaphore_signal(barrier, inc=1, device_id=device, device_id_type=MESH)

    for delta, there in zip(DELTAS, in_range):
        pl.when(there)(functools.partial(greet, (jnp.clip(blk + delta, 0, nb - 1), smp)))
    loads = [
        pltpu.make_async_copy(src, dst, sem_in.at[i])
        for i, (src, dst) in enumerate(
            ((feat_in, feat), (cot_in, cot), (act_in, act), (lists_in, lists), (nbr_in, nbr), (w1_in, w1), (w2_in, w2))
        )
    ]
    for load in loads:
        load.start()

    beside = [row * across + lax.rem(place_in_row + step, across) for step in (1, across - 1)]
    if nj > across:
        beside += [lax.rem(chip + step, nj) for step in (across, nj - across)]
    beside = [(p * 2 + core, smp) for p in beside]
    for device in beside + [(blk, along(1)), (blk, along(nz - 1))]:
        greet(device)
    greeted = sum(there.astype(jnp.int32) for there in in_range) + len(beside) + 2

    def tell(step):
        for device in beside:
            pl.semaphore_signal(heard.at[0, step], inc=1, device_id=device, device_id_type=MESH)
        if step < rounds:
            for i in (1 << step, nz - (1 << step)):
                pl.semaphore_signal(heard.at[1, step], inc=1, device_id=(blk, along(i)), device_id_type=MESH)

    def hear_plane(step):
        pl.semaphore_wait(heard.at[0, step], len(beside))

    def hear_samples(step):
        if step < rounds:
            pl.semaphore_wait(heard.at[1, step], 2)

    rounds = max(nz // 4, 1).bit_length()

    for load in loads[:4]:
        load.wait()
    live = act[...] > 0
    live_f = live.astype(f32)
    field[0:channels, :] = jnp.where(live, feat[0].astype(f32), 0.0).astype(bf16)
    field[channels:both, :] = jnp.where(live, cot[0].astype(f32), 0.0).astype(bf16)

    spread = jnp.concatenate(
        [jnp.broadcast_to(lists[0, 0, d : d + 1, :], (per_list, per_list)) for d in range(8)], axis=0
    )
    at_row = lax.broadcasted_iota(jnp.int32, spread.shape, 0)
    at_col = lax.broadcasted_iota(jnp.int32, spread.shape, 1)
    column = jnp.sum(jnp.where(lax.rem(at_row, per_list) == at_col, spread, 0), axis=1, keepdims=True)
    pick[...] = one_hot(lax.broadcasted_iota(jnp.int32, (8 * per_list, voxels), 1), column)

    def face_copies(sent, halo, sems):
        copies = []
        for d, delta in enumerate(DELTAS):
            if d < 4:
                rows = pl.ds(d * per_list, per_list)
                into = rows
            else:
                rows = pl.ds(d * per_list, CORNER)
                into = pl.ds(4 * per_list + (d - 4) * CORNER, CORNER)
            target, source = blk + delta, blk - delta
            copy = pltpu.make_async_remote_copy(
                src_ref=sent.at[rows, :], dst_ref=halo.at[into, :],
                send_sem=sems.at[0, d], recv_sem=sems.at[1, d],
                device_id=(jnp.clip(target, 0, nb - 1), smp), device_id_type=MESH,
            )
            has_target = (target >= 0) & (target < nb)
            has_source = (source >= 0) & (source < nb)
            copies.append((copy, has_target, has_source))
        return copies

    def start_faces(copies):
        for copy, has_target, _ in copies:
            pl.when(has_target)(copy.start)

    def arrive_faces(copies):
        for copy, _, has_source in copies:
            pl.when(has_source)(copy.wait_recv)

    def finish_faces(copies):
        for copy, has_target, _ in copies:
            pl.when(has_target)(copy.wait_send)

    faces_a = face_copies(sent_a, halo_a, sem_a)
    faces_c = face_copies(sent_c, halo_c, sem_c)
    sent_a[:, 0:both] = nt(pick[...], field[...]).astype(bf16)
    sent_a[:, both:] = jnp.zeros((8 * per_list, sent_a.shape[1] - both), bf16)
    pl.semaphore_wait(barrier, greeted)
    start_faces(faces_a)
    tell(0)

    for load in loads[4:]:
        load.wait()
    unit = eye(channels, bf16)
    local_rows = lax.broadcasted_iota(jnp.int32, (voxels, voxels), 0)
    place = lax.broadcasted_iota(jnp.int32, (halo_rows, voxels), 0)
    past = place - 4 * per_list
    corner_code = jnp.where(
        lax.rem(past, CORNER) < 4, voxels + 4 * per_list + lax.div(past, CORNER) * 4 + lax.rem(past, CORNER), -1
    )
    halo_codes = jnp.where(past < 0, voxels + place, corner_code)

    def at(o):
        return pl.ds(pl.multiple_of(o * channels, 32), channels)

    def prepare(step, _):
        for u in range(UNROLL):
            o = step * UNROLL + u
            codes = nbr[o]
            hot = one_hot(local_rows, codes)
            local_hot[o] = hot
            halo_hot[o] = one_hot(halo_codes, codes)
            got = nn(field[...], hot).astype(bf16)
            picked[0, at(o), :] = got[:channels]
            picked[1, at(OFFSETS - 1 - o), :] = got[channels:]
            turned[o] = nt(unit, w1[o]).astype(bf16)
        return 0

    lax.fori_loop(0, OFFSETS // UNROLL, prepare, 0)
    blank = jnp.zeros((channels, channels), bf16)
    for g in range(GROUPS):
        lanes = pl.ds(g * GROUP * channels, GROUP * channels)
        group = range(g * GROUP, (g + 1) * GROUP)
        side_by_side[0, :, lanes] = jnp.concatenate([w1[o] if o < OFFSETS else blank for o in group], axis=1)
        side_by_side[1, :, lanes] = jnp.concatenate(
            [nt(unit, w2[o]) if o < OFFSETS else blank.astype(f32) for o in group], axis=1
        ).astype(bf16)
    tail = picked.shape[1] - OFFSETS * channels
    picked[:, OFFSETS * channels :, :] = jnp.zeros((2, tail, voxels), bf16)
    rest = half_rows - GROUPS * group_rows
    own[GROUPS * group_rows :, :] = jnp.zeros((rest, 128), f32)
    from_core[GROUPS * group_rows :, :] = jnp.zeros((rest, 128), bf16)

    hear_plane(0)
    hear_samples(0)
    tell(1)
    arrive_faces(faces_a)
    turned_halo = nt(eye(halo_a.shape[1], bf16)[:both], halo_a[...]).astype(bf16)
    zeros = jnp.zeros((channels, voxels), f32)

    def first_pass(step, _):
        for u in range(UNROLL):
            o = step * UNROLL + u
            mirror = OFFSETS - 1 - o
            got = nn(turned_halo, halo_hot[o]).astype(bf16)
            picked[0, at(o), :] += got[:channels]
            picked[1, at(mirror), :] += got[channels:]
        return 0

    lax.fori_loop(0, OFFSETS // UNROLL, first_pass, 0)
    hear_plane(1)
    hear_samples(1)
    tell(2)
    forth = nn(side_by_side[0], picked[0])
    back = nn(side_by_side[1], picked[1])
    pre = live_f * forth
    gate = 1.0 / (1.0 + jnp.exp(-pre))
    hidden = (live_f * (pre * gate)).astype(bf16)
    grad_pre = ((live_f * back) * gate * (1.0 + pre * (1.0 - gate))).astype(bf16)
    sides[0] = grad_pre
    sides[1] = hidden
    field[0:channels, :] = hidden
    field[channels:both, :] = grad_pre
    sent_c[:, 0:both] = nt(pick[...], field[...]).astype(bf16)
    sent_c[:, both:] = jnp.zeros((8 * per_list, sent_c.shape[1] - both), bf16)
    start_faces(faces_c)

    def core_copy(g):
        rows = pl.ds(pl.multiple_of(g * group_rows, 32), group_rows)
        return remote(to_core.at[rows, :], from_core.at[rows, :], sem_core, g, g, partner)

    def correlate(which, g):
        rows = pl.ds(pl.multiple_of(g * (GROUP * channels), 128), GROUP * channels)
        if which == 0:
            return nt(sides[0], picked[0, rows, :])
        tall = nt(picked[1, rows, :], sides[1])
        return jnp.concatenate([tall[k * channels : (k + 1) * channels] for k in range(GROUP)], axis=1)

    def tile_rows(g, t):
        return pl.ds(pl.multiple_of(g * group_rows + t * channels, 32), channels)

    def give(which, g):
        product = correlate(which, g)
        for t in range(tiles):
            to_core[tile_rows(g, t), :] = product[:, t * 128 : (t + 1) * 128].astype(bf16)
        core_copy(g).start()

    def keep(which, g):
        product = correlate(which, g)
        for t in range(tiles):
            own[tile_rows(g, t), :] = product[:, t * 128 : (t + 1) * 128]

    def join():
        done = 0
        for p in range(nj):
            while done < GROUPS and done * group_rows < (p + 1) * piece:
                core_copy(done).wait_recv()
                done += 1
            rows = pl.ds(p * piece, piece)
            total = own[rows, :] + from_core[rows, :].astype(f32)
            own[rows, :] = total
            summed[p, 0:piece, :] = total.astype(bf16)
            summed[p, piece:, :] = total[:quarter].astype(bf16)

    for which in range(2):

        @pl.when(core == which)
        def _():
            for g in range(GROUPS):
                give(1 - which, g)
            for g in range(GROUPS):
                keep(which, g)

    join()

    def quarter_rows(q):
        return pl.ds(pl.multiple_of(q * quarter, 8), quarter)

    starts = (far, near)

    def plane_copy(part, source, target):
        rows = pl.ds(pl.multiple_of(starts[part] * quarter, 8), some)
        return pltpu.make_async_remote_copy(
            src_ref=summed.at[target, rows, :], dst_ref=arrived.at[part, source],
            send_sem=sem_plane.at[0, part, target], recv_sem=sem_plane.at[1, part, source],
            device_id=(target * 2 + core, smp), device_id_type=MESH,
        )

    hear_plane(2)
    for part in range(2):
        loop(0, nj - 1, lambda k: plane_copy(part, chip, plane(k)).start())

    def z_copy(source, target, rows):
        return remote(z_part.at[rows, :], z_in.at[source], sem_z, source, target, (blk, target))

    def z_sends(part, act_on):
        def run(k):
            target = lax.rem(starts[part] * (nz // 4) + k, nz)
            rows = pl.ds(pl.multiple_of(part * some + k * sliver, 8), sliver)

            if part == 0:
                act_on(target, rows)
            else:

                @pl.when(target != smp)
                def _():
                    act_on(target, rows)

        loop(0, nz // 2, run)

    hear_samples(2)
    base = pl.multiple_of(chip * piece, piece)
    for part in range(2):
        for k in range(2):
            first_row = base + lax.rem(starts[part] + k, 4) * quarter
            z_part[part * some + k * quarter : part * some + (k + 1) * quarter, :] = own[
                pl.ds(pl.multiple_of(first_row, 8), quarter), :
            ]

        def add_piece(k):
            source = plane_back(k)
            plane_copy(part, source, source).wait_recv()
            z_part[part * some : (part + 1) * some, :] += arrived[part, source].astype(f32)

        loop(0, nj - 1, add_piece)
        z_sends(part, lambda target, rows: z_copy(smp, target, rows).start())

    arrive_faces(faces_c)
    turned_halo_c = nt(eye(halo_c.shape[1], bf16)[:both], halo_c[...]).astype(bf16)

    def second_pass(step, sums):
        forth, back = sums
        for u in range(UNROLL):
            o = step * UNROLL + u
            got = (nn(field[...], local_hot[o]) + nn(turned_halo_c, halo_hot[o])).astype(bf16)
            forth = forth + nn(w2[o], got[:channels])
            back = back + nn(turned[OFFSETS - 1 - o], got[channels:])
        return forth, back

    most = OFFSETS // UNROLL - 1
    forth, back = lax.fori_loop(0, most, second_pass, (zeros, zeros))

    place_here = lax.rem(smp + nz - near * (nz // 4), nz)
    total = z_part[pl.ds(pl.multiple_of(some + place_here * sliver, 8), sliver), :]

    def add_sliver(i, running):
        source = along(i)
        z_copy(source, source, pl.ds(0, sliver)).wait_recv()
        return running + z_in[source]

    total = lax.fori_loop(1, nz, add_sliver, total)

    def sliver_rows(s):
        return pl.ds(pl.multiple_of(s * sliver, 8), sliver)

    def zg_copy(source, target):
        return remote(
            z_out.at[sliver_rows(source), :], z_out.at[sliver_rows(source), :], sem_zg, source, target,
            (blk, target),
        )

    z_out[sliver_rows(smp), :] = total
    loop(0, nz - 1, lambda k: zg_copy(smp, along(ring_step(k, nz))).start())

    forth, back = lax.fori_loop(most, OFFSETS // UNROLL, second_pass, (forth, back))
    results[0] = (live_f * forth).astype(bf16)
    results[1] = (live_f * back).astype(bf16)
    keeps = [
        pltpu.make_async_copy(results.at[0], out_field, sem_out.at[0]),
        pltpu.make_async_copy(results.at[1], input_grad, sem_out.at[1]),
    ]
    for copy in keeps:
        copy.start()
    finish_faces(faces_a)
    finish_faces(faces_c)
    loop(0, GROUPS, lambda g: core_copy(g).wait_send())
    for part in range(2):
        loop(0, nj - 1, lambda k: plane_copy(part, chip, plane(k)).wait_send())
        z_sends(part, lambda target, rows: z_copy(smp, target, rows).wait_send())

    def gather_copy(part, source, target):
        return pltpu.make_async_remote_copy(
            src_ref=spreading.at[chip, part], dst_ref=spreading.at[source, part],
            send_sem=sem_gather.at[0, part, target], recv_sem=sem_gather.at[1, part, source],
            device_id=(target * 2 + core, smp), device_id_type=MESH,
        )

    def keep_copy(part, p):
        return pltpu.make_async_copy(spreading.at[p, part], gathered.at[core, p, part], sem_keep.at[part])

    def forward_copy(which, part, p):
        return pltpu.make_async_remote_copy(
            src_ref=spreading.at[p, part], dst_ref=gathered.at[which, p, part],
            send_sem=sem_forward.at[0, part], recv_sem=sem_forward.at[1, part],
            device_id=partner, device_id_type=MESH,
        )

    def store(part, p):
        keep_copy(part, p).start()
        forward_copy(core, part, p).start()

    for part, start in enumerate((near, far)):

        def sliver_here(k):
            source = lax.rem(start * (nz // 4) + k, nz)
            if part == 0:
                pl.when(source != smp)(lambda: zg_copy(source, source).wait_recv())
            else:
                zg_copy(source, source).wait_recv()

        loop(0, nz // 2, sliver_here)
        for k in range(2):
            spreading[chip, part, k * quarter : (k + 1) * quarter, :] = z_out[
                quarter_rows(lax.rem(start + k, 4)), :
            ].astype(bf16)
        loop(0, nj - 1, lambda k: gather_copy(part, chip, plane(k)).start())
        store(part, chip)

    loop(1, nz, lambda i: zg_copy(smp, along(i)).wait_send())
    for copy in keeps:
        copy.wait()
    for part in range(2):

        def hand_on(k):
            source = plane_back(k)
            gather_copy(part, source, source).wait_recv()
            store(part, source)

        loop(0, nj - 1, hand_on)
        loop(0, nj - 1, lambda k: gather_copy(part, chip, plane(k)).wait_send())
    for part in range(2):
        pltpu.make_async_copy(spreading.at[:, part], gathered.at[core, :, part], sem_keep.at[part]).wait()
        forwarded = pltpu.make_async_remote_copy(
            src_ref=spreading.at[:, part], dst_ref=gathered.at[other, :, part],
            send_sem=sem_forward.at[0, part], recv_sem=sem_forward.at[1, part],
            device_id=partner, device_id_type=MESH,
        )
        forwarded.wait_send()
        forwarded.wait_recv()


def unpack_kernel(
    nj, nz, scale, field_in, grad_in, gathered, first, second, field_out, grad_out,
    fields, stage, wide_sums, sem_field, sem_in, sem_out,
):
    channels, offsets = first.shape[1], first.shape[0]
    half_rows = stage.shape[1]
    quarter = half_rows // nj // 4
    group_rows = GROUP * channels * channels // 128
    tiles = GROUP * channels // 128
    run = 32
    near = lax.rem(far_quarter(lax.axis_index("smp"), nz) + 2, 4)
    turned = [pl.multiple_of(lax.rem(q + 4 - near, 4) * quarter, 8) for q in range(4)]

    cuts = (0, 3 * half_rows // 16, half_rows // 2, half_rows)

    def load(which, k):
        rows = pl.ds(cuts[k], cuts[k + 1] - cuts[k])
        return pltpu.make_async_copy(gathered.at[which, rows], stage.at[which, rows], sem_in.at[which, k])

    def save(which, g):
        some = pl.ds(g * GROUP, min(GROUP, offsets - g * GROUP))
        return pltpu.make_async_copy(
            wide_sums.at[which, some], (first, second)[which].at[some], sem_out.at[which, g]
        )

    loads = [pltpu.make_async_copy(x, fields.at[i], sem_field.at[0, i]) for i, x in enumerate((field_in, grad_in))]
    saves = [
        pltpu.make_async_copy(fields.at[i], x.at[0], sem_field.at[1, i]) for i, x in enumerate((field_out, grad_out))
    ]
    for which in range(2):
        for k in range(3):
            load(which, k).start()
    for copy in loads:
        copy.start()
    for which in range(2):
        here = 0
        for g in range(GROUPS):
            while here < 3 and cuts[here] < (g + 1) * group_rows:
                load(which, here).wait()
                here += 1

            def part_of(row):
                first_row = row - row % (quarter * 4) + turned[row // quarter % 4] + row % quarter
                return stage[which, pl.ds(pl.multiple_of(first_row, 8), run), :].astype(jnp.float32)

            parts = [part_of(g * group_rows + n) for n in range(0, group_rows, run)]
            step = channels // run
            wide = jnp.concatenate(
                [jnp.concatenate(parts[t * step : (t + 1) * step], axis=0) for t in range(tiles)], axis=1
            )
            wide = wide * scale
            for k in range(GROUP):
                wide_sums[which, g * GROUP + k] = wide[:, k * channels : (k + 1) * channels]
            save(which, g).start()
    for copy in loads:
        copy.wait()
    for copy in saves:
        copy.start()
    for which in range(2):
        for g in range(GROUPS):
            save(which, g).wait()
    for copy in saves:
        copy.wait()


def body(nb, nz, features, active, neighbour_rows, send_rows, first_weight, second_weight, cotangent):
    channels, voxels = features.shape[1], features.shape[2]
    both = 2 * channels
    per_list = send_rows.shape[3]
    halo_rows = 4 * per_list + 4 * CORNER
    nj = nb // 2
    half_rows = 2048
    piece = half_rows // nj
    bf16, f32 = jnp.bfloat16, jnp.float32
    anywhere = pl.BlockSpec(memory_space=pl.ANY)
    slots = lax.axis_size("smp") * features.shape[0] * nb * voxels
    table = jnp.transpose(neighbour_rows, (1, 0, 2))
    operands = (features, active, table, send_rows, first_weight, second_weight, cotangent)
    dma = pltpu.SemaphoreType.DMA
    wide = 256
    out_field, input_grad, gathered = pl.pallas_call(
        functools.partial(main_kernel, nb, nz),
        out_shape=[
            jax.ShapeDtypeStruct((channels, voxels), bf16),
            jax.ShapeDtypeStruct((channels, voxels), bf16),
            jax.ShapeDtypeStruct((2, nj, 2, piece // 2, 128), bf16),
        ],
        in_specs=[anywhere] * 7,
        out_specs=[anywhere] * 3,
        scratch_shapes=[
            *(pltpu.VMEM(x.shape, x.dtype) for x in operands),
            pltpu.VMEM((2, channels, voxels), bf16),
            pltpu.VMEM((nj, 2, piece // 2, 128), bf16),
            pltpu.VMEM((both, voxels), bf16),
            pltpu.VMEM((8 * per_list, voxels), bf16),
            pltpu.VMEM((8 * per_list, wide), bf16),
            pltpu.VMEM((halo_rows, wide), bf16),
            pltpu.VMEM((8 * per_list, wide), bf16),
            pltpu.VMEM((halo_rows, wide), bf16),
            pltpu.VMEM((OFFSETS, voxels, voxels), bf16),
            pltpu.VMEM((OFFSETS, halo_rows, voxels), bf16),
            pltpu.VMEM((OFFSETS, channels, channels), bf16),
            pltpu.VMEM((2, channels, GROUP * GROUPS * channels), bf16),
            pltpu.VMEM((2, GROUP * GROUPS * channels, voxels), bf16),
            pltpu.VMEM((2, channels, voxels), bf16),
            pltpu.VMEM((half_rows, 128), bf16),
            pltpu.VMEM((half_rows, 128), f32),
            pltpu.VMEM((half_rows, 128), bf16),
            pltpu.VMEM((nj, piece + piece // 4, 128), bf16),
            pltpu.VMEM((2, nj, piece // 2, 128), bf16),
            pltpu.VMEM((piece, 128), f32),
            pltpu.VMEM((nz, piece // nz, 128), f32),
            pltpu.VMEM((piece, 128), f32),
            pltpu.SemaphoreType.REGULAR((2, 3)),
            dma((7,)),
            dma((2,)),
            dma((2, 8)),
            dma((2, 8)),
            dma((2, GROUPS)),
            dma((2, 2, nj)),
            dma((2, nz)),
            dma((2, nz)),
            dma((2, 2, nj)),
            dma((2,)),
            dma((2, 2)),
        ],
        compiler_params=pltpu.CompilerParams(
            collective_id=0, has_side_effects=True, vmem_limit_bytes=56 * 2**20
        ),
        name="halo_conv_and_sum",
    )(*operands)

    grad = jax.ShapeDtypeStruct((OFFSETS, channels, channels), f32)
    field = jax.ShapeDtypeStruct((1, channels, voxels), bf16)
    first_grad, second_grad, out_field, input_grad = pl.pallas_call(
        functools.partial(unpack_kernel, nj, nz, 1.0 / slots**0.5),
        out_shape=[grad, grad, field, field],
        in_specs=[anywhere] * 3,
        out_specs=[anywhere] * 4,
        scratch_shapes=[
            pltpu.VMEM((2, channels, voxels), bf16),
            pltpu.VMEM((2, half_rows, 128), bf16),
            pltpu.VMEM((2, GROUP * GROUPS, channels, channels), f32),
            dma((2, 2)),
            dma((2, 3)),
            dma((2, GROUPS)),
        ],
        compiler_params=pltpu.CompilerParams(vmem_limit_bytes=56 * 2**20),
        name="unpack",
    )(out_field, input_grad, gathered.reshape(2, half_rows, 128))
    return out_field, input_grad, first_grad, second_grad


def solution(mesh):
    return jax.shard_map(
        functools.partial(body, mesh.shape["blk"], mesh.shape["smp"]),
        mesh=mesh,
        in_specs=(
            P("smp", None, "blk"),
            P("smp", "blk"),
            P("smp", None, "blk"),
            P("smp", "blk", None, None),
            P(),
            P(),
            P("smp", None, "blk"),
        ),
        out_specs=(P("smp", None, "blk"), P("smp", None, "blk"), P(), P()),
        check_vma=False,
    )
```

```python
import functools

import jax
import jax.numpy as jnp
from jax import lax
from jax.experimental import pallas as pl
from jax.experimental.pallas import tpu as pltpu
from jax.sharding import PartitionSpec as P

MESH = pl.DeviceIdType.MESH
TALL = 4
STEPS = ((-1, 0), (1, 0), (0, -1), (0, 1), (-1, -1), (-1, 1), (1, -1), (1, 1))
DELTAS = tuple(a * TALL + b for a, b in STEPS)
OFFSETS = 27
GROUP = 4
GROUPS = 7
CORNER = 16
UNROLL = 9
FIRST_UNROLL = 9


def nn(a, b):
    return lax.dot_general(a, b, (((1,), (0,)), ((), ())), preferred_element_type=jnp.float32)


def nt(a, b):
    return lax.dot_general(a, b, (((1,), (1,)), ((), ())), preferred_element_type=jnp.float32)


def eye(n, dtype):
    rows = lax.broadcasted_iota(jnp.int32, (n, n), 0)
    cols = lax.broadcasted_iota(jnp.int32, (n, n), 1)
    return (rows == cols).astype(jnp.float32).astype(dtype)


def one_hot(rows, codes):
    return jnp.where(rows == codes, 1.0, 0.0).astype(jnp.bfloat16)


def far_quarter(smp, nz):
    per_quarter = nz // 4
    late = lax.rem(smp, per_quarter) >= per_quarter // 2
    return lax.rem(lax.div(smp, per_quarter) + jnp.where(late, 2, 1), 4)


def main_kernel(
    nb, nz,
    feat_in, act_in, nbr_in, lists_in, w1_in, w2_in, cot_in,
    out_field, input_grad, gathered,
    feat, act, nbr, lists, w1, w2, cot, results, spreading,
    field, pick, sent_a, halo_a, sent_c, halo_c,
    local_hot, halo_hot, turned, side_by_side, picked, sides,
    to_core, own, from_core, summed, arrived, z_part, z_send, z_in, z_out,
    heard, sem_in, sem_out, sem_a, sem_c, sem_core, sem_plane, sem_z, sem_zg, sem_gather, sem_keep, sem_forward,
):
    bf16, f32 = jnp.bfloat16, jnp.float32
    channels, voxels = feat.shape[1], feat.shape[2]
    both = 2 * channels
    per_list = lists.shape[3]
    halo_rows = halo_a.shape[0]
    nj = nb // 2
    half_rows = own.shape[0]
    piece = half_rows // nj
    owners = nz // 2
    sliver = piece // owners
    quarter = piece // 4
    some = piece // 2
    group_rows = GROUP * channels * channels // 128
    tiles = GROUP * channels // 128
    blk = lax.axis_index("blk")
    smp = lax.axis_index("smp")
    core = lax.rem(blk, 2)
    chip = lax.div(blk, 2)
    other = 1 - core
    partner = (chip * 2 + other, smp)

    def loop(start, stop, act_on):
        def run(i, _):
            act_on(i)
            return 0

        lax.fori_loop(start, stop, run, 0)

    far = far_quarter(smp, nz)
    near = lax.rem(far + 2, 4)

    across = min(4, nj)
    row, place_in_row = lax.div(chip, across), lax.rem(chip, across)

    def ring_step(k, n):
        return jnp.where(k == n - 1, 0, n // 2 + jnp.where(lax.rem(k, 2) == 1, -lax.div(k + 1, 2), lax.div(k, 2)))

    def plane(k):
        down = lax.rem(row + ring_step(lax.div(k, across), nj // across), nj // across) if nj > across else row
        return down * across + lax.rem(place_in_row + ring_step(lax.rem(k, across), across), across)

    def plane_back(k):
        return plane(nj - 2 - k)

    def along(i):
        return lax.rem(smp + i, nz)

    def remote(src, dst, sems, source, target, device):
        return pltpu.make_async_remote_copy(
            src_ref=src, dst_ref=dst, send_sem=sems.at[0, target], recv_sem=sems.at[1, source],
            device_id=device, device_id_type=MESH,
        )

    halo_a[...] = jnp.zeros_like(halo_a)
    halo_c[...] = jnp.zeros_like(halo_c)
    barrier = pltpu.get_barrier_semaphore()
    in_range = [(blk + delta >= 0) & (blk + delta < nb) for delta in DELTAS]

    def greet(device):
        pl.semaphore_signal(barrier, inc=1, device_id=device, device_id_type=MESH)

    for delta, there in zip(DELTAS, in_range):
        pl.when(there)(functools.partial(greet, (jnp.clip(blk + delta, 0, nb - 1), smp)))
    loads = [
        pltpu.make_async_copy(src, dst, sem_in.at[i])
        for i, (src, dst) in enumerate(
            ((feat_in, feat), (cot_in, cot), (act_in, act), (lists_in, lists), (nbr_in, nbr), (w1_in, w1), (w2_in, w2))
        )
    ]
    for load in loads:
        load.start()

    beside = [row * across + lax.rem(place_in_row + step, across) for step in (1, across - 1)]
    if nj > across:
        beside += [lax.rem(chip + step, nj) for step in (across, nj - across)]
    beside = [(p * 2 + core, smp) for p in beside]
    for device in beside + [(blk, along(1)), (blk, along(nz - 1))]:
        greet(device)
    greeted = sum(there.astype(jnp.int32) for there in in_range) + len(beside) + 2

    def tell(step):
        for device in beside:
            pl.semaphore_signal(heard.at[0, step], inc=1, device_id=device, device_id_type=MESH)
        if step < rounds:
            for i in (1 << step, nz - (1 << step)):
                pl.semaphore_signal(heard.at[1, step], inc=1, device_id=(blk, along(i)), device_id_type=MESH)

    def hear_plane(step):
        pl.semaphore_wait(heard.at[0, step], len(beside))

    def hear_samples(step):
        if step < rounds:
            pl.semaphore_wait(heard.at[1, step], 2)

    rounds = max(nz // 4, 1).bit_length()

    for load in loads[:4]:
        load.wait()
    live = act[...] > 0
    live_f = live.astype(f32)
    field[0:channels, :] = jnp.where(live, feat[0].astype(f32), 0.0).astype(bf16)
    field[channels:both, :] = jnp.where(live, cot[0].astype(f32), 0.0).astype(bf16)

    spread = jnp.concatenate(
        [jnp.broadcast_to(lists[0, 0, d : d + 1, :], (per_list, per_list)) for d in range(8)], axis=0
    )
    at_row = lax.broadcasted_iota(jnp.int32, spread.shape, 0)
    at_col = lax.broadcasted_iota(jnp.int32, spread.shape, 1)
    column = jnp.sum(jnp.where(lax.rem(at_row, per_list) == at_col, spread, 0), axis=1, keepdims=True)
    pick[...] = one_hot(lax.broadcasted_iota(jnp.int32, (8 * per_list, voxels), 1), column)

    def face_copies(sent, halo, sems):
        copies = []
        for d, delta in enumerate(DELTAS):
            if d < 4:
                rows = pl.ds(d * per_list, per_list)
                into = rows
            else:
                rows = pl.ds(d * per_list, CORNER)
                into = pl.ds(4 * per_list + (d - 4) * CORNER, CORNER)
            target, source = blk + delta, blk - delta
            copy = pltpu.make_async_remote_copy(
                src_ref=sent.at[rows, :], dst_ref=halo.at[into, :],
                send_sem=sems.at[0, d], recv_sem=sems.at[1, d],
                device_id=(jnp.clip(target, 0, nb - 1), smp), device_id_type=MESH,
            )
            has_target = (target >= 0) & (target < nb)
            has_source = (source >= 0) & (source < nb)
            copies.append((copy, has_target, has_source))
        return copies

    def start_faces(copies):
        for copy, has_target, _ in copies:
            pl.when(has_target)(copy.start)

    def arrive_faces(copies):
        for copy, _, has_source in copies:
            pl.when(has_source)(copy.wait_recv)

    def finish_faces(copies):
        for copy, has_target, _ in copies:
            pl.when(has_target)(copy.wait_send)

    faces_a = face_copies(sent_a, halo_a, sem_a)
    faces_c = face_copies(sent_c, halo_c, sem_c)
    sent_a[:, 0:both] = nt(pick[...], field[...]).astype(bf16)
    sent_a[:, both:] = jnp.zeros((8 * per_list, sent_a.shape[1] - both), bf16)
    pl.semaphore_wait(barrier, greeted)
    start_faces(faces_a)
    tell(0)

    for load in loads[4:]:
        load.wait()
    unit = eye(channels, bf16)
    local_rows = lax.broadcasted_iota(jnp.int32, (voxels, voxels), 0)
    place = lax.broadcasted_iota(jnp.int32, (halo_rows, voxels), 0)
    past = place - 4 * per_list
    corner_code = jnp.where(
        lax.rem(past, CORNER) < 4, voxels + 4 * per_list + lax.div(past, CORNER) * 4 + lax.rem(past, CORNER), -1
    )
    halo_codes = jnp.where(past < 0, voxels + place, corner_code)

    def at(o):
        return pl.ds(pl.multiple_of(o * channels, 32), channels)

    def prepare(step, _):
        for u in range(UNROLL):
            o = step * UNROLL + u
            codes = nbr[o]
            hot = one_hot(local_rows, codes)
            local_hot[o] = hot
            halo_hot[o] = one_hot(halo_codes, codes)
            got = nn(field[...], hot).astype(bf16)
            picked[0, at(o), :] = got[:channels]
            picked[1, at(OFFSETS - 1 - o), :] = got[channels:]
            turned[o] = nt(unit, w1[o]).astype(bf16)
        return 0

    lax.fori_loop(0, OFFSETS // UNROLL, prepare, 0)
    blank = jnp.zeros((channels, channels), bf16)
    for g in range(GROUPS):
        lanes = pl.ds(g * GROUP * channels, GROUP * channels)
        group = range(g * GROUP, (g + 1) * GROUP)
        side_by_side[0, :, lanes] = jnp.concatenate([w1[o] if o < OFFSETS else blank for o in group], axis=1)
        side_by_side[1, :, lanes] = jnp.concatenate(
            [nt(unit, w2[o]) if o < OFFSETS else blank.astype(f32) for o in group], axis=1
        ).astype(bf16)
    tail = picked.shape[1] - OFFSETS * channels
    picked[:, OFFSETS * channels :, :] = jnp.zeros((2, tail, voxels), bf16)
    rest = half_rows - GROUPS * group_rows
    own[GROUPS * group_rows :, :] = jnp.zeros((rest, 128), f32)
    from_core[GROUPS * group_rows :, :] = jnp.zeros((rest, 128), bf16)

    hear_plane(0)
    hear_samples(0)
    tell(1)
    arrive_faces(faces_a)
    turned_halo = nt(eye(halo_a.shape[1], bf16)[:both], halo_a[...]).astype(bf16)
    zeros = jnp.zeros((channels, voxels), f32)

    def first_pass(step, _):
        for u in range(FIRST_UNROLL):
            o = step * FIRST_UNROLL + u
            mirror = OFFSETS - 1 - o
            got = nn(turned_halo, halo_hot[o]).astype(bf16)
            picked[0, at(o), :] += got[:channels]
            picked[1, at(mirror), :] += got[channels:]
        return 0

    lax.fori_loop(0, OFFSETS // FIRST_UNROLL, first_pass, 0)
    hear_plane(1)
    hear_samples(1)
    tell(2)
    forth = nn(side_by_side[0], picked[0])
    back = nn(side_by_side[1], picked[1])
    pre = live_f * forth
    gate = 1.0 / (1.0 + jnp.exp(-pre))
    hidden = (live_f * (pre * gate)).astype(bf16)
    grad_pre = ((live_f * back) * gate * (1.0 + pre * (1.0 - gate))).astype(bf16)
    sides[0] = grad_pre
    sides[1] = hidden
    field[0:channels, :] = hidden
    field[channels:both, :] = grad_pre
    sent_c[:, 0:both] = nt(pick[...], field[...]).astype(bf16)
    sent_c[:, both:] = jnp.zeros((8 * per_list, sent_c.shape[1] - both), bf16)
    start_faces(faces_c)

    def core_copy(g):
        rows = pl.ds(pl.multiple_of(g * group_rows, 32), group_rows)
        return remote(to_core.at[rows, :], from_core.at[rows, :], sem_core, g, g, partner)

    def correlate(which, g):
        rows = pl.ds(pl.multiple_of(g * (GROUP * channels), 128), GROUP * channels)
        if which == 0:
            return nt(sides[0], picked[0, rows, :])
        tall = nt(picked[1, rows, :], sides[1])
        return jnp.concatenate([tall[k * channels : (k + 1) * channels] for k in range(GROUP)], axis=1)

    def tile_rows(g, t):
        return pl.ds(pl.multiple_of(g * group_rows + t * channels, 32), channels)

    def give(which, g):
        product = correlate(which, g)
        for t in range(tiles):
            to_core[tile_rows(g, t), :] = product[:, t * 128 : (t + 1) * 128].astype(bf16)
        core_copy(g).start()

    def keep(which, g):
        product = correlate(which, g)
        for t in range(tiles):
            own[tile_rows(g, t), :] = product[:, t * 128 : (t + 1) * 128]

    def join():
        done = 0
        for p in range(nj):
            while done < GROUPS and done * group_rows < (p + 1) * piece:
                core_copy(done).wait_recv()
                done += 1
            rows = pl.ds(p * piece, piece)
            total = own[rows, :] + from_core[rows, :].astype(f32)
            own[rows, :] = total
            summed[p, 0:piece, :] = total.astype(bf16)
            summed[p, piece:, :] = total[:quarter].astype(bf16)

    for which in range(2):

        @pl.when(core == which)
        def _():
            for g in range(GROUPS):
                give(1 - which, g)
            for g in range(GROUPS):
                keep(which, g)

    join()

    def quarter_rows(q):
        return pl.ds(pl.multiple_of(q * quarter, 16), quarter)

    starts = (far, near)

    def plane_copy(part, source, target):
        rows = pl.ds(pl.multiple_of(starts[part] * quarter, 8), some)
        return pltpu.make_async_remote_copy(
            src_ref=summed.at[target, rows, :], dst_ref=arrived.at[part, source],
            send_sem=sem_plane.at[0, part, target], recv_sem=sem_plane.at[1, part, source],
            device_id=(target * 2 + core, smp), device_id_type=MESH,
        )

    hear_plane(2)
    for part in range(2):
        loop(0, nj - 1, lambda k: plane_copy(part, chip, plane(k)).start())

    def owner(w):
        return 2 * w + core

    owns = lax.rem(smp, 2) == core
    here = lax.div(smp, 2)

    def z_copy(source, target, rows):
        return remote(z_send.at[rows, :], z_in.at[source], sem_z, source, target, (blk, target))

    def part_owners(start, act_on):
        def run(k):
            w = lax.rem(start * (owners // 4) + k, owners)
            pl.when(owner(w) != smp)(lambda: act_on(w, k))

        loop(0, owners // 2, run)

    def z_sends(part, act_on):
        def run(w, k):
            act_on(owner(w), pl.ds(pl.multiple_of(part * some + k * sliver, 16), sliver))

        part_owners(starts[part], run)

    hear_samples(2)
    base = pl.multiple_of(chip * piece, piece)
    for part in range(2):
        for k in range(2):
            first_row = base + lax.rem(starts[part] + k, 4) * quarter
            z_part[part * some + k * quarter : part * some + (k + 1) * quarter, :] = own[
                pl.ds(pl.multiple_of(first_row, 8), quarter), :
            ]

        def add_piece(k):
            source = plane_back(k)
            plane_copy(part, source, source).wait_recv()
            z_part[part * some : (part + 1) * some, :] += arrived[part, source].astype(f32)

        loop(0, nj - 1, add_piece)
        z_send[part * some : (part + 1) * some, :] = z_part[part * some : (part + 1) * some, :].astype(bf16)
        z_sends(part, lambda target, rows: z_copy(smp, target, rows).start())

    arrive_faces(faces_c)
    turned_halo_c = nt(eye(halo_c.shape[1], bf16)[:both], halo_c[...]).astype(bf16)

    def second_pass(step, sums):
        forth, back = sums
        for u in range(UNROLL):
            o = step * UNROLL + u
            got = (nn(field[...], local_hot[o]) + nn(turned_halo_c, halo_hot[o])).astype(bf16)
            forth = forth + nn(w2[o], got[:channels])
            back = back + nn(turned[OFFSETS - 1 - o], got[channels:])
        return forth, back

    most = OFFSETS // UNROLL - 1
    forth, back = lax.fori_loop(0, most, second_pass, (zeros, zeros))

    def sliver_rows(w):
        return pl.ds(pl.multiple_of(w * sliver, 16), sliver)

    def zg_copy(w, target):
        part = z_out.at[sliver_rows(w), :]
        return remote(part, part, sem_zg, owner(w), target, (blk, target))

    @pl.when(owns)
    def _():
        place_here = lax.rem(here + owners - near * (owners // 4), owners)

        def add_sliver(i, running):
            source = along(i)
            z_copy(source, source, pl.ds(0, sliver)).wait_recv()
            return running + z_in[source].astype(f32)

        total = z_part[pl.ds(pl.multiple_of(some + place_here * sliver, 16), sliver), :]
        z_out[sliver_rows(here), :] = lax.fori_loop(1, nz, add_sliver, total).astype(bf16)
        loop(0, nz - 1, lambda k: zg_copy(here, along(ring_step(k, nz))).start())

    forth, back = lax.fori_loop(most, OFFSETS // UNROLL, second_pass, (forth, back))
    results[0] = (live_f * forth).astype(bf16)
    results[1] = (live_f * back).astype(bf16)
    keeps = [
        pltpu.make_async_copy(results.at[0], out_field, sem_out.at[0]),
        pltpu.make_async_copy(results.at[1], input_grad, sem_out.at[1]),
    ]
    for copy in keeps:
        copy.start()
    finish_faces(faces_a)
    finish_faces(faces_c)
    loop(0, GROUPS, lambda g: core_copy(g).wait_send())
    for part in range(2):
        loop(0, nj - 1, lambda k: plane_copy(part, chip, plane(k)).wait_send())
        z_sends(part, lambda target, rows: z_copy(smp, target, rows).wait_send())

    def gather_copy(part, source, target):
        return pltpu.make_async_remote_copy(
            src_ref=spreading.at[chip, part], dst_ref=spreading.at[source, part],
            send_sem=sem_gather.at[0, part, target], recv_sem=sem_gather.at[1, part, source],
            device_id=(target * 2 + core, smp), device_id_type=MESH,
        )

    def keep_copy(part, p):
        return pltpu.make_async_copy(spreading.at[p, part], gathered.at[core, p, part], sem_keep.at[part])

    def forward_copy(which, part, p):
        return pltpu.make_async_remote_copy(
            src_ref=spreading.at[p, part], dst_ref=gathered.at[which, p, part],
            send_sem=sem_forward.at[0, part], recv_sem=sem_forward.at[1, part],
            device_id=partner, device_id_type=MESH,
        )

    def store(part, p):
        keep_copy(part, p).start()
        forward_copy(core, part, p).start()

    for part, start in enumerate((near, far)):

        part_owners(start, lambda w, k: zg_copy(w, smp).wait_recv())
        for k in range(2):
            spreading[chip, part, k * quarter : (k + 1) * quarter, :] = z_out[
                quarter_rows(lax.rem(start + k, 4)), :
            ]
        loop(0, nj - 1, lambda k: gather_copy(part, chip, plane(k)).start())
        store(part, chip)


    @pl.when(owns)
    def _():
        loop(1, nz, lambda i: zg_copy(here, along(i)).wait_send())

    for copy in keeps:
        copy.wait()
    for part in range(2):

        def hand_on(k):
            source = plane_back(k)
            gather_copy(part, source, source).wait_recv()
            store(part, source)

        loop(0, nj - 1, hand_on)
        loop(0, nj - 1, lambda k: gather_copy(part, chip, plane(k)).wait_send())
    for part in range(2):
        pltpu.make_async_copy(spreading.at[:, part], gathered.at[core, :, part], sem_keep.at[part]).wait()
        forwarded = pltpu.make_async_remote_copy(
            src_ref=spreading.at[:, part], dst_ref=gathered.at[other, :, part],
            send_sem=sem_forward.at[0, part], recv_sem=sem_forward.at[1, part],
            device_id=partner, device_id_type=MESH,
        )
        forwarded.wait_send()
        forwarded.wait_recv()


def unpack_kernel(
    nj, nz, scale, field_in, grad_in, gathered, first, second, field_out, grad_out,
    fields, stage, wide_sums, sem_field, sem_in, sem_out,
):
    channels, offsets = first.shape[1], first.shape[0]
    half_rows = stage.shape[1]
    quarter = half_rows // nj // 4
    group_rows = GROUP * channels * channels // 128
    tiles = GROUP * channels // 128
    run = 32
    near = lax.rem(far_quarter(lax.axis_index("smp"), nz) + 2, 4)
    turned = [pl.multiple_of(lax.rem(q + 4 - near, 4) * quarter, 8) for q in range(4)]

    cuts = (0, 3 * half_rows // 16, half_rows // 2, half_rows)

    def load(which, k):
        rows = pl.ds(cuts[k], cuts[k + 1] - cuts[k])
        return pltpu.make_async_copy(gathered.at[which, rows], stage.at[which, rows], sem_in.at[which, k])

    def save(which, g):
        some = pl.ds(g * GROUP, min(GROUP, offsets - g * GROUP))
        return pltpu.make_async_copy(
            wide_sums.at[which, some], (first, second)[which].at[some], sem_out.at[which, g]
        )

    loads = [pltpu.make_async_copy(x, fields.at[i], sem_field.at[0, i]) for i, x in enumerate((field_in, grad_in))]
    saves = [
        pltpu.make_async_copy(fields.at[i], x.at[0], sem_field.at[1, i]) for i, x in enumerate((field_out, grad_out))
    ]
    for which in range(2):
        for k in range(3):
            load(which, k).start()
    for copy in loads:
        copy.start()
    for which in range(2):
        here = 0
        for g in range(GROUPS):
            while here < 3 and cuts[here] < (g + 1) * group_rows:
                load(which, here).wait()
                here += 1

            def part_of(row):
                first_row = row - row % (quarter * 4) + turned[row // quarter % 4] + row % quarter
                return stage[which, pl.ds(pl.multiple_of(first_row, 8), run), :].astype(jnp.float32)

            parts = [part_of(g * group_rows + n) for n in range(0, group_rows, run)]
            step = channels // run
            wide = jnp.concatenate(
                [jnp.concatenate(parts[t * step : (t + 1) * step], axis=0) for t in range(tiles)], axis=1
            )
            wide = wide * scale
            for k in range(GROUP):
                wide_sums[which, g * GROUP + k] = wide[:, k * channels : (k + 1) * channels]
            save(which, g).start()
    for copy in loads:
        copy.wait()
    for copy in saves:
        copy.start()
    for which in range(2):
        for g in range(GROUPS):
            save(which, g).wait()
    for copy in saves:
        copy.wait()


def body(nb, nz, features, active, neighbour_rows, send_rows, first_weight, second_weight, cotangent):
    channels, voxels = features.shape[1], features.shape[2]
    both = 2 * channels
    per_list = send_rows.shape[3]
    halo_rows = 4 * per_list + 4 * CORNER
    nj = nb // 2
    half_rows = 2048
    piece = half_rows // nj
    bf16, f32 = jnp.bfloat16, jnp.float32
    anywhere = pl.BlockSpec(memory_space=pl.ANY)
    slots = lax.axis_size("smp") * features.shape[0] * nb * voxels
    table = jnp.transpose(neighbour_rows, (1, 0, 2))
    operands = (features, active, table, send_rows, first_weight, second_weight, cotangent)
    dma = pltpu.SemaphoreType.DMA
    wide = 256
    out_field, input_grad, gathered = pl.pallas_call(
        functools.partial(main_kernel, nb, nz),
        out_shape=[
            jax.ShapeDtypeStruct((channels, voxels), bf16),
            jax.ShapeDtypeStruct((channels, voxels), bf16),
            jax.ShapeDtypeStruct((2, nj, 2, piece // 2, 128), bf16),
        ],
        in_specs=[anywhere] * 7,
        out_specs=[anywhere] * 3,
        scratch_shapes=[
            *(pltpu.VMEM(x.shape, x.dtype) for x in operands),
            pltpu.VMEM((2, channels, voxels), bf16),
            pltpu.VMEM((nj, 2, piece // 2, 128), bf16),
            pltpu.VMEM((both, voxels), bf16),
            pltpu.VMEM((8 * per_list, voxels), bf16),
            pltpu.VMEM((8 * per_list, wide), bf16),
            pltpu.VMEM((halo_rows, wide), bf16),
            pltpu.VMEM((8 * per_list, wide), bf16),
            pltpu.VMEM((halo_rows, wide), bf16),
            pltpu.VMEM((OFFSETS, voxels, voxels), bf16),
            pltpu.VMEM((OFFSETS, halo_rows, voxels), bf16),
            pltpu.VMEM((OFFSETS, channels, channels), bf16),
            pltpu.VMEM((2, channels, GROUP * GROUPS * channels), bf16),
            pltpu.VMEM((2, GROUP * GROUPS * channels, voxels), bf16),
            pltpu.VMEM((2, channels, voxels), bf16),
            pltpu.VMEM((half_rows, 128), bf16),
            pltpu.VMEM((half_rows, 128), f32),
            pltpu.VMEM((half_rows, 128), bf16),
            pltpu.VMEM((nj, piece + piece // 4, 128), bf16),
            pltpu.VMEM((2, nj, piece // 2, 128), bf16),
            pltpu.VMEM((piece, 128), f32),
            pltpu.VMEM((piece, 128), bf16),
            pltpu.VMEM((nz, piece // (nz // 2), 128), bf16),
            pltpu.VMEM((piece, 128), bf16),
            pltpu.SemaphoreType.REGULAR((2, 3)),
            dma((7,)),
            dma((2,)),
            dma((2, 8)),
            dma((2, 8)),
            dma((2, GROUPS)),
            dma((2, 2, nj)),
            dma((2, nz)),
            dma((2, nz)),
            dma((2, 2, nj)),
            dma((2,)),
            dma((2, 2)),
        ],
        compiler_params=pltpu.CompilerParams(
            collective_id=0, has_side_effects=True, vmem_limit_bytes=56 * 2**20
        ),
        name="halo_conv_and_sum",
    )(*operands)

    grad = jax.ShapeDtypeStruct((OFFSETS, channels, channels), f32)
    field = jax.ShapeDtypeStruct((1, channels, voxels), bf16)
    first_grad, second_grad, out_field, input_grad = pl.pallas_call(
        functools.partial(unpack_kernel, nj, nz, 1.0 / slots**0.5),
        out_shape=[grad, grad, field, field],
        in_specs=[anywhere] * 3,
        out_specs=[anywhere] * 4,
        scratch_shapes=[
            pltpu.VMEM((2, channels, voxels), bf16),
            pltpu.VMEM((2, half_rows, 128), bf16),
            pltpu.VMEM((2, GROUP * GROUPS, channels, channels), f32),
            dma((2, 2)),
            dma((2, 3)),
            dma((2, GROUPS)),
        ],
        compiler_params=pltpu.CompilerParams(vmem_limit_bytes=56 * 2**20),
        name="unpack",
    )(out_field, input_grad, gathered.reshape(2, half_rows, 128))
    return out_field, input_grad, first_grad, second_grad


def solution(mesh):
    return jax.shard_map(
        functools.partial(body, mesh.shape["blk"], mesh.shape["smp"]),
        mesh=mesh,
        in_specs=(
            P("smp", None, "blk"),
            P("smp", "blk"),
            P("smp", None, "blk"),
            P("smp", "blk", None, None),
            P(),
            P(),
            P("smp", None, "blk"),
        ),
        out_specs=(P("smp", None, "blk"), P("smp", None, "blk"), P(), P()),
        check_vma=False,
    )
```

```python
import functools

import jax
import jax.numpy as jnp
from jax import lax
from jax.experimental import pallas as pl
from jax.experimental.pallas import tpu as pltpu
from jax.sharding import PartitionSpec as P

MESH = pl.DeviceIdType.MESH
TALL = 4
STEPS = ((-1, 0), (1, 0), (0, -1), (0, 1), (-1, -1), (-1, 1), (1, -1), (1, 1))
DELTAS = tuple(a * TALL + b for a, b in STEPS)
OFFSETS = 27
GROUP = 4
GROUPS = 7
CORNER = 16
UNROLL = 9
FIRST_UNROLL = 27
CHUNKS = ((0, 7),)


def nn(a, b):
    return lax.dot_general(a, b, (((1,), (0,)), ((), ())), preferred_element_type=jnp.float32)


def nt(a, b):
    return lax.dot_general(a, b, (((1,), (1,)), ((), ())), preferred_element_type=jnp.float32)


def eye(n, dtype):
    rows = lax.broadcasted_iota(jnp.int32, (n, n), 0)
    cols = lax.broadcasted_iota(jnp.int32, (n, n), 1)
    return (rows == cols).astype(jnp.float32).astype(dtype)


def one_hot(rows, codes):
    return jnp.where(rows == codes, 1.0, 0.0).astype(jnp.bfloat16)


def far_quarter(smp, nz):
    per_quarter = nz // 4
    late = lax.rem(smp, per_quarter) >= per_quarter // 2
    return lax.rem(lax.div(smp, per_quarter) + jnp.where(late, 2, 1), 4)


def main_kernel(
    nb, nz,
    feat_in, act_in, nbr_in, lists_in, w1_in, w2_in, cot_in,
    out_field, input_grad, gathered,
    feat, act, nbr, lists, w1, w2, cot, results, spreading,
    field, pick, sent_a, halo_a, sent_c, halo_c,
    local_hot, halo_hot, turned, side_by_side, picked, sides,
    to_core, own, from_core, summed, arrived, z_part, z_send, z_in, z_out,
    heard, sem_in, sem_out, sem_a, sem_c, sem_core, sem_plane, sem_z, sem_zg, sem_gather, sem_keep, sem_forward,
):
    bf16, f32 = jnp.bfloat16, jnp.float32
    channels, voxels = feat.shape[1], feat.shape[2]
    both = 2 * channels
    per_list = lists.shape[3]
    halo_rows = halo_a.shape[0]
    nj = nb // 2
    half_rows = own.shape[0]
    piece = half_rows // nj
    owners = nz // 2
    sliver = piece // owners
    quarter = piece // 4
    some = piece // 2
    group_rows = GROUP * channels * channels // 128
    tiles = GROUP * channels // 128
    blk = lax.axis_index("blk")
    smp = lax.axis_index("smp")
    core = lax.rem(blk, 2)
    chip = lax.div(blk, 2)
    other = 1 - core
    partner = (chip * 2 + other, smp)

    def loop(start, stop, act_on):
        def run(i, _):
            act_on(i)
            return 0

        lax.fori_loop(start, stop, run, 0)

    far = far_quarter(smp, nz)
    near = lax.rem(far + 2, 4)

    across = min(4, nj)
    row, place_in_row = lax.div(chip, across), lax.rem(chip, across)

    def ring_step(k, n):
        return jnp.where(k == n - 1, 0, n // 2 + jnp.where(lax.rem(k, 2) == 1, -lax.div(k + 1, 2), lax.div(k, 2)))

    def plane(k):
        down = lax.rem(row + ring_step(lax.div(k, across), nj // across), nj // across) if nj > across else row
        return down * across + lax.rem(place_in_row + ring_step(lax.rem(k, across), across), across)

    def plane_back(k):
        return plane(nj - 2 - k)

    def along(i):
        return lax.rem(smp + i, nz)

    def remote(src, dst, sems, source, target, device):
        return pltpu.make_async_remote_copy(
            src_ref=src, dst_ref=dst, send_sem=sems.at[0, target], recv_sem=sems.at[1, source],
            device_id=device, device_id_type=MESH,
        )

    halo_a[...] = jnp.zeros_like(halo_a)
    halo_c[...] = jnp.zeros_like(halo_c)
    barrier = pltpu.get_barrier_semaphore()
    in_range = [(blk + delta >= 0) & (blk + delta < nb) for delta in DELTAS]

    def greet(device):
        pl.semaphore_signal(barrier, inc=1, device_id=device, device_id_type=MESH)

    for delta, there in zip(DELTAS, in_range):
        pl.when(there)(functools.partial(greet, (jnp.clip(blk + delta, 0, nb - 1), smp)))
    loads = [
        pltpu.make_async_copy(src, dst, sem_in.at[i])
        for i, (src, dst) in enumerate(
            ((feat_in, feat), (cot_in, cot), (act_in, act), (lists_in, lists), (nbr_in, nbr), (w1_in, w1), (w2_in, w2))
        )
    ]
    for load in loads:
        load.start()

    beside = [row * across + lax.rem(place_in_row + step, across) for step in (1, across - 1)]
    if nj > across:
        beside += [lax.rem(chip + step, nj) for step in (across, nj - across)]
    beside = [(p * 2 + core, smp) for p in beside]
    for device in beside + [(blk, along(1)), (blk, along(nz - 1))]:
        greet(device)
    greeted = sum(there.astype(jnp.int32) for there in in_range) + len(beside) + 2

    def tell(step):
        for device in beside:
            pl.semaphore_signal(heard.at[0, step], inc=1, device_id=device, device_id_type=MESH)
        if step < rounds:
            for i in (1 << step, nz - (1 << step)):
                pl.semaphore_signal(heard.at[1, step], inc=1, device_id=(blk, along(i)), device_id_type=MESH)

    def hear_plane(step):
        pl.semaphore_wait(heard.at[0, step], len(beside))

    def hear_samples(step):
        if step < rounds:
            pl.semaphore_wait(heard.at[1, step], 2)

    rounds = max(nz // 4, 1).bit_length()

    for load in loads[:4]:
        load.wait()
    live = act[...] > 0
    live_f = live.astype(f32)
    field[0:channels, :] = jnp.where(live, feat[0].astype(f32), 0.0).astype(bf16)
    field[channels:both, :] = jnp.where(live, cot[0].astype(f32), 0.0).astype(bf16)

    spread = jnp.concatenate(
        [jnp.broadcast_to(lists[0, 0, d : d + 1, :], (per_list, per_list)) for d in range(8)], axis=0
    )
    at_row = lax.broadcasted_iota(jnp.int32, spread.shape, 0)
    at_col = lax.broadcasted_iota(jnp.int32, spread.shape, 1)
    column = jnp.sum(jnp.where(lax.rem(at_row, per_list) == at_col, spread, 0), axis=1, keepdims=True)
    pick[...] = one_hot(lax.broadcasted_iota(jnp.int32, (8 * per_list, voxels), 1), column)

    def face_copies(sent, halo, sems):
        copies = []
        for d, delta in enumerate(DELTAS):
            if d < 4:
                rows = pl.ds(d * per_list, per_list)
                into = rows
            else:
                rows = pl.ds(d * per_list, CORNER)
                into = pl.ds(4 * per_list + (d - 4) * CORNER, CORNER)
            target, source = blk + delta, blk - delta
            copy = pltpu.make_async_remote_copy(
                src_ref=sent.at[rows, :], dst_ref=halo.at[into, :],
                send_sem=sems.at[0, d], recv_sem=sems.at[1, d],
                device_id=(jnp.clip(target, 0, nb - 1), smp), device_id_type=MESH,
            )
            has_target = (target >= 0) & (target < nb)
            has_source = (source >= 0) & (source < nb)
            copies.append((copy, has_target, has_source))
        return copies

    def start_faces(copies):
        for copy, has_target, _ in copies:
            pl.when(has_target)(copy.start)

    def arrive_faces(copies):
        for copy, _, has_source in copies:
            pl.when(has_source)(copy.wait_recv)

    def finish_faces(copies):
        for copy, has_target, _ in copies:
            pl.when(has_target)(copy.wait_send)

    faces_a = face_copies(sent_a, halo_a, sem_a)
    faces_c = face_copies(sent_c, halo_c, sem_c)
    sent_a[:, 0:both] = nt(pick[...], field[...]).astype(bf16)
    sent_a[:, both:] = jnp.zeros((8 * per_list, sent_a.shape[1] - both), bf16)
    pl.semaphore_wait(barrier, greeted)
    start_faces(faces_a)
    tell(0)

    for load in loads[4:]:
        load.wait()
    unit = eye(channels, bf16)
    local_rows = lax.broadcasted_iota(jnp.int32, (voxels, voxels), 0)
    place = lax.broadcasted_iota(jnp.int32, (halo_rows, voxels), 0)
    past = place - 4 * per_list
    corner_code = jnp.where(
        lax.rem(past, CORNER) < 4, voxels + 4 * per_list + lax.div(past, CORNER) * 4 + lax.rem(past, CORNER), -1
    )
    halo_codes = jnp.where(past < 0, voxels + place, corner_code)

    def at(o):
        return pl.ds(pl.multiple_of(o * channels, 32), channels)

    def prepare(step, _):
        for u in range(UNROLL):
            o = step * UNROLL + u
            codes = nbr[o]
            hot = one_hot(local_rows, codes)
            local_hot[o] = hot
            halo_hot[o] = one_hot(halo_codes, codes)
            got = nn(field[...], hot).astype(bf16)
            picked[0, at(o), :] = got[:channels]
            picked[1, at(OFFSETS - 1 - o), :] = got[channels:]
            turned[o] = nt(unit, w1[o]).astype(bf16)
        return 0

    lax.fori_loop(0, OFFSETS // UNROLL, prepare, 0)
    blank = jnp.zeros((channels, channels), bf16)
    for g in range(GROUPS):
        lanes = pl.ds(g * GROUP * channels, GROUP * channels)
        group = range(g * GROUP, (g + 1) * GROUP)
        side_by_side[0, :, lanes] = jnp.concatenate([w1[o] if o < OFFSETS else blank for o in group], axis=1)
        side_by_side[1, :, lanes] = jnp.concatenate(
            [nt(unit, w2[o]) if o < OFFSETS else blank.astype(f32) for o in group], axis=1
        ).astype(bf16)
    tail = picked.shape[1] - OFFSETS * channels
    picked[:, OFFSETS * channels :, :] = jnp.zeros((2, tail, voxels), bf16)
    rest = half_rows - GROUPS * group_rows
    own[GROUPS * group_rows :, :] = jnp.zeros((rest, 128), f32)
    from_core[GROUPS * group_rows :, :] = jnp.zeros((rest, 128), bf16)

    hear_plane(0)
    hear_samples(0)
    tell(1)
    arrive_faces(faces_a)
    turned_halo = nt(eye(halo_a.shape[1], bf16)[:both], halo_a[...]).astype(bf16)
    zeros = jnp.zeros((channels, voxels), f32)

    def first_pass(step, _):
        for u in range(FIRST_UNROLL):
            o = step * FIRST_UNROLL + u
            mirror = OFFSETS - 1 - o
            got = nn(turned_halo, halo_hot[o]).astype(bf16)
            picked[0, at(o), :] += got[:channels]
            picked[1, at(mirror), :] += got[channels:]
        return 0

    lax.fori_loop(0, OFFSETS // FIRST_UNROLL, first_pass, 0)
    hear_plane(1)
    hear_samples(1)
    tell(2)
    forth = nn(side_by_side[0], picked[0])
    back = nn(side_by_side[1], picked[1])
    pre = live_f * forth
    gate = 1.0 / (1.0 + jnp.exp(-pre))
    hidden = (live_f * (pre * gate)).astype(bf16)
    grad_pre = ((live_f * back) * gate * (1.0 + pre * (1.0 - gate))).astype(bf16)
    sides[0] = grad_pre
    sides[1] = hidden
    field[0:channels, :] = hidden
    field[channels:both, :] = grad_pre
    sent_c[:, 0:both] = nt(pick[...], field[...]).astype(bf16)
    sent_c[:, both:] = jnp.zeros((8 * per_list, sent_c.shape[1] - both), bf16)
    start_faces(faces_c)

    def core_copy(g):
        rows = pl.ds(pl.multiple_of(g * group_rows, 32), group_rows)
        return remote(to_core.at[rows, :], from_core.at[rows, :], sem_core, g, g, partner)

    def correlate(which, groups, dtype):
        wide = GROUP * channels
        rows = pl.ds(groups[0] * wide, (groups[1] - groups[0]) * wide)
        if which == 0:
            flat = nt(sides[0], picked[0, rows, :]).astype(dtype)
            return [flat[:, n * wide : (n + 1) * wide] for n in range(groups[1] - groups[0])]
        tall = nt(picked[1, rows, :], sides[1]).astype(dtype)
        return [
            jnp.concatenate([tall[n + k * channels : n + (k + 1) * channels] for k in range(GROUP)], axis=1)
            for n in range(0, tall.shape[0], wide)
        ]

    def put(where, g, block):
        for t in range(tiles):
            rows = pl.ds(g * group_rows + t * channels, channels)
            where[rows, :] = block[:, t * 128 : (t + 1) * 128]

    def give(which, groups):
        for g, block in zip(range(*groups), correlate(which, groups, bf16)):
            put(to_core, g, block)
            core_copy(g).start()

    def keep(which, groups):
        for g, block in zip(range(*groups), correlate(which, groups, f32)):
            put(own, g, block)

    def join():
        done = 0
        for p in range(nj):
            while done < GROUPS and done * group_rows < (p + 1) * piece:
                core_copy(done).wait_recv()
                done += 1
            rows = pl.ds(p * piece, piece)
            total = own[rows, :] + from_core[rows, :].astype(f32)
            own[rows, :] = total
            summed[p, 0:piece, :] = total.astype(bf16)
            summed[p, piece:, :] = total[:quarter].astype(bf16)

    for which in range(2):

        @pl.when(core == which)
        def _():
            for groups in CHUNKS:
                give(1 - which, groups)
            for groups in CHUNKS:
                keep(which, groups)

    join()

    def quarter_rows(q):
        return pl.ds(pl.multiple_of(q * quarter, 16), quarter)

    starts = (far, near)

    def plane_copy(part, source, target):
        rows = pl.ds(pl.multiple_of(starts[part] * quarter, 8), some)
        return pltpu.make_async_remote_copy(
            src_ref=summed.at[target, rows, :], dst_ref=arrived.at[part, source],
            send_sem=sem_plane.at[0, part, target], recv_sem=sem_plane.at[1, part, source],
            device_id=(target * 2 + core, smp), device_id_type=MESH,
        )

    hear_plane(2)
    for part in range(2):
        loop(0, nj - 1, lambda k: plane_copy(part, chip, plane(k)).start())

    def owner(w):
        return 2 * w + core

    owns = lax.rem(smp, 2) == core
    here = lax.div(smp, 2)

    def z_copy(source, target, rows):
        return remote(z_send.at[rows, :], z_in.at[source], sem_z, source, target, (blk, target))

    def part_owners(start, act_on):
        def run(k):
            w = lax.rem(start * (owners // 4) + k, owners)
            pl.when(owner(w) != smp)(lambda: act_on(w, k))

        loop(0, owners // 2, run)

    def z_sends(part, act_on):
        def run(w, k):
            act_on(owner(w), pl.ds(pl.multiple_of(part * some + k * sliver, 16), sliver))

        part_owners(starts[part], run)

    hear_samples(2)
    base = pl.multiple_of(chip * piece, piece)
    for part in range(2):
        for k in range(2):
            first_row = base + lax.rem(starts[part] + k, 4) * quarter
            z_part[part * some + k * quarter : part * some + (k + 1) * quarter, :] = own[
                pl.ds(pl.multiple_of(first_row, 8), quarter), :
            ]

        def add_piece(k):
            source = plane_back(k)
            plane_copy(part, source, source).wait_recv()
            z_part[part * some : (part + 1) * some, :] += arrived[part, source].astype(f32)

        loop(0, nj - 1, add_piece)
        z_send[part * some : (part + 1) * some, :] = z_part[part * some : (part + 1) * some, :].astype(bf16)
        z_sends(part, lambda target, rows: z_copy(smp, target, rows).start())

    arrive_faces(faces_c)
    turned_halo_c = nt(eye(halo_c.shape[1], bf16)[:both], halo_c[...]).astype(bf16)

    def second_pass(step, sums):
        forth, back = sums
        for u in range(UNROLL):
            o = step * UNROLL + u
            got = (nn(field[...], local_hot[o]) + nn(turned_halo_c, halo_hot[o])).astype(bf16)
            forth = forth + nn(w2[o], got[:channels])
            back = back + nn(turned[OFFSETS - 1 - o], got[channels:])
        return forth, back

    most = OFFSETS // UNROLL - 1
    forth, back = lax.fori_loop(0, most, second_pass, (zeros, zeros))

    def sliver_rows(w):
        return pl.ds(pl.multiple_of(w * sliver, 16), sliver)

    def zg_copy(w, target):
        part = z_out.at[sliver_rows(w), :]
        return remote(part, part, sem_zg, owner(w), target, (blk, target))

    @pl.when(owns)
    def _():
        place_here = lax.rem(here + owners - near * (owners // 4), owners)

        def add_sliver(i, running):
            source = along(i)
            z_copy(source, source, pl.ds(0, sliver)).wait_recv()
            return running + z_in[source].astype(f32)

        total = z_part[pl.ds(pl.multiple_of(some + place_here * sliver, 16), sliver), :]
        z_out[sliver_rows(here), :] = lax.fori_loop(1, nz, add_sliver, total).astype(bf16)
        loop(0, nz - 1, lambda k: zg_copy(here, along(ring_step(k, nz))).start())

    forth, back = lax.fori_loop(most, OFFSETS // UNROLL, second_pass, (forth, back))
    results[0] = (live_f * forth).astype(bf16)
    results[1] = (live_f * back).astype(bf16)
    keeps = [
        pltpu.make_async_copy(results.at[0], out_field, sem_out.at[0]),
        pltpu.make_async_copy(results.at[1], input_grad, sem_out.at[1]),
    ]
    for copy in keeps:
        copy.start()
    finish_faces(faces_a)
    finish_faces(faces_c)
    loop(0, GROUPS, lambda g: core_copy(g).wait_send())
    for part in range(2):
        loop(0, nj - 1, lambda k: plane_copy(part, chip, plane(k)).wait_send())
        z_sends(part, lambda target, rows: z_copy(smp, target, rows).wait_send())

    def gather_copy(part, source, target):
        return pltpu.make_async_remote_copy(
            src_ref=spreading.at[chip, part], dst_ref=spreading.at[source, part],
            send_sem=sem_gather.at[0, part, target], recv_sem=sem_gather.at[1, part, source],
            device_id=(target * 2 + core, smp), device_id_type=MESH,
        )

    def keep_copy(part, p):
        return pltpu.make_async_copy(spreading.at[p, part], gathered.at[core, p, part], sem_keep.at[part])

    def forward_copy(which, part, p):
        return pltpu.make_async_remote_copy(
            src_ref=spreading.at[p, part], dst_ref=gathered.at[which, p, part],
            send_sem=sem_forward.at[0, part], recv_sem=sem_forward.at[1, part],
            device_id=partner, device_id_type=MESH,
        )

    def store(part, p):
        keep_copy(part, p).start()
        forward_copy(core, part, p).start()

    for part, start in enumerate((near, far)):

        part_owners(start, lambda w, k: zg_copy(w, smp).wait_recv())
        for k in range(2):
            spreading[chip, part, k * quarter : (k + 1) * quarter, :] = z_out[
                quarter_rows(lax.rem(start + k, 4)), :
            ]
        loop(0, nj - 1, lambda k: gather_copy(part, chip, plane(k)).start())
        store(part, chip)


    @pl.when(owns)
    def _():
        loop(1, nz, lambda i: zg_copy(here, along(i)).wait_send())

    for copy in keeps:
        copy.wait()
    for part in range(2):

        def hand_on(k):
            source = plane_back(k)
            gather_copy(part, source, source).wait_recv()
            store(part, source)

        loop(0, nj - 1, hand_on)
        loop(0, nj - 1, lambda k: gather_copy(part, chip, plane(k)).wait_send())
    for part in range(2):
        pltpu.make_async_copy(spreading.at[:, part], gathered.at[core, :, part], sem_keep.at[part]).wait()
        forwarded = pltpu.make_async_remote_copy(
            src_ref=spreading.at[:, part], dst_ref=gathered.at[other, :, part],
            send_sem=sem_forward.at[0, part], recv_sem=sem_forward.at[1, part],
            device_id=partner, device_id_type=MESH,
        )
        forwarded.wait_send()
        forwarded.wait_recv()


def unpack_kernel(
    nj, nz, scale, field_in, grad_in, gathered, first, second, field_out, grad_out,
    fields, stage, wide_sums, sem_field, sem_in, sem_out,
):
    channels, offsets = first.shape[1], first.shape[0]
    half_rows = stage.shape[1]
    quarter = half_rows // nj // 4
    group_rows = GROUP * channels * channels // 128
    tiles = GROUP * channels // 128
    run = 32
    near = lax.rem(far_quarter(lax.axis_index("smp"), nz) + 2, 4)
    turned = [pl.multiple_of(lax.rem(q + 4 - near, 4) * quarter, 8) for q in range(4)]

    cuts = (0, 3 * half_rows // 16, half_rows // 2, half_rows)

    def load(which, k):
        rows = pl.ds(cuts[k], cuts[k + 1] - cuts[k])
        return pltpu.make_async_copy(gathered.at[which, rows], stage.at[which, rows], sem_in.at[which, k])

    def save(which, g):
        some = pl.ds(g * GROUP, min(GROUP, offsets - g * GROUP))
        return pltpu.make_async_copy(
            wide_sums.at[which, some], (first, second)[which].at[some], sem_out.at[which, g]
        )

    loads = [pltpu.make_async_copy(x, fields.at[i], sem_field.at[0, i]) for i, x in enumerate((field_in, grad_in))]
    saves = [
        pltpu.make_async_copy(fields.at[i], x.at[0], sem_field.at[1, i]) for i, x in enumerate((field_out, grad_out))
    ]
    for which in range(2):
        for k in range(3):
            load(which, k).start()
    for copy in loads:
        copy.start()
    for which in range(2):
        here = 0
        for g in range(GROUPS):
            while here < 3 and cuts[here] < (g + 1) * group_rows:
                load(which, here).wait()
                here += 1

            def part_of(row):
                first_row = row - row % (quarter * 4) + turned[row // quarter % 4] + row % quarter
                return stage[which, pl.ds(pl.multiple_of(first_row, 8), run), :].astype(jnp.float32)

            parts = [part_of(g * group_rows + n) for n in range(0, group_rows, run)]
            step = channels // run
            wide = jnp.concatenate(
                [jnp.concatenate(parts[t * step : (t + 1) * step], axis=0) for t in range(tiles)], axis=1
            )
            wide = wide * scale
            for k in range(GROUP):
                wide_sums[which, g * GROUP + k] = wide[:, k * channels : (k + 1) * channels]
            save(which, g).start()
    for copy in loads:
        copy.wait()
    for copy in saves:
        copy.start()
    for which in range(2):
        for g in range(GROUPS):
            save(which, g).wait()
    for copy in saves:
        copy.wait()


def body(nb, nz, features, active, neighbour_rows, send_rows, first_weight, second_weight, cotangent):
    channels, voxels = features.shape[1], features.shape[2]
    both = 2 * channels
    per_list = send_rows.shape[3]
    halo_rows = 4 * per_list + 4 * CORNER
    nj = nb // 2
    half_rows = 2048
    piece = half_rows // nj
    bf16, f32 = jnp.bfloat16, jnp.float32
    anywhere = pl.BlockSpec(memory_space=pl.ANY)
    slots = lax.axis_size("smp") * features.shape[0] * nb * voxels
    table = jnp.transpose(neighbour_rows, (1, 0, 2))
    operands = (features, active, table, send_rows, first_weight, second_weight, cotangent)
    dma = pltpu.SemaphoreType.DMA
    wide = 256
    out_field, input_grad, gathered = pl.pallas_call(
        functools.partial(main_kernel, nb, nz),
        out_shape=[
            jax.ShapeDtypeStruct((channels, voxels), bf16),
            jax.ShapeDtypeStruct((channels, voxels), bf16),
            jax.ShapeDtypeStruct((2, nj, 2, piece // 2, 128), bf16),
        ],
        in_specs=[anywhere] * 7,
        out_specs=[anywhere] * 3,
        scratch_shapes=[
            *(pltpu.VMEM(x.shape, x.dtype) for x in operands),
            pltpu.VMEM((2, channels, voxels), bf16),
            pltpu.VMEM((nj, 2, piece // 2, 128), bf16),
            pltpu.VMEM((both, voxels), bf16),
            pltpu.VMEM((8 * per_list, voxels), bf16),
            pltpu.VMEM((8 * per_list, wide), bf16),
            pltpu.VMEM((halo_rows, wide), bf16),
            pltpu.VMEM((8 * per_list, wide), bf16),
            pltpu.VMEM((halo_rows, wide), bf16),
            pltpu.VMEM((OFFSETS, voxels, voxels), bf16),
            pltpu.VMEM((OFFSETS, halo_rows, voxels), bf16),
            pltpu.VMEM((OFFSETS, channels, channels), bf16),
            pltpu.VMEM((2, channels, GROUP * GROUPS * channels), bf16),
            pltpu.VMEM((2, GROUP * GROUPS * channels, voxels), bf16),
            pltpu.VMEM((2, channels, voxels), bf16),
            pltpu.VMEM((half_rows, 128), bf16),
            pltpu.VMEM((half_rows, 128), f32),
            pltpu.VMEM((half_rows, 128), bf16),
            pltpu.VMEM((nj, piece + piece // 4, 128), bf16),
            pltpu.VMEM((2, nj, piece // 2, 128), bf16),
            pltpu.VMEM((piece, 128), f32),
            pltpu.VMEM((piece, 128), bf16),
            pltpu.VMEM((nz, piece // (nz // 2), 128), bf16),
            pltpu.VMEM((piece, 128), bf16),
            pltpu.SemaphoreType.REGULAR((2, 3)),
            dma((7,)),
            dma((2,)),
            dma((2, 8)),
            dma((2, 8)),
            dma((2, GROUPS)),
            dma((2, 2, nj)),
            dma((2, nz)),
            dma((2, nz)),
            dma((2, 2, nj)),
            dma((2,)),
            dma((2, 2)),
        ],
        compiler_params=pltpu.CompilerParams(
            collective_id=0, has_side_effects=True, vmem_limit_bytes=56 * 2**20
        ),
        name="halo_conv_and_sum",
    )(*operands)

    grad = jax.ShapeDtypeStruct((OFFSETS, channels, channels), f32)
    field = jax.ShapeDtypeStruct((1, channels, voxels), bf16)
    first_grad, second_grad, out_field, input_grad = pl.pallas_call(
        functools.partial(unpack_kernel, nj, nz, 1.0 / slots**0.5),
        out_shape=[grad, grad, field, field],
        in_specs=[anywhere] * 3,
        out_specs=[anywhere] * 4,
        scratch_shapes=[
            pltpu.VMEM((2, channels, voxels), bf16),
            pltpu.VMEM((2, half_rows, 128), bf16),
            pltpu.VMEM((2, GROUP * GROUPS, channels, channels), f32),
            dma((2, 2)),
            dma((2, 3)),
            dma((2, GROUPS)),
        ],
        compiler_params=pltpu.CompilerParams(vmem_limit_bytes=56 * 2**20),
        name="unpack",
    )(out_field, input_grad, gathered.reshape(2, half_rows, 128))
    return out_field, input_grad, first_grad, second_grad


def solution(mesh):
    return jax.shard_map(
        functools.partial(body, mesh.shape["blk"], mesh.shape["smp"]),
        mesh=mesh,
        in_specs=(
            P("smp", None, "blk"),
            P("smp", "blk"),
            P("smp", None, "blk"),
            P("smp", "blk", None, None),
            P(),
            P(),
            P("smp", None, "blk"),
        ),
        out_specs=(P("smp", None, "blk"), P("smp", None, "blk"), P(), P()),
        check_vma=False,
    )
```

```python
import functools

import jax
import jax.numpy as jnp
from jax import lax
from jax.experimental import pallas as pl
from jax.experimental.pallas import tpu as pltpu
from jax.sharding import PartitionSpec as P

MESH = pl.DeviceIdType.MESH
TALL = 4
STEPS = ((-1, 0), (1, 0), (0, -1), (0, 1), (-1, -1), (-1, 1), (1, -1), (1, 1))
DELTAS = tuple(a * TALL + b for a, b in STEPS)
OFFSETS = 27
GROUP = 4
GROUPS = 7
CORNER = 16
UNROLL = 9
FIRST_UNROLL = 27
CHUNKS = ((0, 7),)


def nn(a, b):
    return lax.dot_general(a, b, (((1,), (0,)), ((), ())), preferred_element_type=jnp.float32)


def nt(a, b):
    return lax.dot_general(a, b, (((1,), (1,)), ((), ())), preferred_element_type=jnp.float32)


def eye(n, dtype):
    rows = lax.broadcasted_iota(jnp.int32, (n, n), 0)
    cols = lax.broadcasted_iota(jnp.int32, (n, n), 1)
    return (rows == cols).astype(jnp.float32).astype(dtype)


def one_hot(rows, codes):
    return jnp.where(rows == codes, 1.0, 0.0).astype(jnp.bfloat16)


def far_quarter(smp, nz):
    per_quarter = nz // 4
    late = lax.rem(smp, per_quarter) >= per_quarter // 2
    return lax.rem(lax.div(smp, per_quarter) + jnp.where(late, 2, 1), 4)


def main_kernel(
    nb, nz,
    feat_in, act_in, nbr_in, lists_in, w1_in, w2_in, cot_in,
    out_field, input_grad, gathered,
    feat, act, nbr, lists, w1, w2, cot, results, spreading,
    field, pick, sent_a, halo_a, sent_c, halo_c,
    local_hot, halo_hot, turned, side_by_side, picked, sides,
    to_core, own, from_core, summed, arrived, z_part, z_send, z_in, z_out,
    heard, sem_in, sem_out, sem_a, sem_c, sem_core, sem_plane, sem_z, sem_zg, sem_gather, sem_keep, sem_forward,
):
    bf16, f32 = jnp.bfloat16, jnp.float32
    channels, voxels = feat.shape[1], feat.shape[2]
    both = 2 * channels
    per_list = lists.shape[3]
    halo_rows = halo_a.shape[0]
    nj = nb // 2
    half_rows = own.shape[0]
    piece = half_rows // nj
    owners = nz // 2
    sliver = piece // owners
    quarter = piece // 4
    some = piece // 2
    group_rows = GROUP * channels * channels // 128
    tiles = GROUP * channels // 128
    blk = lax.axis_index("blk")
    smp = lax.axis_index("smp")
    core = lax.rem(blk, 2)
    chip = lax.div(blk, 2)
    other = 1 - core
    partner = (chip * 2 + other, smp)

    def loop(start, stop, act_on):
        def run(i, _):
            act_on(i)
            return 0

        lax.fori_loop(start, stop, run, 0)

    far = far_quarter(smp, nz)
    near = lax.rem(far + 2, 4)

    across = min(4, nj)
    row, place_in_row = lax.div(chip, across), lax.rem(chip, across)

    def ring_step(k, n):
        return jnp.where(k == n - 1, 0, n // 2 + jnp.where(lax.rem(k, 2) == 1, -lax.div(k + 1, 2), lax.div(k, 2)))

    def plane(k):
        down = lax.rem(row + ring_step(lax.div(k, across), nj // across), nj // across) if nj > across else row
        return down * across + lax.rem(place_in_row + ring_step(lax.rem(k, across), across), across)

    def plane_back(k):
        return plane(nj - 2 - k)

    def along(i):
        return lax.rem(smp + i, nz)

    def remote(src, dst, sems, source, target, device):
        return pltpu.make_async_remote_copy(
            src_ref=src, dst_ref=dst, send_sem=sems.at[0, target], recv_sem=sems.at[1, source],
            device_id=device, device_id_type=MESH,
        )

    halo_a[...] = jnp.zeros_like(halo_a)
    halo_c[...] = jnp.zeros_like(halo_c)
    barrier = pltpu.get_barrier_semaphore()
    in_range = [(blk + delta >= 0) & (blk + delta < nb) for delta in DELTAS]

    def greet(device):
        pl.semaphore_signal(barrier, inc=1, device_id=device, device_id_type=MESH)

    for delta, there in zip(DELTAS, in_range):
        pl.when(there)(functools.partial(greet, (jnp.clip(blk + delta, 0, nb - 1), smp)))
    loads = [
        pltpu.make_async_copy(src, dst, sem_in.at[i])
        for i, (src, dst) in enumerate(
            ((feat_in, feat), (cot_in, cot), (act_in, act), (lists_in, lists), (nbr_in, nbr), (w1_in, w1), (w2_in, w2))
        )
    ]
    for load in loads:
        load.start()

    beside = [row * across + lax.rem(place_in_row + step, across) for step in (1, across - 1)]
    if nj > across:
        beside += [lax.rem(chip + step, nj) for step in (across, nj - across)]
    beside = [(p * 2 + core, smp) for p in beside]
    for device in beside + [(blk, along(1)), (blk, along(nz - 1))]:
        greet(device)
    greeted = sum(there.astype(jnp.int32) for there in in_range) + len(beside) + 2

    def tell(step):
        for device in beside:
            pl.semaphore_signal(heard.at[0, step], inc=1, device_id=device, device_id_type=MESH)
        if step < rounds:
            for i in (1 << step, nz - (1 << step)):
                pl.semaphore_signal(heard.at[1, step], inc=1, device_id=(blk, along(i)), device_id_type=MESH)

    def hear_plane(step):
        pl.semaphore_wait(heard.at[0, step], len(beside))

    def hear_samples(step):
        if step < rounds:
            pl.semaphore_wait(heard.at[1, step], 2)

    rounds = max(nz // 4, 1).bit_length()

    for load in loads[:4]:
        load.wait()
    live = act[...] > 0
    live_f = live.astype(f32)
    field[0:channels, :] = jnp.where(live, feat[0].astype(f32), 0.0).astype(bf16)
    field[channels:both, :] = jnp.where(live, cot[0].astype(f32), 0.0).astype(bf16)

    spread = jnp.concatenate(
        [jnp.broadcast_to(lists[0, 0, d : d + 1, :], (per_list, per_list)) for d in range(8)], axis=0
    )
    at_row = lax.broadcasted_iota(jnp.int32, spread.shape, 0)
    at_col = lax.broadcasted_iota(jnp.int32, spread.shape, 1)
    column = jnp.sum(jnp.where(lax.rem(at_row, per_list) == at_col, spread, 0), axis=1, keepdims=True)
    pick[...] = one_hot(lax.broadcasted_iota(jnp.int32, (8 * per_list, voxels), 1), column)

    def face_copies(sent, halo, sems):
        copies = []
        for d, delta in enumerate(DELTAS):
            if d < 4:
                rows = pl.ds(d * per_list, per_list)
                into = rows
            else:
                rows = pl.ds(d * per_list, CORNER)
                into = pl.ds(4 * per_list + (d - 4) * CORNER, CORNER)
            target, source = blk + delta, blk - delta
            copy = pltpu.make_async_remote_copy(
                src_ref=sent.at[rows, :], dst_ref=halo.at[into, :],
                send_sem=sems.at[0, d], recv_sem=sems.at[1, d],
                device_id=(jnp.clip(target, 0, nb - 1), smp), device_id_type=MESH,
            )
            has_target = (target >= 0) & (target < nb)
            has_source = (source >= 0) & (source < nb)
            copies.append((copy, has_target, has_source))
        return copies

    def start_faces(copies):
        for copy, has_target, _ in copies:
            pl.when(has_target)(copy.start)

    def arrive_faces(copies):
        for copy, _, has_source in copies:
            pl.when(has_source)(copy.wait_recv)

    def finish_faces(copies):
        for copy, has_target, _ in copies:
            pl.when(has_target)(copy.wait_send)

    faces_a = face_copies(sent_a, halo_a, sem_a)
    faces_c = face_copies(sent_c, halo_c, sem_c)
    sent_a[:, 0:both] = nt(pick[...], field[...]).astype(bf16)
    sent_a[:, both:] = jnp.zeros((8 * per_list, sent_a.shape[1] - both), bf16)
    pl.semaphore_wait(barrier, greeted)
    start_faces(faces_a)
    tell(0)

    for load in loads[4:]:
        load.wait()
    unit = eye(channels, bf16)
    local_rows = lax.broadcasted_iota(jnp.int32, (voxels, voxels), 0)
    place = lax.broadcasted_iota(jnp.int32, (halo_rows, voxels), 0)
    past = place - 4 * per_list
    corner_code = jnp.where(
        lax.rem(past, CORNER) < 4, voxels + 4 * per_list + lax.div(past, CORNER) * 4 + lax.rem(past, CORNER), -1
    )
    halo_codes = jnp.where(past < 0, voxels + place, corner_code)

    def at(o):
        return pl.ds(pl.multiple_of(o * channels, 32), channels)

    def prepare(step, _):
        for u in range(UNROLL):
            o = step * UNROLL + u
            codes = nbr[o]
            hot = one_hot(local_rows, codes)
            local_hot[o] = hot
            halo_hot[o] = one_hot(halo_codes, codes)
            got = nn(field[...], hot).astype(bf16)
            picked[0, at(o), :] = got[:channels]
            picked[1, at(OFFSETS - 1 - o), :] = got[channels:]
            turned[o] = nt(unit, w1[o]).astype(bf16)
        return 0

    lax.fori_loop(0, OFFSETS // UNROLL, prepare, 0)
    blank = jnp.zeros((channels, channels), bf16)
    for g in range(GROUPS):
        lanes = pl.ds(g * GROUP * channels, GROUP * channels)
        group = range(g * GROUP, (g + 1) * GROUP)
        side_by_side[0, :, lanes] = jnp.concatenate([w1[o] if o < OFFSETS else blank for o in group], axis=1)
        side_by_side[1, :, lanes] = jnp.concatenate(
            [nt(unit, w2[o]) if o < OFFSETS else blank.astype(f32) for o in group], axis=1
        ).astype(bf16)
    tail = picked.shape[1] - OFFSETS * channels
    picked[:, OFFSETS * channels :, :] = jnp.zeros((2, tail, voxels), bf16)
    rest = half_rows - GROUPS * group_rows
    own[GROUPS * group_rows :, :] = jnp.zeros((rest, 128), f32)
    from_core[GROUPS * group_rows :, :] = jnp.zeros((rest, 128), bf16)

    hear_plane(0)
    hear_samples(0)
    tell(1)
    arrive_faces(faces_a)
    turned_halo = nt(eye(halo_a.shape[1], bf16)[:both], halo_a[...]).astype(bf16)
    zeros = jnp.zeros((channels, voxels), f32)

    def first_pass(step, _):
        for u in range(FIRST_UNROLL):
            o = step * FIRST_UNROLL + u
            mirror = OFFSETS - 1 - o
            got = nn(turned_halo, halo_hot[o]).astype(bf16)
            picked[0, at(o), :] += got[:channels]
            picked[1, at(mirror), :] += got[channels:]
        return 0

    lax.fori_loop(0, OFFSETS // FIRST_UNROLL, first_pass, 0)
    hear_plane(1)
    hear_samples(1)
    tell(2)
    forth = nn(side_by_side[0], picked[0])
    back = nn(side_by_side[1], picked[1])
    pre = live_f * forth
    gate = 1.0 / (1.0 + jnp.exp(-pre))
    hidden = (live_f * (pre * gate)).astype(bf16)
    grad_pre = ((live_f * back) * gate * (1.0 + pre * (1.0 - gate))).astype(bf16)
    sides[0] = grad_pre
    sides[1] = hidden
    field[0:channels, :] = hidden
    field[channels:both, :] = grad_pre
    sent_c[:, 0:both] = nt(pick[...], field[...]).astype(bf16)
    sent_c[:, both:] = jnp.zeros((8 * per_list, sent_c.shape[1] - both), bf16)
    start_faces(faces_c)

    def core_copy(g):
        rows = pl.ds(pl.multiple_of(g * group_rows, 32), group_rows)
        return remote(to_core.at[rows, :], from_core.at[rows, :], sem_core, g, g, partner)

    def correlate(which, groups, dtype):
        wide = GROUP * channels
        rows = pl.ds(groups[0] * wide, (groups[1] - groups[0]) * wide)
        if which == 0:
            flat = nt(sides[0], picked[0, rows, :]).astype(dtype)
            return [flat[:, n * wide : (n + 1) * wide] for n in range(groups[1] - groups[0])]
        tall = nt(picked[1, rows, :], sides[1]).astype(dtype)
        return [
            jnp.concatenate([tall[n + k * channels : n + (k + 1) * channels] for k in range(GROUP)], axis=1)
            for n in range(0, tall.shape[0], wide)
        ]

    def put(where, g, block):
        for t in range(tiles):
            rows = pl.ds(g * group_rows + t * channels, channels)
            where[rows, :] = block[:, t * 128 : (t + 1) * 128]

    def give(which, groups):
        for g, block in zip(range(*groups), correlate(which, groups, bf16)):
            put(to_core, g, block)
            core_copy(g).start()

    def keep(which, groups):
        for g, block in zip(range(*groups), correlate(which, groups, f32)):
            put(own, g, block)

    def join():
        done = 0
        for p in range(nj):
            while done < GROUPS and done * group_rows < (p + 1) * piece:
                core_copy(done).wait_recv()
                done += 1
            rows = pl.ds(p * piece, piece)
            total = own[rows, :] + from_core[rows, :].astype(f32)
            own[rows, :] = total
            summed[p, 0:piece, :] = total.astype(bf16)
            summed[p, piece:, :] = total[:quarter].astype(bf16)

    for which in range(2):

        @pl.when(core == which)
        def _():
            for groups in CHUNKS:
                give(1 - which, groups)
            for groups in CHUNKS:
                keep(which, groups)

    join()

    def quarter_rows(q):
        return pl.ds(pl.multiple_of(q * quarter, 16), quarter)

    starts = (far, near)

    def plane_copy(part, source, target):
        rows = pl.ds(pl.multiple_of(starts[part] * quarter, 8), some)
        return pltpu.make_async_remote_copy(
            src_ref=summed.at[target, rows, :], dst_ref=arrived.at[part, source],
            send_sem=sem_plane.at[0, part, target], recv_sem=sem_plane.at[1, part, source],
            device_id=(target * 2 + core, smp), device_id_type=MESH,
        )

    hear_plane(2)
    for part in range(2):
        loop(0, nj - 1, lambda k: plane_copy(part, chip, plane(k)).start())

    def owner(w):
        return 2 * w + core

    owns = lax.rem(smp, 2) == core
    here = lax.div(smp, 2)

    def z_copy(source, target, rows):
        return remote(z_send.at[rows, :], z_in.at[source], sem_z, source, target, (blk, target))

    def part_owners(start, act_on):
        def run(k):
            w = lax.rem(start * (owners // 4) + k, owners)
            pl.when(owner(w) != smp)(lambda: act_on(w, k))

        loop(0, owners // 2, run)

    def z_sends(part, act_on):
        def run(w, k):
            act_on(owner(w), pl.ds(pl.multiple_of(part * some + k * sliver, 16), sliver))

        part_owners(starts[part], run)

    hear_samples(2)
    base = pl.multiple_of(chip * piece, piece)
    for part in range(2):
        for k in range(2):
            first_row = base + lax.rem(starts[part] + k, 4) * quarter
            z_part[part * some + k * quarter : part * some + (k + 1) * quarter, :] = own[
                pl.ds(pl.multiple_of(first_row, 8), quarter), :
            ]

        def add_piece(k):
            source = plane_back(k)
            plane_copy(part, source, source).wait_recv()
            z_part[part * some : (part + 1) * some, :] += arrived[part, source].astype(f32)

        loop(0, nj - 1, add_piece)
        z_send[part * some : (part + 1) * some, :] = z_part[part * some : (part + 1) * some, :].astype(bf16)
        z_sends(part, lambda target, rows: z_copy(smp, target, rows).start())

    arrive_faces(faces_c)
    turned_halo_c = nt(eye(halo_c.shape[1], bf16)[:both], halo_c[...]).astype(bf16)

    def second_pass(step, sums):
        forth, back = sums
        for u in range(UNROLL):
            o = step * UNROLL + u
            got = (nn(field[...], local_hot[o]) + nn(turned_halo_c, halo_hot[o])).astype(bf16)
            forth = forth + nn(w2[o], got[:channels])
            back = back + nn(turned[OFFSETS - 1 - o], got[channels:])
        return forth, back

    most = OFFSETS // UNROLL - 1
    forth, back = lax.fori_loop(0, most, second_pass, (zeros, zeros))

    def sliver_rows(w):
        return pl.ds(pl.multiple_of(w * sliver, 16), sliver)

    def zg_copy(w, target):
        part = z_out.at[sliver_rows(w), :]
        return remote(part, part, sem_zg, owner(w), target, (blk, target))

    @pl.when(owns)
    def _():
        place_here = lax.rem(here + owners - near * (owners // 4), owners)

        def add_sliver(i, running):
            source = along(i)
            z_copy(source, source, pl.ds(0, sliver)).wait_recv()
            return running + z_in[source].astype(f32)

        total = z_part[pl.ds(pl.multiple_of(some + place_here * sliver, 16), sliver), :]
        z_out[sliver_rows(here), :] = lax.fori_loop(1, nz, add_sliver, total).astype(bf16)
        loop(0, nz - 1, lambda k: zg_copy(here, along(ring_step(k, nz))).start())

    forth, back = lax.fori_loop(most, OFFSETS // UNROLL, second_pass, (forth, back))
    results[0] = (live_f * forth).astype(bf16)
    results[1] = (live_f * back).astype(bf16)
    keeps = [
        pltpu.make_async_copy(results.at[0], out_field, sem_out.at[0]),
        pltpu.make_async_copy(results.at[1], input_grad, sem_out.at[1]),
    ]
    for copy in keeps:
        copy.start()
    finish_faces(faces_a)
    finish_faces(faces_c)
    loop(0, GROUPS, lambda g: core_copy(g).wait_send())
    for part in range(2):
        loop(0, nj - 1, lambda k: plane_copy(part, chip, plane(k)).wait_send())
        z_sends(part, lambda target, rows: z_copy(smp, target, rows).wait_send())

    def gather_copy(part, source, target):
        return pltpu.make_async_remote_copy(
            src_ref=spreading.at[chip, part], dst_ref=spreading.at[source, part],
            send_sem=sem_gather.at[0, part, target], recv_sem=sem_gather.at[1, part, source],
            device_id=(target * 2 + core, smp), device_id_type=MESH,
        )

    def keep_copy(part):
        return pltpu.make_async_copy(spreading.at[:, part], gathered.at[core, :, part], sem_keep.at[part])

    def forward_copy(which, part, p):
        return pltpu.make_async_remote_copy(
            src_ref=spreading.at[p, part], dst_ref=gathered.at[which, p, part],
            send_sem=sem_forward.at[0, part], recv_sem=sem_forward.at[1, part],
            device_id=partner, device_id_type=MESH,
        )

    def store(part, p):
        forward_copy(core, part, p).start()

    for part, start in enumerate((near, far)):

        part_owners(start, lambda w, k: zg_copy(w, smp).wait_recv())
        for k in range(2):
            spreading[chip, part, k * quarter : (k + 1) * quarter, :] = z_out[
                quarter_rows(lax.rem(start + k, 4)), :
            ]
        loop(0, nj - 1, lambda k: gather_copy(part, chip, plane(k)).start())
        store(part, chip)


    @pl.when(owns)
    def _():
        loop(1, nz, lambda i: zg_copy(here, along(i)).wait_send())

    for copy in keeps:
        copy.wait()
    for part in range(2):

        def hand_on(k):
            source = plane_back(k)
            gather_copy(part, source, source).wait_recv()
            store(part, source)

        loop(0, nj - 1, hand_on)
        keep_copy(part).start()
        loop(0, nj - 1, lambda k: gather_copy(part, chip, plane(k)).wait_send())
    for part in range(2):
        keep_copy(part).wait()
        forwarded = pltpu.make_async_remote_copy(
            src_ref=spreading.at[:, part], dst_ref=gathered.at[other, :, part],
            send_sem=sem_forward.at[0, part], recv_sem=sem_forward.at[1, part],
            device_id=partner, device_id_type=MESH,
        )
        forwarded.wait_send()
        forwarded.wait_recv()


def unpack_kernel(
    nj, nz, scale, field_in, grad_in, gathered, first, second, field_out, grad_out,
    fields, stage, wide_sums, sem_field, sem_in, sem_out,
):
    channels, offsets = first.shape[1], first.shape[0]
    half_rows = stage.shape[1]
    quarter = half_rows // nj // 4
    group_rows = GROUP * channels * channels // 128
    tiles = GROUP * channels // 128
    run = 32
    near = lax.rem(far_quarter(lax.axis_index("smp"), nz) + 2, 4)
    turned = [pl.multiple_of(lax.rem(q + 4 - near, 4) * quarter, 8) for q in range(4)]

    cuts = (0, 3 * half_rows // 16, half_rows // 2, half_rows)

    def load(which, k):
        rows = pl.ds(cuts[k], cuts[k + 1] - cuts[k])
        return pltpu.make_async_copy(gathered.at[which, rows], stage.at[which, rows], sem_in.at[which, k])

    def save(which, g):
        some = pl.ds(g * GROUP, min(GROUP, offsets - g * GROUP))
        return pltpu.make_async_copy(
            wide_sums.at[which, some], (first, second)[which].at[some], sem_out.at[which, g]
        )

    loads = [pltpu.make_async_copy(x, fields.at[i], sem_field.at[0, i]) for i, x in enumerate((field_in, grad_in))]
    saves = [
        pltpu.make_async_copy(fields.at[i], x.at[0], sem_field.at[1, i]) for i, x in enumerate((field_out, grad_out))
    ]
    for which in range(2):
        for k in range(3):
            load(which, k).start()
    for copy in loads:
        copy.start()
    for which in range(2):
        here = 0
        for g in range(GROUPS):
            while here < 3 and cuts[here] < (g + 1) * group_rows:
                load(which, here).wait()
                here += 1

            def part_of(row):
                first_row = row - row % (quarter * 4) + turned[row // quarter % 4] + row % quarter
                return stage[which, pl.ds(pl.multiple_of(first_row, 8), run), :].astype(jnp.float32)

            parts = [part_of(g * group_rows + n) for n in range(0, group_rows, run)]
            step = channels // run
            wide = jnp.concatenate(
                [jnp.concatenate(parts[t * step : (t + 1) * step], axis=0) for t in range(tiles)], axis=1
            )
            wide = wide * scale
            for k in range(GROUP):
                wide_sums[which, g * GROUP + k] = wide[:, k * channels : (k + 1) * channels]
            save(which, g).start()
    for copy in loads:
        copy.wait()
    for copy in saves:
        copy.start()
    for which in range(2):
        for g in range(GROUPS):
            save(which, g).wait()
    for copy in saves:
        copy.wait()


def body(nb, nz, features, active, neighbour_rows, send_rows, first_weight, second_weight, cotangent):
    channels, voxels = features.shape[1], features.shape[2]
    both = 2 * channels
    per_list = send_rows.shape[3]
    halo_rows = 4 * per_list + 4 * CORNER
    nj = nb // 2
    half_rows = 2048
    piece = half_rows // nj
    bf16, f32 = jnp.bfloat16, jnp.float32
    anywhere = pl.BlockSpec(memory_space=pl.ANY)
    slots = lax.axis_size("smp") * features.shape[0] * nb * voxels
    table = jnp.transpose(neighbour_rows, (1, 0, 2))
    operands = (features, active, table, send_rows, first_weight, second_weight, cotangent)
    dma = pltpu.SemaphoreType.DMA
    wide = 256
    out_field, input_grad, gathered = pl.pallas_call(
        functools.partial(main_kernel, nb, nz),
        out_shape=[
            jax.ShapeDtypeStruct((channels, voxels), bf16),
            jax.ShapeDtypeStruct((channels, voxels), bf16),
            jax.ShapeDtypeStruct((2, nj, 2, piece // 2, 128), bf16),
        ],
        in_specs=[anywhere] * 7,
        out_specs=[anywhere] * 3,
        scratch_shapes=[
            *(pltpu.VMEM(x.shape, x.dtype) for x in operands),
            pltpu.VMEM((2, channels, voxels), bf16),
            pltpu.VMEM((nj, 2, piece // 2, 128), bf16),
            pltpu.VMEM((both, voxels), bf16),
            pltpu.VMEM((8 * per_list, voxels), bf16),
            pltpu.VMEM((8 * per_list, wide), bf16),
            pltpu.VMEM((halo_rows, wide), bf16),
            pltpu.VMEM((8 * per_list, wide), bf16),
            pltpu.VMEM((halo_rows, wide), bf16),
            pltpu.VMEM((OFFSETS, voxels, voxels), bf16),
            pltpu.VMEM((OFFSETS, halo_rows, voxels), bf16),
            pltpu.VMEM((OFFSETS, channels, channels), bf16),
            pltpu.VMEM((2, channels, GROUP * GROUPS * channels), bf16),
            pltpu.VMEM((2, GROUP * GROUPS * channels, voxels), bf16),
            pltpu.VMEM((2, channels, voxels), bf16),
            pltpu.VMEM((half_rows, 128), bf16),
            pltpu.VMEM((half_rows, 128), f32),
            pltpu.VMEM((half_rows, 128), bf16),
            pltpu.VMEM((nj, piece + piece // 4, 128), bf16),
            pltpu.VMEM((2, nj, piece // 2, 128), bf16),
            pltpu.VMEM((piece, 128), f32),
            pltpu.VMEM((piece, 128), bf16),
            pltpu.VMEM((nz, piece // (nz // 2), 128), bf16),
            pltpu.VMEM((piece, 128), bf16),
            pltpu.SemaphoreType.REGULAR((2, 3)),
            dma((7,)),
            dma((2,)),
            dma((2, 8)),
            dma((2, 8)),
            dma((2, GROUPS)),
            dma((2, 2, nj)),
            dma((2, nz)),
            dma((2, nz)),
            dma((2, 2, nj)),
            dma((2,)),
            dma((2, 2)),
        ],
        compiler_params=pltpu.CompilerParams(
            collective_id=0, has_side_effects=True, vmem_limit_bytes=56 * 2**20
        ),
        name="halo_conv_and_sum",
    )(*operands)

    grad = jax.ShapeDtypeStruct((OFFSETS, channels, channels), f32)
    field = jax.ShapeDtypeStruct((1, channels, voxels), bf16)
    first_grad, second_grad, out_field, input_grad = pl.pallas_call(
        functools.partial(unpack_kernel, nj, nz, 1.0 / slots**0.5),
        out_shape=[grad, grad, field, field],
        in_specs=[anywhere] * 3,
        out_specs=[anywhere] * 4,
        scratch_shapes=[
            pltpu.VMEM((2, channels, voxels), bf16),
            pltpu.VMEM((2, half_rows, 128), bf16),
            pltpu.VMEM((2, GROUP * GROUPS, channels, channels), f32),
            dma((2, 2)),
            dma((2, 3)),
            dma((2, GROUPS)),
        ],
        compiler_params=pltpu.CompilerParams(vmem_limit_bytes=56 * 2**20),
        name="unpack",
    )(out_field, input_grad, gathered.reshape(2, half_rows, 128))
    return out_field, input_grad, first_grad, second_grad


def solution(mesh):
    return jax.shard_map(
        functools.partial(body, mesh.shape["blk"], mesh.shape["smp"]),
        mesh=mesh,
        in_specs=(
            P("smp", None, "blk"),
            P("smp", "blk"),
            P("smp", None, "blk"),
            P("smp", "blk", None, None),
            P(),
            P(),
            P("smp", None, "blk"),
        ),
        out_specs=(P("smp", None, "blk"), P("smp", None, "blk"), P(), P()),
        check_vma=False,
    )
```
